32 devices in a mesh: section: 2 (over x), dp: 16 (over z, y, core).
Axes of the slice: x: 2, y: 2, z: 4, core: 2. Of those that a mesh axis runs over, the one named last changes fastest.
Arguments:
- frames: bfloat16 [4096, 1024], P('dp'), may hold values from -6 to 6
- lengths: int32 [32, 3], P('dp'), may hold values from 16 to 64, as said below
- cotangent: bfloat16 [4096, 1024], P('dp'), may hold values from -6 to 6
- project_weight: float32 [2, 1024, 3072], P('section', 'dp'), may hold values from -0.1875 to 0.1875
- merge_weight: float32 [2, 1024, 1024], P('section', 'dp'), may hold values from -1 to 1
- expand_weight: float32 [2, 1024, 4096], P('section', 'dp'), may hold values from -0.1875 to 0.1875
- shrink_weight: float32 [2, 4096, 1024], P('section', 'dp'), may hold values from -0.09375 to 0.09375
- vectors: float32 [2, 12, 1024], P('section', None, 'dp'), may hold values from -0.9 to 2.1, as said below
- project_row: float32 [2, 1024], P('section', 'dp'), may hold values from 6144 to 24576
- project_col: float32 [2, 3072], P('section'), may hold values from 2048 to 32768
- merge_row: float32 [2, 1024], P('section', 'dp'), may hold values from 409.6 to 1638.4
- merge_col: float32 [2, 1024], P('section'), may hold values from 409.6 to 1638.4
- expand_row: float32 [2, 1024], P('section', 'dp'), may hold values from 2048 to 8192
- expand_col: float32 [2, 4096], P('section'), may hold values from 2048 to 8192
- shrink_row: float32 [2, 4096], P('section', 'dp'), may hold values from 6144 to 24576
- shrink_col: float32 [2, 1024], P('section'), may hold values from 6144 to 24576
- vector_moment: float32 [2, 12, 1024], P('section', None, 'dp'), may hold values from 2048 to 20480
Outputs:
- layer_outputs: float32 [2, 4096, 1024], P('section', 'dp')
- input_grads: float32 [2, 4096, 1024], P('section', 'dp')
- project_grad: float32 [2, 1024, 3072], P('section', 'dp')
- project_rowstat: float32 [2, 1024], P('section', 'dp')
- project_colstat: float32 [2, 3072], P('section')
- project_updated: float32 [2, 1024, 3072], P('section', 'dp')
- merge_grad: float32 [2, 1024, 1024], P('section', 'dp')
- merge_rowstat: float32 [2, 1024], P('section', 'dp')
- merge_colstat: float32 [2, 1024], P('section')
- merge_updated: float32 [2, 1024, 1024], P('section', 'dp')
- expand_grad: float32 [2, 1024, 4096], P('section', 'dp')
- expand_rowstat: float32 [2, 1024], P('section', 'dp')
- expand_colstat: float32 [2, 4096], P('section')
- expand_updated: float32 [2, 1024, 4096], P('section', 'dp')
- shrink_grad: float32 [2, 4096, 1024], P('section', 'dp')
- shrink_rowstat: float32 [2, 4096], P('section', 'dp')
- shrink_colstat: float32 [2, 1024], P('section')
- shrink_updated: float32 [2, 4096, 1024], P('section', 'dp')
- vector_grad: float32 [2, 12, 1024], P('section', None, 'dp')
- vector_second: float32 [2, 12, 1024], P('section', None, 'dp')
- vector_updated: float32 [2, 12, 1024], P('section', None, 'dp')
The draws below stay inside these ranges and needn't reach their ends.
Inputs may be any that keep to these rules, and one draw needn't show every extreme that they name: Row b lists the lengths of the utterances of micro-batch b, laid end to end from its first frame; the frames after them are padding. In every row one length is exactly 64 and the others lie between 16 and 32. `vectors`: rows 0 and 5 of each layer are positive gains, the other rows biases.
All inputs are finite; a program needn't handle non-finite values.
Results may differ from the reference program's by a relative error of at most 0.018.
The reference program's roundings to bfloat16 on the way count: a program that leaves them out, or rounds other values in their place, can miss the bound.
Values may be sent and summed in bfloat16 or wider, within the bound.
No kernel may reach another device: no remote copies, remote signals or barrier semaphores. Data moves between devices by JAX's collectives and lax.ppermute only.
A program may use at most 192 MiB of HBM per device.

```python
import math
import jax
import jax.numpy as jnp
from jax import lax

D = 1024
FF = 4096
HEADS = 16
HEAD_DIM = 64
MB = 128
UTTS = 3
STEP = 10
BLOCKS = 32
TOKENS = 4096


def draw_lengths(key, part):
    key = jax.random.fold_in(key, 11)
    first_key, second_key = jax.random.split(key)
    others = jax.random.randint(first_key, (BLOCKS, UTTS), MB // 8, MB // 4 + 1)
    longest = jax.random.randint(second_key, (BLOCKS, 1), 0, UTTS)
    places = jnp.arange(UTTS, dtype=jnp.int32)[None, :]
    return jnp.where(places == longest, MB // 2, others).astype(jnp.int32)


def draw_vectors(key, part):
    key = jax.random.fold_in(key, 5)
    first_key, second_key = jax.random.split(key)
    biases = 0.3 * jax.random.truncated_normal(first_key, -3.0, 3.0, (2, 12, D), jnp.float32)
    rising = 0.6 + 1.2 * jnp.arange(D, dtype=jnp.float32) / D
    gains = rising * (1.0 + 0.15 * jax.random.uniform(second_key, (2, 12, D), jnp.float32, -1.0, 1.0))
    rows = jnp.arange(12, dtype=jnp.int32)[None, :, None]
    is_gain = (rows == 0) | (rows == 5)
    return jnp.where(is_gain, gains, biases).astype(jnp.float32)


def block_scale(key, extent, shards, low, largest):
    level, own = 1.0, jax.random.fold_in(key, 6)
    for dim, parts in shards:
        heights = jnp.exp(jax.random.uniform(jax.random.fold_in(own, dim), (parts,), jnp.float32, low / len(shards), largest / len(shards)))
        level = level * jnp.repeat(heights, extent[dim] // parts).reshape([-1 if axis == dim else 1 for axis in range(len(extent))])
    return level


def bell_draw(stream_key, shape, scale, reach, cuts=(), kind=jnp.bfloat16):
    values = scale * jax.random.normal(stream_key, shape, jnp.float32)
    if cuts:
        values = values * block_scale(stream_key, shape, cuts, -0.22, 0.18)
    return jnp.clip(values, -reach, reach).astype(kind)


def setup_inputs(seed: int = 0) -> dict:
    seeds = jax.random.split(jax.random.key(seed), 18)
    frames = bell_draw(seeds[0], (TOKENS, D), 1.0, 6.0, ((0, 16),))
    lengths = draw_lengths(jax.random.fold_in(seeds[17], 71), 0)
    cotangent = bell_draw(seeds[2], (TOKENS, D), 1.0, 6.0, ((0, 16),))
    project_weight = bell_draw(seeds[3], (2, D, 3 * D), D ** -0.5, 0.1875, ((0, 2), (1, 16)), jnp.float32)
    merge_weight = bell_draw(seeds[4], (2, D, D), (D // 32) ** -0.5, 1.0, ((0, 2), (1, 16)), jnp.float32)
    expand_weight = bell_draw(seeds[5], (2, D, FF), D ** -0.5, 0.1875, ((0, 2), (1, 16)), jnp.float32)
    shrink_weight = bell_draw(seeds[6], (2, FF, D), FF ** -0.5, 0.09375, ((0, 2), (1, 16)), jnp.float32)
    vectors = draw_vectors(jax.random.fold_in(seeds[17], 71), 0)
    project_row = jnp.clip(jnp.exp(math.log(24576.0) - 1.3862944 * jax.random.uniform(seeds[8], (2, D), jnp.float32) ** block_scale(seeds[8], (2, D), ((0, 2), (1, 16)), -0.2, 0.2)), 6144.0, 24576.0)
    project_col = jnp.clip(jnp.exp(math.log(32768.0) - 2.7725887 * jax.random.uniform(seeds[9], (2, 3 * D), jnp.float32) ** block_scale(seeds[9], (2, 3 * D), ((0, 2),), -0.2, 0.2)), 2048.0, 32768.0)
    merge_row = jnp.clip(jnp.exp(math.log(1638.4) - 1.3862944 * jax.random.uniform(seeds[10], (2, D), jnp.float32) ** block_scale(seeds[10], (2, D), ((0, 2), (1, 16)), -0.2, 0.2)), 409.6, 1638.4)
    merge_col = jnp.clip(jnp.exp(math.log(1638.4) - 1.3862944 * jax.random.uniform(seeds[11], (2, D), jnp.float32) ** block_scale(seeds[11], (2, D), ((0, 2),), -0.2, 0.2)), 409.6, 1638.4)
    expand_row = jnp.clip(jnp.exp(math.log(8192.0) - 1.3862944 * jax.random.uniform(seeds[12], (2, D), jnp.float32) ** block_scale(seeds[12], (2, D), ((0, 2), (1, 16)), -0.2, 0.2)), 2048.0, 8192.0)
    expand_col = jnp.clip(jnp.exp(math.log(8192.0) - 1.3862944 * jax.random.uniform(seeds[13], (2, FF), jnp.float32) ** block_scale(seeds[13], (2, FF), ((0, 2),), -0.2, 0.2)), 2048.0, 8192.0)
    shrink_row = jnp.clip(jnp.exp(math.log(24576.0) - 1.3862944 * jax.random.uniform(seeds[14], (2, FF), jnp.float32) ** block_scale(seeds[14], (2, FF), ((0, 2), (1, 16)), -0.2, 0.2)), 6144.0, 24576.0)
    shrink_col = jnp.clip(jnp.exp(math.log(24576.0) - 1.3862944 * jax.random.uniform(seeds[15], (2, D), jnp.float32) ** block_scale(seeds[15], (2, D), ((0, 2),), -0.2, 0.2)), 6144.0, 24576.0)
    vector_moment = jnp.clip(jnp.exp(math.log(20480.0) - 2.3025851 * jax.random.uniform(seeds[16], (2, 12, D), jnp.float32) ** block_scale(seeds[16], (2, 12, D), ((0, 2), (2, 16)), -0.2, 0.2)), 2048.0, 20480.0)
    return {"frames": frames, "lengths": lengths, "cotangent": cotangent, "project_weight": project_weight, "merge_weight": merge_weight, "expand_weight": expand_weight, "shrink_weight": shrink_weight, "vectors": vectors, "project_row": project_row, "project_col": project_col, "merge_row": merge_row, "merge_col": merge_col, "expand_row": expand_row, "expand_col": expand_col, "shrink_row": shrink_row, "shrink_col": shrink_col, "vector_moment": vector_moment}


@jax.custom_vjp
def low(v):
    return lax.optimization_barrier(v.astype(jnp.bfloat16)).astype(jnp.float32)

@jax.custom_vjp
def low_back(v):
    return v

def low_keep(v):
    return (low(v), None)

def low_pass(kept, grad):
    return (grad,)

def back_keep(v):
    return (v, None)

def back_low(kept, grad):
    return (low(grad),)
low.defvjp(low_keep, low_pass)
low_back.defvjp(back_keep, back_low)
EPSILON = 1e-05
PRECISE = lax.Precision.HIGHEST
RATE = 0.04
VECTOR_RATE = 0.25
MASKED = -1e+30

def layer_norm(values, gain, shift):
    centred = values - lax.optimization_barrier(jnp.mean(values, axis=-1, keepdims=True))
    spread = lax.optimization_barrier(jnp.mean(centred * centred, axis=-1, keepdims=True))
    return centred * lax.rsqrt(spread + EPSILON) * gain + shift

def segments(lengths_row, count):
    ends = jnp.cumsum(lengths_row)
    places = jnp.arange(count, dtype=jnp.int32)
    return lax.optimization_barrier(jnp.sum((places[:, None] >= ends[None, :]).astype(jnp.int32), axis=1))

def layer(inputs, project, merge, expand, shrink, params, segment):
    count = inputs.shape[0]
    normed = low(layer_norm(inputs, params[0], params[1]))
    bias = jnp.concatenate([params[2], jnp.zeros_like(params[2]), params[3]])
    packed = low_back(low(jnp.dot(normed, project, precision=PRECISE) + bias))
    heads = packed.reshape(count, 3, HEADS, HEAD_DIM)
    queries, keys, values = (heads[:, 0], heads[:, 1], heads[:, 2])
    scores = low_back(jnp.einsum('qhd,khd->hqk', queries, keys, precision=PRECISE) * HEAD_DIM ** (-0.5))
    visible = segment[:, None] == segment[None, :]
    scores = jnp.where(visible[None], scores, MASKED)
    attend = jax.nn.softmax(scores, axis=-1)
    mixed = jnp.einsum('hqk,khd->qhd', low(attend), values, precision=PRECISE).reshape(count, D)
    mixed = low_back(low(mixed))
    branch = low_back(jnp.dot(mixed, merge, precision=PRECISE) + params[4])
    middle = inputs + branch
    normed_two = low(layer_norm(middle, params[5], params[6]))
    hidden_pre = low_back(jnp.dot(normed_two, expand, precision=PRECISE) + params[8:12].reshape(-1))
    hidden = low(jax.nn.gelu(hidden_pre, approximate=False))
    return middle + low_back(jnp.dot(hidden, shrink, precision=PRECISE) + params[7])

def factored(grad, row_old, col_old, weight):
    decay = 1.0 - STEP ** (-0.8)
    squares = grad * grad + 1e-30
    row_new = decay * row_old + (1.0 - decay) * lax.optimization_barrier(jnp.mean(squares, axis=2))
    col_new = decay * col_old + (1.0 - decay) * lax.optimization_barrier(jnp.mean(squares, axis=1))
    relative = row_new / lax.optimization_barrier(jnp.mean(row_new, axis=1, keepdims=True))
    update = grad * lax.rsqrt(relative)[:, :, None] * lax.rsqrt(col_new)[:, None, :]
    scale = jnp.sqrt(lax.optimization_barrier(jnp.mean(update * update, axis=(1, 2), keepdims=True)))
    return (row_new, col_new, weight - RATE * update / jnp.maximum(1.0, scale))

def unfactored(grad, moment, weight):
    decay = 1.0 - STEP ** (-0.8)
    moment_new = decay * moment + (1.0 - decay) * (grad * grad + 1e-30)
    update = grad * lax.rsqrt(moment_new)
    scale = jnp.sqrt(lax.optimization_barrier(jnp.mean(update * update, axis=2, keepdims=True)))
    return (moment_new, weight - VECTOR_RATE * update / jnp.maximum(1.0, scale))

def reference(frames, lengths, cotangent, project_weight, merge_weight, expand_weight, shrink_weight, vectors, project_row, project_col, merge_row, merge_col, expand_row, expand_col, shrink_row, shrink_col, vector_moment):
    blocks = lengths.shape[0]
    segment = jax.vmap(lambda lengths_row: segments(lengths_row, MB))(lengths)
    live = (segment < UTTS).astype(jnp.float32)
    inputs = frames.astype(jnp.float32).reshape(blocks, MB, D)
    targets = cotangent.astype(jnp.float32).reshape(blocks, MB, D) * live[:, :, None]
    params = (project_weight, merge_weight, expand_weight, shrink_weight, vectors)

    def forward(params, inputs, probe):
        copies = jax.tree.map(low, params)
        first = [array[0] for array in copies]
        second = [array[1] for array in copies]

        def pair(total, item):
            block, extra, marks, target = item
            lower = layer(block, *first, marks)
            passed = low_back(low(lower + extra))
            upper = layer(passed, *second, marks)
            return (total + jnp.sum(upper * target), (lower, upper))
        return lax.scan(jax.checkpoint(pair), jnp.zeros((), jnp.float32), (inputs, probe, segment, targets))
    probe = jnp.zeros_like(inputs)
    loss, backward, outputs = jax.vjp(forward, params, inputs, probe, has_aux=True)
    grads, input_back, probe_back = backward(jnp.ones((), jnp.float32))
    lower, upper = outputs
    layer_outputs = jnp.stack([lower, upper]).reshape(2, blocks * MB, D)
    input_grads = jnp.stack([input_back, probe_back]).reshape(2, blocks * MB, D)
    g_project, g_merge, g_expand, g_shrink, g_vectors = grads
    p_rows, p_cols, p_new = factored(g_project, project_row, project_col, project_weight)
    m_rows, m_cols, m_new = factored(g_merge, merge_row, merge_col, merge_weight)
    e_rows, e_cols, e_new = factored(g_expand, expand_row, expand_col, expand_weight)
    s_rows, s_cols, s_new = factored(g_shrink, shrink_row, shrink_col, shrink_weight)
    v_moment, v_new = unfactored(g_vectors, vector_moment, vectors)
    return (layer_outputs, input_grads, g_project, p_rows, p_cols, p_new, g_merge, m_rows, m_cols, m_new, g_expand, e_rows, e_cols, e_new, g_shrink, s_rows, s_cols, s_new, g_vectors, v_moment, v_new)
```

```python
import math

import jax
import jax.numpy as jnp
from jax import lax
from jax.sharding import PartitionSpec as P

HEADS = 16
HEAD_DIM = 64
UTTS = 3
STEP = 10

EPSILON = 1e-05
RATE = 0.04
VECTOR_RATE = 0.25
MASKED = -1e30
BF16 = jnp.bfloat16
F32 = jnp.float32


def ring_of(chips):
    return list(range(0, chips, 2)) + list(range(chips - 1, 0, -2))


def ring_shift(array, ring, by):
    count = len(ring)
    pairs = []
    for place in range(count):
        for core in range(2):
            pairs.append((ring[place] * 2 + core, ring[(place + by) % count] * 2 + core))
    return lax.ppermute(array, "dp", pairs)


def core_swap(array, chips):
    pairs = [(chip * 2 + core, chip * 2 + 1 - core) for chip in range(chips) for core in range(2)]
    return lax.ppermute(array, "dp", pairs)


def chip_swap(array, chips, mask):
    pairs = [
        (chip * 2 + core, (chip ^ mask) * 2 + core) for chip in range(chips) for core in range(2)
    ]
    return lax.ppermute(array, "dp", pairs)


def section_shift(array, by):
    size = lax.axis_size("section")
    pairs = [(i, i + by) for i in range(size) if 0 <= i + by < size]
    return lax.ppermute(array, "section", pairs)


class Place:
    def __init__(self):
        self.size = lax.axis_size("dp")
        self.chips = self.size // 2
        self.ring = ring_of(self.chips)
        self.small = self.size == 16
        index = lax.axis_index("dp")
        self.chip = index // 2
        self.core = index % 2
        where = [0] * self.chips
        for place, chip in enumerate(self.ring):
            where[chip] = place
        self.place = jnp.array(where, jnp.int32)[self.chip]

    def chip_at(self, offset):
        return jnp.array(self.ring, jnp.int32)[(self.place + offset) % self.chips]


def gather_rows(own, here):
    rows, columns = own.shape
    if not here.small:
        return lax.all_gather(own, "dp", axis=0, tiled=True)
    whole = jnp.zeros((here.chips, 2, rows, columns), own.dtype)

    def put(whole, piece, offset):
        other = core_swap(piece, here.chips)
        chip = here.chip_at(offset)
        whole = lax.dynamic_update_slice(whole, piece[None, None], (chip, here.core, 0, 0))
        return lax.dynamic_update_slice(whole, other[None, None], (chip, 1 - here.core, 0, 0))

    whole = put(whole, own, 0)
    ahead = behind = own
    half = here.chips // 2
    for step in range(1, half):
        ahead = ring_shift(ahead, here.ring, 1)
        behind = ring_shift(behind, here.ring, -1)
        whole = put(whole, ahead, -step)
        whole = put(whole, behind, step)
    upper = ring_shift(ahead[: rows // 2], here.ring, 1)
    lower = ring_shift(behind[rows // 2 :], here.ring, -1)
    whole = put(whole, jnp.concatenate([upper, lower], axis=0), half)
    return whole.reshape(here.size * rows, columns)


def scatter_sum(blocks, here):
    chips, rows, columns = blocks.shape
    half = chips // 2

    def block(offset):
        return lax.dynamic_index_in_dim(blocks, here.chip_at(offset), 0, keepdims=False)

    far = block(half)
    ahead = ring_shift(far[: rows // 2].astype(BF16), here.ring, 1)
    behind = ring_shift(far[rows // 2 :].astype(BF16), here.ring, -1)
    mine = block(half - 1)
    ahead = jnp.concatenate([mine[: rows // 2] + ahead.astype(F32), mine[rows // 2 :]], axis=0)
    mine = block(1 - half)
    behind = jnp.concatenate([mine[: rows // 2], mine[rows // 2 :] + behind.astype(F32)], axis=0)
    for step in range(half - 1, 0, -1):
        ahead = ring_shift(ahead.astype(BF16), here.ring, 1).astype(F32)
        behind = ring_shift(behind.astype(BF16), here.ring, -1).astype(F32)
        if step > 1:
            ahead = ahead + block(step - 1)
            behind = behind + block(1 - step)
    return block(0) + ahead + behind


def small_sum(vector, here):
    if not here.small:
        return lax.psum(vector, "dp")
    vector = vector + core_swap(vector, here.chips)
    parts = [vector] + [chip_swap(vector, here.chips, mask) for mask in range(1, here.chips)]
    while len(parts) > 1:
        parts = [parts[i] + parts[i + 1] for i in range(0, len(parts), 2)]
    return parts[0]


def moments(values):
    centred = values - jnp.mean(values, axis=-1, keepdims=True)
    spread = jnp.mean(centred * centred, axis=-1, keepdims=True)
    scale = lax.rsqrt(spread + EPSILON)
    return centred * scale, scale


def norm_back(grad, unit, scale, gain):
    inner = grad * gain
    first = jnp.mean(inner, axis=-1, keepdims=True)
    second = jnp.mean(inner * unit, axis=-1, keepdims=True)
    return (
        scale * (inner - first - unit * second),
        jnp.sum(grad * unit, axis=0),
        jnp.sum(grad, axis=0),
    )


def segments(lengths_row, count):
    ends = jnp.cumsum(lengths_row)
    places = jnp.arange(count, dtype=jnp.int32)
    return jnp.sum((places[:, None] >= ends[None, :]).astype(jnp.int32), axis=1)


def contract_last(left, right):
    return lax.dot_general(
        left, right, (((1,), (1,)), ((), ())), preferred_element_type=F32
    )


def contract_first(left, right):
    return lax.dot_general(
        left, right, (((0,), (0,)), ((), ())), preferred_element_type=F32
    )


def split_heads(packed, segment):
    micro, block = segment.shape
    heads = packed.reshape(micro, block, 3, HEADS, HEAD_DIM)
    return heads[:, :, 0], heads[:, :, 1], heads[:, :, 2]


def attention_weights(queries, keys, segment):
    scores = jnp.einsum(
        "bqhd,bkhd->bhqk", queries, keys, preferred_element_type=F32
    ) * HEAD_DIM ** (-0.5)
    visible = segment[:, :, None] == segment[:, None, :]
    scores = jnp.where(visible[:, None], scores, MASKED)
    highest = jnp.max(scores, axis=-1, keepdims=True)
    shifted = jnp.exp(scores - highest)
    return shifted / jnp.sum(shifted, axis=-1, keepdims=True)


def forward_layer(inputs, weights, segment):
    project, merge, expand, shrink, params = weights
    count, width = inputs.shape
    unit, scale = moments(inputs)
    normed = (unit * params[0] + params[1]).astype(BF16)
    bias = jnp.concatenate([params[2], jnp.zeros_like(params[2]), params[3]])
    packed = (jnp.dot(normed, project, preferred_element_type=F32) + bias).astype(BF16)
    queries, keys, values = split_heads(packed, segment)
    attend = attention_weights(queries, keys, segment).astype(BF16)
    mixed = jnp.einsum("bhqk,bkhd->bqhd", attend, values, preferred_element_type=F32)
    mixed = mixed.reshape(count, width).astype(BF16)
    middle = inputs + jnp.dot(mixed, merge, preferred_element_type=F32) + params[4]
    unit_two, scale_two = moments(middle)
    normed_two = (unit_two * params[5] + params[6]).astype(BF16)
    hidden_pre = jnp.dot(normed_two, expand, preferred_element_type=F32) + params[8:12].reshape(-1)
    hidden = jax.nn.gelu(hidden_pre, approximate=False).astype(BF16)
    output = middle + jnp.dot(hidden, shrink, preferred_element_type=F32) + params[7]
    return output, (inputs, normed, packed, mixed, middle, normed_two, hidden_pre, hidden)


def gelu_slope(values):
    cdf = 0.5 * (1.0 + lax.erf(values * math.sqrt(0.5)))
    return cdf + values * jnp.exp(-0.5 * values * values) * (1.0 / math.sqrt(2.0 * math.pi))


def backward_layer(grad_output, kept, weights, segment):
    project, merge, expand, shrink, params = weights
    inputs, normed, packed, mixed, middle, normed_two, hidden_pre, hidden = kept
    count, width = inputs.shape
    micro, block = segment.shape
    back_out = grad_output.astype(BF16)
    back_hidden = contract_last(back_out, shrink)
    back_pre = (back_hidden * gelu_slope(hidden_pre)).astype(BF16)
    back_normed_two = contract_last(back_pre, expand)
    unit_two, scale_two = moments(middle)
    back_norm, gain_two, shift_two = norm_back(back_normed_two, unit_two, scale_two, params[5])
    back_middle = grad_output + back_norm
    back_branch = back_middle.astype(BF16)
    back_mixed = contract_last(back_branch, merge).astype(BF16)
    back_mixed = back_mixed.reshape(micro, block, HEADS, HEAD_DIM)
    queries, keys, values = split_heads(packed, segment)
    attend = attention_weights(queries, keys, segment)
    back_attend = jnp.einsum("bqhd,bkhd->bhqk", back_mixed, values, preferred_element_type=F32)
    back_scores = attend * (back_attend - jnp.sum(attend * back_attend, axis=-1, keepdims=True))
    back_scores = back_scores.astype(BF16)
    factor = HEAD_DIM ** (-0.5)
    back_query = (
        jnp.einsum("bhqk,bkhd->bqhd", back_scores, keys, preferred_element_type=F32) * factor
    )
    back_key = (
        jnp.einsum("bhqk,bqhd->bkhd", back_scores, queries, preferred_element_type=F32) * factor
    )
    back_value = jnp.einsum(
        "bhqk,bqhd->bkhd", attend.astype(BF16), back_mixed, preferred_element_type=F32
    )
    back_packed = (
        jnp.stack([back_query, back_key, back_value], axis=2)
        .reshape(count, 3 * width)
        .astype(BF16)
    )
    back_normed = contract_last(back_packed, project)
    unit, scale = moments(inputs)
    back_norm, gain_one, shift_one = norm_back(back_normed, unit, scale, params[0])
    back_inputs = back_middle + back_norm

    def column_sums(values):
        return jnp.sum(values.astype(F32), axis=0)

    def vector_rows():
        rows = [
            gain_one,
            shift_one,
            column_sums(back_packed[:, :width]),
            column_sums(back_packed[:, 2 * width :]),
            column_sums(back_branch),
            gain_two,
            shift_two,
            column_sums(back_out),
        ]
        return jnp.concatenate(
            [jnp.stack(rows), column_sums(back_pre).reshape(4, width)], axis=0
        )

    return back_inputs, (back_out, back_pre, back_branch, back_packed), vector_rows


def weight_grad(left, right, here):
    count, width = left.shape
    rows = width // here.size
    cut = left.reshape(count, here.chips, 2, rows)
    kept = lax.dynamic_index_in_dim(cut, here.core, 2, keepdims=False).reshape(count, -1)
    sent = lax.dynamic_index_in_dim(cut, 1 - here.core, 2, keepdims=False).reshape(count, -1)
    kept = jnp.concatenate([kept, core_swap(sent, here.chips)], axis=0)
    both = jnp.concatenate([right, core_swap(right, here.chips)], axis=0)
    return contract_first(kept, both).reshape(here.chips, rows, right.shape[1])


def summed_grad(left, right, here):
    if not here.small:
        whole = contract_first(left, right).astype(BF16)
        return lax.psum_scatter(whole, "dp", scatter_dimension=0, tiled=True).astype(F32)
    return scatter_sum(weight_grad(left, right, here), here)


def per_device(
    frames,
    lengths,
    cotangent,
    project_weight,
    merge_weight,
    expand_weight,
    shrink_weight,
    vectors,
    project_row,
    project_col,
    merge_row,
    merge_col,
    expand_row,
    expand_col,
    shrink_row,
    shrink_col,
    vector_moment,
):
    here = Place()
    is_first = lax.axis_index("section") == 0
    micro = lengths.shape[0]
    count, width = frames.shape
    block = count // micro
    segment = jax.vmap(lambda lengths_row: segments(lengths_row, block))(lengths)
    live = (segment < UTTS).astype(F32).reshape(count, 1)

    vector_shard = vectors[0].astype(BF16)
    vector_whole = lax.all_gather(vector_shard, "dp", axis=0)
    params = vector_whole.transpose(1, 0, 2).reshape(vectors.shape[1], width).astype(F32)
    masters = (project_weight, merge_weight, expand_weight, shrink_weight)
    weights = tuple(gather_rows(master[0].astype(BF16), here) for master in masters) + (params,)

    start = frames.astype(F32)
    first_output, unused = forward_layer(start, weights, segment)
    inbox = section_shift(first_output.astype(BF16), 1)
    start = jnp.where(is_first, frames, inbox).astype(F32)
    output, kept = forward_layer(start, weights, segment)

    targets = cotangent.astype(F32) * live
    mail, unused, unused_rows = backward_layer(targets, kept, weights, segment)
    mailbox = section_shift(mail.astype(BF16), -1)
    incoming = jnp.where(is_first, mailbox.astype(F32), targets)
    back_inputs, carried, vector_rows = backward_layer(incoming, kept, weights, segment)
    back_out, back_pre, back_branch, back_packed = carried
    inputs, normed, packed, mixed, middle, normed_two, hidden_pre, hidden = kept

    shrink_grad = summed_grad(hidden, back_out, here)
    expand_grad = summed_grad(normed_two, back_pre, here)
    merge_grad = summed_grad(mixed, back_branch, here)
    project_grad = summed_grad(normed, back_packed, here)
    vector_grad = lax.psum_scatter(
        vector_rows().reshape(-1, here.size, width // here.size).transpose(1, 0, 2),
        "dp",
        scatter_dimension=0,
        tiled=False,
    )

    layer_outputs = output[None]
    rounded = lax.optimization_barrier(back_inputs.astype(BF16)).astype(F32)
    input_grads = jnp.where(is_first, back_inputs, rounded)[None]

    decay = 1.0 - STEP ** (-0.8)
    grads = (project_grad, merge_grad, expand_grad, shrink_grad)
    rows_old = (project_row, merge_row, expand_row, shrink_row)
    cols_old = (project_col, merge_col, expand_col, shrink_col)
    rows_new = []
    sums = []
    for grad, old in zip(grads, rows_old):
        square = grad * grad
        row_stat = decay * old[0] + (1.0 - decay) * jnp.mean(square + 1e-30, axis=1)
        column_part = jnp.sum(square + 1e-30, axis=0)
        norm_part = jnp.sum(square * (1.0 / row_stat)[:, None], axis=0)
        rows_new.append(row_stat)
        total = jnp.broadcast_to(jnp.sum(row_stat), (128,))
        sums.append(small_sum(jnp.concatenate([column_part, norm_part, total]), here))
    vector_second = decay * vector_moment[0] + (1.0 - decay) * (vector_grad * vector_grad + 1e-30)
    vector_update = vector_grad * lax.rsqrt(vector_second)
    vector_norm = small_sum(jnp.sum(vector_update * vector_update, axis=1), here)
    vector_scale = jnp.sqrt(vector_norm / width)[:, None]
    vector_updated = vectors[0] - VECTOR_RATE * vector_update / jnp.maximum(1.0, vector_scale)

    results = []
    for grad, master, row_stat, old, summed in zip(grads, masters, rows_new, cols_old, sums):
        full_rows = grad.shape[0] * here.size
        columns = grad.shape[1]
        col_stat = decay * old[0] + (1.0 - decay) * summed[:columns] / full_rows
        row_mean = summed[2 * columns] / full_rows
        norm = row_mean * jnp.sum(summed[columns : 2 * columns] / col_stat)
        scale = jnp.sqrt(norm / (full_rows * columns))
        update = grad * lax.rsqrt(row_stat / row_mean)[:, None] * lax.rsqrt(col_stat)[None, :]
        updated = master[0] - RATE * update / jnp.maximum(1.0, scale)
        results += [grad[None], row_stat[None], col_stat[None], updated[None]]
    return (
        layer_outputs,
        input_grads,
        *results,
        vector_grad[None],
        vector_second[None],
        vector_updated[None],
    )


def solution(mesh):
    placed = (
        P("dp", None),
        P("dp", None),
        P("dp", None),
        P("section", "dp", None),
        P("section", "dp", None),
        P("section", "dp", None),
        P("section", "dp", None),
        P("section", None, "dp"),
        P("section", "dp"),
        P("section", None),
        P("section", "dp"),
        P("section", None),
        P("section", "dp"),
        P("section", None),
        P("section", "dp"),
        P("section", None),
        P("section", None, "dp"),
    )
    matrix = (
        P("section", "dp", None),
        P("section", "dp"),
        P("section", None),
        P("section", "dp", None),
    )
    return jax.shard_map(
        per_device,
        mesh=mesh,
        in_specs=placed,
        out_specs=(
            P("section", "dp", None),
            P("section", "dp", None),
            *matrix,
            *matrix,
            *matrix,
            *matrix,
            P("section", None, "dp"),
            P("section", None, "dp"),
            P("section", None, "dp"),
        ),
        check_vma=False,
    )
```

```python
import math

import jax
import jax.numpy as jnp
from jax import lax
from jax.experimental import pallas as pl
from jax.experimental.pallas import tpu as pltpu
from jax.sharding import PartitionSpec as P

HEADS = 16
HEAD_DIM = 64
UTTS = 3
STEP = 10

EPSILON = 1e-05
RATE = 0.04
VECTOR_RATE = 0.25
MASKED = -1e30
BF16 = jnp.bfloat16
F32 = jnp.float32
VMEM = pl.BlockSpec(memory_space=pltpu.VMEM)
HBM = pl.BlockSpec(memory_space=pl.ANY)
LIMIT = 56 * 1024 * 1024


def dot(left, right):
    return lax.dot_general(left, right, (((1,), (0,)), ((), ())), preferred_element_type=F32)


def dot_last(left, right):
    return lax.dot_general(left, right, (((1,), (1,)), ((), ())), preferred_element_type=F32)


def dot_first(left, right):
    return lax.dot_general(left, right, (((0,), (0,)), ((), ())), preferred_element_type=F32)


def moments(values):
    centred = values - jnp.mean(values, axis=-1, keepdims=True)
    spread = jnp.mean(centred * centred, axis=-1, keepdims=True)
    scale = lax.rsqrt(spread + EPSILON)
    return centred * scale, scale


def norm_back(grad, unit, scale, gain):
    inner = grad * gain
    first = jnp.mean(inner, axis=-1, keepdims=True)
    second = jnp.mean(inner * unit, axis=-1, keepdims=True)
    return scale * (inner - first - unit * second)


def fetch(pairs, sems):
    copies = [
        pltpu.make_async_copy(source, target, sems.at[index])
        for index, (source, target) in enumerate(pairs)
    ]
    for copy in copies:
        copy.start()
    return copies


def half_masks():
    lane = lax.broadcasted_iota(jnp.int32, (1, 128), 1)
    low = jnp.where(lane < HEAD_DIM, 1.0, 0.0)
    return low.astype(BF16), (1.0 - low).astype(BF16)


def two_heads(tile, masks):
    return jnp.concatenate([tile * masks[0], tile * masks[1]], axis=0)


def side_by_side(both):
    half = both.shape[0] // 2
    return jnp.concatenate([both[:half], both[half:]], axis=1)


def weights_of(both_queries, keys, visible):
    scores = jnp.where(visible, dot_last(both_queries, keys) * HEAD_DIM**-0.5, MASKED)
    shifted = jnp.exp(scores - jnp.max(scores, axis=-1, keepdims=True))
    return shifted / jnp.sum(shifted, axis=-1, keepdims=True)


def attend_kernel(x_ref, mask_ref, vec_ref, pm0, pm1, a_ref, packed_ref, near_ref, far_ref, x1_ref, c_ref, w, sems):
    chips, pair, wide = w.shape[1:]
    heads = chips * HEAD_DIM
    cols = 3 * heads
    width = chips * pair
    count = x_ref.shape[0]
    block = mask_ref.shape[1]
    copies = fetch(
        [
            (pm0.at[:, :, :cols], w.at[0, :, :, :cols]),
            (pm0.at[:, :, cols:], w.at[0, :, :, cols:]),
            (pm1.at[:, :, :cols], w.at[1, :, :, :cols]),
            (pm1.at[:, :, cols:], w.at[1, :, :, cols:]),
        ],
        sems,
    )
    unit, unused = moments(x_ref[...].astype(F32))
    a_ref[...] = (unit * vec_ref[0:1] + vec_ref[1:2]).astype(BF16)
    masks = half_masks()
    for part in range(2):
        copies[2 * part].wait()
        own = slice(part * heads, part * heads + heads)
        o_ref = (near_ref, far_ref)[part]
        for third in range(3):
            matrix = w[part, :, :, third * heads : (third + 1) * heads].reshape(width, heads)
            result = dot(a_ref[...], matrix)
            if third == 0:
                result = result + vec_ref[2:3, own]
            if third == 2:
                result = result + vec_ref[3:4, own]
            at = part * cols + third * heads
            packed_ref[:, at : at + heads] = result.astype(BF16)
        for micro in range(count // block):
            rows = slice(micro * block, (micro + 1) * block)
            visible = mask_ref[micro] > 0.0
            visible = jnp.concatenate([visible, visible], axis=0)
            for tile in range(heads // 128):
                at = part * cols + tile * 128
                queries = packed_ref[rows, at : at + 128]
                keys = packed_ref[rows, at + heads : at + heads + 128]
                values = packed_ref[rows, at + 2 * heads : at + 2 * heads + 128]
                attend = weights_of(two_heads(queries, masks), keys, visible).astype(BF16)
                mixed = dot(side_by_side(attend), two_heads(values, masks))
                o_ref[rows, tile * 128 : (tile + 1) * 128] = mixed.astype(BF16)
        copies[2 * part + 1].wait()
        for side in range(2):
            at = slice(side * heads, (side + 1) * heads)
            matrix = w[part, :, side * HEAD_DIM : (side + 1) * HEAD_DIM, cols:].reshape(heads, heads)
            result = dot(o_ref[...], matrix)
            if part == 0:
                x1_ref[:, at] = x_ref[:, at].astype(F32) + result
            else:
                x1_ref[:, at] = x1_ref[:, at] + result + vec_ref[4:5, at]
    unit, unused = moments(x1_ref[...])
    c_ref[...] = (unit * vec_ref[5:6] + vec_ref[6:7]).astype(BF16)


def call(kernel, outs, scratch, args, specs, flops, size):
    return pl.pallas_call(
        kernel,
        out_shape=outs,
        in_specs=specs,
        out_specs=jax.tree.map(lambda unused: VMEM, outs),
        scratch_shapes=scratch,
        compiler_params=pltpu.CompilerParams(vmem_limit_bytes=LIMIT),
        cost_estimate=pl.CostEstimate(flops=flops, bytes_accessed=size, transcendentals=0),
    )(*args)


def array(shape, kind):
    return jax.ShapeDtypeStruct(shape, kind)


def attend_block(x, mask, vec, pm0, pm1):
    count, width = x.shape
    outs = (
        array((count, width), BF16),
        array((count, 3 * width), BF16),
        array((count, width // 2), BF16),
        array((count, width // 2), BF16),
        array((count, width), F32),
        array((count, width), BF16),
    )
    scratch = [pltpu.VMEM((2, *pm0.shape), BF16), pltpu.SemaphoreType.DMA((4,))]
    return call(attend_kernel, outs, scratch, (x, mask, vec, pm0, pm1), [VMEM] * 3 + [HBM] * 2, 8 * count * width * width, 20 << 20)


def gelu_parts(values):
    cdf = 0.5 * (1.0 + lax.erf(values * math.sqrt(0.5)))
    slope = cdf + values * jnp.exp(-0.5 * values * values) * (1.0 / math.sqrt(2.0 * math.pi))
    return values * cdf, slope


def expand_kernel(c_ref, bias_ref, e0, e1, near_ref, far_ref, slope_hbm, w, slope, sems, out_sems):
    half = w.shape[3] // 2
    width = w.shape[1] * w.shape[2]
    step = 256
    copies = fetch(
        [
            (matrix.at[:, :, side * half : (side + 1) * half], w.at[part, :, :, side * half : (side + 1) * half])
            for part, matrix in enumerate((e0, e1))
            for side in range(2)
        ],
        sems,
    )
    sent = []
    for index in range(4):
        copies[index].wait()
        part, side = index // 2, index % 2
        for cut in range(half // step):
            at = index * half + cut * step
            matrix = w[part, :, :, side * half + cut * step : side * half + (cut + 1) * step]
            result = dot(c_ref[...], matrix.reshape(width, step)) + bias_ref[:, at : at + step]
            hidden, rise = gelu_parts(result)
            to = side * half + cut * step
            (near_ref, far_ref)[part][:, to : to + step] = hidden.astype(BF16)
            slope[:, at : at + step] = rise
        at = slice(index * half, (index + 1) * half)
        copy = pltpu.make_async_copy(slope.at[:, at], slope_hbm.at[:, at], out_sems.at[index])
        copy.start()
        sent.append(copy)
    for copy in sent:
        copy.wait()


def expand_block(c, bias, e0, e1):
    count, width = c.shape
    hidden = bias.shape[1]
    return pl.pallas_call(
        expand_kernel,
        out_shape=(
            array((count, hidden // 2), BF16),
            array((count, hidden // 2), BF16),
            array((count, hidden), F32),
        ),
        in_specs=[VMEM, VMEM, HBM, HBM],
        out_specs=(VMEM, VMEM, HBM),
        scratch_shapes=[
            pltpu.VMEM((2, *e0.shape), BF16),
            pltpu.VMEM((count, hidden), F32),
            pltpu.SemaphoreType.DMA((4,)),
            pltpu.SemaphoreType.DMA((4,)),
        ],
        compiler_params=pltpu.CompilerParams(vmem_limit_bytes=LIMIT),
        cost_estimate=pl.CostEstimate(flops=2 * count * width * hidden, bytes_accessed=20 << 20, transcendentals=0),
    )(c, bias, e0, e1)


def shrink_kernel(x1_ref, near_ref, far_ref, vec_ref, s0, s1, y_ref, low_ref, w, sems):
    half = w.shape[3] // 2
    width = w.shape[1] * w.shape[2]
    copies = fetch(
        [
            (matrix.at[:, :, side * half : (side + 1) * half], w.at[part, :, :, side * half : (side + 1) * half])
            for part, matrix in enumerate((s0, s1))
            for side in range(2)
        ],
        sems,
    )
    for index in range(4):
        copies[index].wait()
        part, side = index // 2, index % 2
        left = (near_ref, far_ref)[part][:, side * width : (side + 1) * width]
        for cut in range(2):
            at = slice(cut * half // 2, (cut + 1) * half // 2)
            base = side * half + cut * half // 2
            result = dot(left, w[part, :, :, base : base + half // 2].reshape(width, half // 2))
            if index == 0:
                y_ref[:, at] = x1_ref[:, at] + result
            elif index < 3:
                y_ref[:, at] += result
            else:
                total = y_ref[:, at] + result + vec_ref[7:8, at]
                y_ref[:, at] = total
                low_ref[:, at] = total.astype(BF16)


def shrink_block(x1, near, far, vec, s0, s1):
    count, width = x1.shape
    outs = (array((count, width), F32), array((count, width), BF16))
    scratch = [pltpu.VMEM((2, *s0.shape), BF16), pltpu.SemaphoreType.DMA((4,))]
    return call(shrink_kernel, outs, scratch, (x1, near, far, vec, s0, s1), [VMEM] * 4 + [HBM] * 2, 8 * count * width * width, 16 << 20)


def back_hidden_kernel(dy_ref, x1_ref, vec_ref, s0, s1, e0, e1, slope_hbm, gf_ref, gu_ref, dx1_ref, gat_ref, sums_ref, bias_ref, ws, we, slope, dc, sems):
    half = ws.shape[3] // 2
    width = ws.shape[1] * ws.shape[2]
    pairs = []
    for index in range(4):
        part, side = index // 2, index % 2
        cut = slice(side * half, (side + 1) * half)
        at = slice(index * half, (index + 1) * half)
        pairs.append(((s0, s1)[part].at[:, :, cut], ws.at[part, :, :, cut]))
        pairs.append((slope_hbm.at[:, at], slope.at[:, at]))
        pairs.append(((e0, e1)[part].at[:, :, cut], we.at[part, :, :, cut]))
    copies = fetch(pairs, sems)
    gf_ref[...] = dy_ref[...].astype(BF16)
    for index in range(4):
        part, side = index // 2, index % 2
        cut = slice(side * half, (side + 1) * half)
        copies[3 * index].wait()
        copies[3 * index + 1].wait()
        for quarter in range(2):
            rows = slice(quarter * (ws.shape[1] // 2), (quarter + 1) * (ws.shape[1] // 2))
            matrix = ws[part, rows, :, cut].reshape(width // 2, half)
            at = slice(index * width + quarter * width // 2, index * width + (quarter + 1) * width // 2)
            back = (dot_last(gf_ref[...], matrix) * slope[:, at]).astype(BF16)
            gu_ref[:, at] = back
            bias_ref[:, at] = jnp.sum(back.astype(F32), axis=0, keepdims=True)
        copies[3 * index + 2].wait()
        left = gu_ref[:, index * width : (index + 1) * width]
        for quarter in range(2):
            rows = slice(quarter * (we.shape[1] // 2), (quarter + 1) * (we.shape[1] // 2))
            matrix = we[part, rows, :, cut].reshape(width // 2, half)
            at = slice(quarter * width // 2, (quarter + 1) * width // 2)
            result = dot_last(left, matrix)
            if index == 0:
                dc[:, at] = result
            else:
                dc[:, at] += result
    unit, scale = moments(x1_ref[...])
    grad = dc[...]
    back = dy_ref[...] + norm_back(grad, unit, scale, vec_ref[5:6])
    dx1_ref[...] = back
    gat_ref[...] = back.astype(BF16)
    sums_ref[...] = jnp.zeros_like(sums_ref)
    sums_ref[0:1] = jnp.sum(grad * unit, axis=0, keepdims=True)
    sums_ref[1:2] = jnp.sum(grad, axis=0, keepdims=True)
    sums_ref[2:3] = jnp.sum(gf_ref[...].astype(F32), axis=0, keepdims=True)
    sums_ref[3:4] = jnp.sum(gat_ref[...].astype(F32), axis=0, keepdims=True)


def back_hidden_block(dy, x1, vec, s0, s1, e0, e1, slope):
    count, width = x1.shape
    hidden = slope.shape[1]
    outs = (
        array((count, width), BF16),
        array((count, hidden), BF16),
        array((count, width), F32),
        array((count, width), BF16),
        array((8, width), F32),
        array((1, hidden), F32),
    )
    scratch = [
        pltpu.VMEM((2, *s0.shape), BF16),
        pltpu.VMEM((2, *e0.shape), BF16),
        pltpu.VMEM((count, hidden), F32),
        pltpu.VMEM((count, width), F32),
        pltpu.SemaphoreType.DMA((12,)),
    ]
    return call(back_hidden_kernel, outs, scratch, (dy, x1, vec, s0, s1, e0, e1, slope), [VMEM] * 3 + [HBM] * 5, 16 * count * width * width, 32 << 20)


def back_attend_kernel(x_ref, dx1_ref, gat_ref, packed_ref, mask_ref, vec_ref, pm0, pm1, gqkv_ref, dx_ref, low_ref, sums_ref, bias_ref, w, go, da, sems):
    chips, pair, wide = w.shape[1:]
    heads = chips * HEAD_DIM
    cols = 3 * heads
    width = chips * pair
    count = x_ref.shape[0]
    block = mask_ref.shape[1]
    copies = fetch(
        [
            (pm0.at[:, :, cols:], w.at[0, :, :, cols:]),
            (pm0.at[:, :, :cols], w.at[0, :, :, :cols]),
            (pm1.at[:, :, cols:], w.at[1, :, :, cols:]),
            (pm1.at[:, :, :cols], w.at[1, :, :, :cols]),
        ],
        sems,
    )
    masks = half_masks()
    factor = HEAD_DIM**-0.5
    for part in range(2):
        copies[2 * part].wait()
        total = None
        for side in range(2):
            matrix = w[part, :, side * HEAD_DIM : (side + 1) * HEAD_DIM, cols:].reshape(heads, heads)
            result = dot_last(gat_ref[:, side * heads : (side + 1) * heads], matrix)
            total = result if total is None else total + result
        go[...] = total.astype(BF16)
        for micro in range(count // block):
            rows = slice(micro * block, (micro + 1) * block)
            visible = mask_ref[micro] > 0.0
            visible = jnp.concatenate([visible, visible], axis=0)
            for tile in range(heads // 128):
                at = part * cols + tile * 128
                queries = two_heads(packed_ref[rows, at : at + 128], masks)
                keys = packed_ref[rows, at + heads : at + heads + 128]
                values = packed_ref[rows, at + 2 * heads : at + 2 * heads + 128]
                back = two_heads(go[rows, tile * 128 : (tile + 1) * 128], masks)
                attend = weights_of(queries, keys, visible)
                slope = dot_last(back, values)
                inner = jnp.sum(attend * slope, axis=-1, keepdims=True)
                scores = (attend * (slope - inner)).astype(BF16)
                grad_q = dot(side_by_side(scores), two_heads(keys, masks)) * factor
                grad_k = dot_first(scores, queries) * factor
                grad_v = dot_first(attend.astype(BF16), back)
                gqkv_ref[rows, at : at + 128] = grad_q.astype(BF16)
                gqkv_ref[rows, at + heads : at + heads + 128] = grad_k.astype(BF16)
                gqkv_ref[rows, at + 2 * heads : at + 2 * heads + 128] = grad_v.astype(BF16)
        copies[2 * part + 1].wait()
        for side in range(2):
            near = slice(side * (chips // 2), (side + 1) * (chips // 2))
            matrix = w[part, near, :, :cols].reshape(width // 2, cols)
            at = slice(side * width // 2, (side + 1) * width // 2)
            result = dot_last(gqkv_ref[:, part * cols : (part + 1) * cols], matrix)
            if part == 0:
                da[:, at] = result
            else:
                da[:, at] += result
    unit, scale = moments(x_ref[...].astype(F32))
    grad = da[...]
    back = dx1_ref[...] + norm_back(grad, unit, scale, vec_ref[0:1])
    dx_ref[...] = back
    low_ref[...] = back.astype(BF16)
    sums_ref[...] = jnp.zeros_like(sums_ref)
    sums_ref[0:1] = jnp.sum(grad * unit, axis=0, keepdims=True)
    sums_ref[1:2] = jnp.sum(grad, axis=0, keepdims=True)
    bias_ref[...] = jnp.sum(gqkv_ref[...].astype(F32), axis=0, keepdims=True)


def back_attend_block(x, dx1, gat, packed, mask, vec, pm0, pm1):
    count, width = x.shape
    outs = (
        array((count, 3 * width), BF16),
        array((count, width), F32),
        array((count, width), BF16),
        array((8, width), F32),
        array((1, 3 * width), F32),
    )
    scratch = [
        pltpu.VMEM((2, *pm0.shape), BF16),
        pltpu.VMEM((count, width // 2), BF16),
        pltpu.VMEM((count, width), F32),
        pltpu.SemaphoreType.DMA((4,)),
    ]
    return call(back_attend_kernel, outs, scratch, (x, dx1, gat, packed, mask, vec, pm0, pm1), [VMEM] * 6 + [HBM] * 2, 12 * count * width * width, 20 << 20)


def rows_grad_kernel(near_ref, far_ref, right_ref, other_ref, out_ref):
    rows = out_ref.shape[0]
    step = min(512, rows)
    for at in range(0, rows, step):
        cut = slice(at, at + step)
        total = dot_first(near_ref[:, cut], right_ref[...]) + dot_first(far_ref[:, cut], other_ref[...])
        out_ref[cut, :] = total.astype(out_ref.dtype)


def rows_grad(near, far, right, other):
    out = array((near.shape[1], right.shape[1]), BF16)
    return call(rows_grad_kernel, out, [], (near, far, right, other), [VMEM] * 4, 4 * near.shape[0] * out.shape[0] * out.shape[1], 8 << 20)


def own_rows(core_ref, near_ref, far_ref, turned):
    chips, unused, rows, both = turned.shape
    tokens = near_ref.shape[0]
    turned[:, :, :, :tokens] = near_ref[...].T.reshape(chips, 2, rows, tokens)
    turned[:, :, :, tokens:] = far_ref[...].T.reshape(chips, 2, rows, tokens)
    return turned[:, pl.ds(core_ref[0], 1)].reshape(chips * rows, both)


def expand_grad_kernel(core_ref, near_ref, far_ref, right_ref, other_ref, out_ref, turned):
    chips, rows, columns = out_ref.shape
    left = own_rows(core_ref, near_ref, far_ref, turned)
    half = columns // 2
    step = 512
    for at in range(0, columns, step):
        to = (at + half) % columns
        right = jnp.concatenate([right_ref[:, at : at + step], other_ref[:, to : to + step]], axis=0)
        out_ref[:, :, at : at + step] = dot(left, right).astype(BF16).reshape(chips, rows, step)


def expand_grad(core, near, far, right, other, chips):
    tokens, width = near.shape
    rows = width // chips // 2
    out = array((chips, rows, right.shape[1]), BF16)
    return call(
        expand_grad_kernel,
        out,
        [pltpu.VMEM((chips, 2, rows, 2 * tokens), BF16)],
        (core, near, far, right, other),
        [pl.BlockSpec(memory_space=pltpu.SMEM)] + [VMEM] * 4,
        2 * tokens * width * right.shape[1],
        12 << 20,
    )


def project_grad_kernel(core_ref, near_ref, far_ref, right_ref, other_ref, mixed_ref, mixed_far_ref, gat_ref, gat_far_ref, out_ref, turned):
    chips, rows, columns = out_ref.shape
    left = own_rows(core_ref, near_ref, far_ref, turned)
    cols = right_ref.shape[1]
    half = cols // 2
    step = 512
    for at in range(0, cols, step):
        to = (at + half) % cols
        right = jnp.concatenate([right_ref[:, at : at + step], other_ref[:, to : to + step]], axis=0)
        out_ref[:, :, at : at + step] = dot(left, right).astype(BF16).reshape(chips, rows, step)
    for at in range(0, columns - cols, step):
        cut = slice(at, at + step)
        total = dot_first(mixed_ref[...], gat_ref[:, cut]) + dot_first(mixed_far_ref[...], gat_far_ref[:, cut])
        out_ref[:, :, cols + at : cols + at + step] = total.astype(BF16).reshape(chips, rows, step)


def project_grad(core, near, far, right, other, mixed, mixed_far, gat, gat_far, chips):
    tokens, width = near.shape
    rows = width // chips // 2
    out = array((chips, rows, right.shape[1] + width), BF16)
    return call(
        project_grad_kernel,
        out,
        [pltpu.VMEM((chips, 2, rows, 2 * tokens), BF16)],
        (core, near, far, right, other, mixed, mixed_far, gat, gat_far),
        [pl.BlockSpec(memory_space=pltpu.SMEM)] + [VMEM] * 8,
        2 * tokens * width * 4 * width,
        12 << 20,
    )


class Place:
    def __init__(self):
        self.size = lax.axis_size("dp")
        self.chips = self.size // 2
        self.ring = list(range(0, self.chips, 2)) + list(range(self.chips - 1, 0, -2))
        self.small = self.size == HEADS
        index = lax.axis_index("dp")
        self.chip = index // 2
        self.core = index % 2 if self.small else jnp.zeros_like(index)
        where = [0] * self.chips
        for place, chip in enumerate(self.ring):
            where[chip] = place
        self.place = jnp.array(where, jnp.int32)[self.chip]

    def chip_at(self, offset):
        return jnp.array(self.ring, jnp.int32)[(self.place + offset) % self.chips]

    def permute(self, array, target):
        pairs = []
        for chip in range(self.chips):
            for core in range(2):
                to_chip, to_core = target(chip, core)
                pairs.append((chip * 2 + core, to_chip * 2 + to_core))
        return lax.ppermute(array, "dp", pairs)

    def shift(self, array, by):
        where = {chip: place for place, chip in enumerate(self.ring)}
        return self.permute(
            array, lambda chip, core: (self.ring[(where[chip] + by) % self.chips], core)
        )

    def swap(self, array):
        return self.permute(array, lambda chip, core: (chip, 1 - core))

    def cross(self, array, mask):
        return self.permute(array, lambda chip, core: (chip ^ mask, core))

    def masks(self):
        return [1 << bit for bit in range(self.chips.bit_length() - 1)]


def section_shift(array, by):
    size = lax.axis_size("section")
    pairs = [(i, i + by) for i in range(size) if 0 <= i + by < size]
    return lax.ppermute(array, "section", pairs)


def after(array, token):
    zero = jnp.minimum(jnp.abs(token.reshape(-1)[0].astype(F32)), 0.0)
    return array + zero.astype(array.dtype)


def ring_gather(own, here):
    rows, columns = own.shape
    half = here.chips // 2
    whole = jnp.zeros((here.chips, rows, columns), own.dtype)

    def put(whole, piece, offset, row=0):
        return lax.dynamic_update_slice(whole, piece[None], (here.chip_at(offset), row, 0))

    whole = put(whole, own, 0)
    ahead = behind = own
    for step in range(1, half):
        ahead = here.shift(ahead, 1)
        behind = here.shift(behind, -1)
        whole = put(put(whole, ahead, -step), behind, step)
    upper = here.shift(ahead[: rows // 2], 1)
    lower = here.shift(behind[rows // 2 :], -1)
    return put(put(whole, upper, half), lower, half, rows // 2), lower


def ring_sum(blocks, here):
    rows = blocks.shape[1]
    half = here.chips // 2
    cut = rows // 2

    def block(offset):
        return lax.dynamic_index_in_dim(blocks, here.chip_at(offset), 0, keepdims=False)

    far = block(half)
    ahead = here.shift(far[:cut], 1)
    behind = here.shift(far[cut:], -1)
    mine = block(half - 1)
    ahead = jnp.concatenate([(mine[:cut].astype(F32) + ahead.astype(F32)).astype(BF16), mine[cut:]], axis=0)
    mine = block(1 - half)
    behind = jnp.concatenate([mine[:cut], (mine[cut:].astype(F32) + behind.astype(F32)).astype(BF16)], axis=0)
    for step in range(half - 1, 0, -1):
        ahead = here.shift(ahead, 1)
        behind = here.shift(behind, -1)
        if step > 1:
            ahead = (ahead.astype(F32) + block(step - 1).astype(F32)).astype(BF16)
            behind = (behind.astype(F32) + block(1 - step).astype(F32)).astype(BF16)
    return block(0).astype(F32) + ahead.astype(F32) + behind.astype(F32)


def small_gather(own, here):
    if not here.small:
        return lax.all_gather(own, "dp", axis=0)
    other = here.swap(own)
    whole = jnp.where(here.core == 0, jnp.stack([own, other]), jnp.stack([other, own]))
    for bit, mask in enumerate(here.masks()):
        other = here.cross(whole, mask)
        low = (here.chip >> bit) % 2 == 0
        whole = jnp.where(low, jnp.concatenate([whole, other]), jnp.concatenate([other, whole]))
    return whole


def small_scatter(blocks, here):
    if not here.small:
        return lax.psum_scatter(blocks, "dp", scatter_dimension=0, tiled=False)
    size, rows, columns = blocks.shape
    cut = blocks.reshape(here.chips, 2, rows, columns)
    sent = jnp.where(here.core == 0, cut[:, 1], cut[:, 0])
    kept = jnp.where(here.core == 0, cut[:, 0], cut[:, 1]) + here.swap(sent)
    for bit in range(len(here.masks()) - 1, -1, -1):
        half = kept.shape[0] // 2
        low = (here.chip >> bit) % 2 == 0
        sent = jnp.where(low, kept[half:], kept[:half])
        kept = jnp.where(low, kept[:half], kept[half:]) + here.cross(sent, 1 << bit)
    return kept[0]


def small_sum(vector, here):
    if not here.small:
        return lax.psum(vector, "dp")
    vector = vector + here.swap(vector)
    for mask in here.masks():
        vector = vector + here.cross(vector, mask)
    return vector


PAIRS = HEADS // 2


def split_project(rows):
    count, columns = rows.shape
    cut = rows.reshape(count, 3, PAIRS, 2, HEAD_DIM).transpose(3, 0, 1, 2, 4)
    return cut.reshape(2, count, columns // 2)


def join_project(parts):
    unused, count, columns = parts.shape
    cut = parts.reshape(2, count, 3, PAIRS, HEAD_DIM).transpose(1, 2, 3, 0, 4)
    return cut.reshape(count, 2 * columns)


def split_expand(rows):
    count, columns = rows.shape
    cut = rows.reshape(count, PAIRS, 2, 2, columns // HEADS // 2).transpose(2, 0, 3, 1, 4)
    return cut.reshape(2, count, columns // 2)


def join_expand(parts):
    unused, count, columns = parts.shape
    cut = parts.reshape(2, count, 2, PAIRS, columns // HEADS).transpose(1, 3, 0, 2, 4)
    return cut.reshape(count, 2 * columns)


def pick(parts, core):
    return (
        jnp.where(core == 0, parts[0], parts[1]),
        jnp.where(core == 0, parts[1], parts[0]),
    )


def halves(rows, core):
    columns = rows.shape[1] // 2
    first, second = rows[:, :columns], rows[:, columns:]
    return jnp.where(core == 0, jnp.stack([first, second]), jnp.stack([second, first]))


def under(rows):
    columns = rows.shape[-1] // 2
    return jnp.concatenate([rows[..., :columns], rows[..., columns:]], axis=-2)


def beside(rows):
    count = rows.shape[-2] // 2
    return jnp.concatenate([rows[..., :count, :], rows[..., count:, :]], axis=-1)


def gather_weights(project, merge, expand, shrink, here):
    if not here.small:
        project, merge, expand, shrink = (
            lax.all_gather(rows, "dp", axis=0, tiled=True) for rows in (project, merge, expand, shrink)
        )
        width = project.shape[0]
        cut = split_project(project).reshape(2, PAIRS, width // PAIRS, -1)
        rows = merge.reshape(PAIRS, 2, HEAD_DIM, -1).transpose(1, 0, 2, 3)
        pm = jnp.concatenate([cut, under(rows)], axis=-1)
        e = split_expand(expand).reshape(2, PAIRS, width // PAIRS, -1)
        s = beside(shrink.reshape(PAIRS, 2, -1, width).transpose(1, 0, 2, 3))
        return tuple((parts[0], parts[1]) for parts in (pm, e, s))
    own_project, other_project = pick(split_project(project), here.core)
    own_expand, other_expand = pick(split_expand(expand), here.core)
    columns = own_project.shape[1]
    other = here.swap(jnp.concatenate([other_project, other_expand], axis=1))

    def pair(own, other):
        return jnp.where(
            here.core == 0, jnp.concatenate([own, other]), jnp.concatenate([other, own])
        )

    pm = jnp.concatenate([pair(own_project, other[:, :columns]), under(merge)], axis=1)
    e = pair(own_expand, other[:, columns:])
    pm, pm_token = ring_gather(pm, here)
    e, e_token = ring_gather(e, here)
    half = shrink.shape[0] // 2
    upper, unused = ring_gather(after(shrink[:half], pm_token), here)
    lower, unused = ring_gather(after(shrink[half:], e_token), here)
    s = jnp.concatenate([upper, lower], axis=-1)
    return tuple((own, here.swap(own)) for own in (pm, e, s))


def segments(lengths_row, count):
    ends = jnp.cumsum(lengths_row)
    places = jnp.arange(count, dtype=jnp.int32)
    return jnp.sum((places[:, None] >= ends[None, :]).astype(jnp.int32), axis=1)


def per_device(
    frames,
    lengths,
    cotangent,
    project_weight,
    merge_weight,
    expand_weight,
    shrink_weight,
    vectors,
    project_row,
    project_col,
    merge_row,
    merge_col,
    expand_row,
    expand_col,
    shrink_row,
    shrink_col,
    vector_moment,
):
    here = Place()
    core = here.core
    is_first = lax.axis_index("section") == 0
    micro = lengths.shape[0]
    count, width = frames.shape
    block = count // micro
    segment = jax.vmap(lambda lengths_row: segments(lengths_row, block))(lengths)
    live = (segment < UTTS).astype(F32).reshape(count, 1)
    visible = (segment[:, :, None] == segment[:, None, :]).astype(F32)

    masters = (project_weight, merge_weight, expand_weight, shrink_weight)
    pm, e, s = gather_weights(*(master[0].astype(BF16) for master in masters), here)
    rows = small_gather(vectors[0].astype(BF16), here).transpose(1, 0, 2)
    rows = rows.reshape(vectors.shape[1], width).astype(F32)

    def by_part(row):
        parts = row.reshape(PAIRS, 2, HEAD_DIM).transpose(1, 0, 2).reshape(2, width // 2)
        return jnp.concatenate(pick(parts, core))

    vec = jnp.concatenate(
        [rows[:2], by_part(rows[2])[None], by_part(rows[3])[None], rows[4:8]], axis=0
    )
    up_bias = jnp.concatenate(pick(split_expand(rows[8:12].reshape(1, 4 * width)), core), axis=1)

    def forward(start):
        normed, packed, near, far, middle, normed_two = attend_block(start, visible, vec, *pm)
        hidden, hidden_far, slope = expand_block(normed_two, up_bias, *e)
        output, low = shrink_block(middle, hidden, hidden_far, vec, *s)
        return output, low, (normed, packed, near, far, middle, normed_two, hidden, hidden_far, slope)

    unused, low, unused_kept = forward(frames)
    start = jnp.where(is_first, frames, section_shift(low, 1))
    output, unused, kept = forward(start)
    normed, packed, mixed, mixed_far, middle, normed_two, hidden, hidden_far, slope = kept

    def backward(incoming):
        low_out, back_pre, back_middle, back_branch, sums_two, sums_up = back_hidden_block(
            incoming, middle, vec, *s, *e, slope
        )
        back_packed, back_inputs, low, sums_one, sums_packed = back_attend_block(
            start, back_middle, back_branch, packed, visible, vec, *pm
        )
        sums = (sums_one, sums_two, sums_packed, sums_up)
        return back_inputs, low, (low_out, back_pre, back_branch, back_packed), sums

    targets = cotangent.astype(F32) * live
    unused, low, unused_carried, unused_sums = backward(targets)
    incoming = jnp.where(is_first, section_shift(low, -1).astype(F32), targets)
    back_inputs, low, carried, sums = backward(incoming)
    low_out, back_pre, back_branch, back_packed = carried
    layer_outputs = output[None]
    input_grads = jnp.where(is_first, back_inputs, low.astype(F32))[None]

    if here.small:
        core_at = core.reshape(1)
        shrink_sum = rows_grad(hidden, here.swap(hidden_far), incoming.astype(BF16), here.swap(incoming.astype(BF16)))
        shrink_sum = shrink_sum.reshape(2, PAIRS, -1, width).transpose(1, 0, 2, 3)
        shrink_grad = ring_sum(shrink_sum.reshape(PAIRS, -1, width), here)
        expand_sum = expand_grad(
            core_at, normed_two, here.swap(normed_two), back_pre, here.swap(back_pre), PAIRS
        )
        expand_grad_rows = ring_sum(expand_sum, here)
        both_sum = project_grad(
            core_at,
            normed,
            here.swap(normed),
            back_packed,
            here.swap(back_packed),
            mixed,
            here.swap(mixed_far),
            back_branch,
            here.swap(back_branch),
            PAIRS,
        )
        both = ring_sum(both_sum, here)
        project_grad_rows = both[:, : 3 * width]
        merge_grad = both[:, 3 * width :]
        project_grad_rows = join_project(halves(project_grad_rows, core))
        expand_grad_rows = join_expand(halves(expand_grad_rows, core))
    else:

        def total(rows):
            return lax.psum_scatter(
                rows.astype(BF16), "dp", scatter_dimension=0, tiled=True
            ).astype(F32)

        project_grad_rows = total(join_project(halves(dot_first(normed, back_packed), core)))
        merge_rows = dot_first(jnp.concatenate([mixed, mixed_far], axis=1), back_branch)
        merge_rows = merge_rows.reshape(2, PAIRS, HEAD_DIM, width).transpose(1, 0, 2, 3)
        merge_grad = total(merge_rows.reshape(width, width))
        expand_grad_rows = total(join_expand(halves(dot_first(normed_two, back_pre), core)))
        shrink_rows = dot_first(jnp.concatenate([hidden, hidden_far], axis=1), low_out)
        shrink_rows = shrink_rows.reshape(2, 2, PAIRS, -1, width).transpose(2, 0, 1, 3, 4)
        shrink_grad = total(shrink_rows.reshape(-1, width))

    sums_one, sums_two, sums_packed, sums_up = sums
    packed_rows = join_project(halves(sums_packed, core)).reshape(3, width)
    vector_rows = jnp.concatenate(
        [
            sums_one[:2],
            packed_rows[0:1],
            packed_rows[2:3],
            sums_two[3:4],
            sums_two[:3],
            join_expand(halves(sums_up, core)).reshape(4, width),
        ],
        axis=0,
    )
    vector_rows = vector_rows.reshape(-1, here.size, width // here.size).transpose(1, 0, 2)
    vector_grad = small_scatter(vector_rows, here)

    decay = 1.0 - STEP ** (-0.8)
    grads = (project_grad_rows, merge_grad, expand_grad_rows, shrink_grad)
    rows_old = (project_row, merge_row, expand_row, shrink_row)
    cols_old = (project_col, merge_col, expand_col, shrink_col)
    rows_new = []
    sums = []
    for grad, old in zip(grads, rows_old):
        square = grad * grad
        row_stat = decay * old[0] + (1.0 - decay) * jnp.mean(square + 1e-30, axis=1)
        column_part = jnp.sum(square + 1e-30, axis=0)
        norm_part = jnp.sum(square * (1.0 / row_stat)[:, None], axis=0)
        rows_new.append(row_stat)
        total_row = jnp.broadcast_to(jnp.sum(row_stat), (128,))
        sums.append(small_sum(jnp.concatenate([column_part, norm_part, total_row]), here))
    vector_second = decay * vector_moment[0] + (1.0 - decay) * (vector_grad * vector_grad + 1e-30)
    vector_update = vector_grad * lax.rsqrt(vector_second)
    vector_norm = small_sum(jnp.sum(vector_update * vector_update, axis=1), here)
    vector_scale = jnp.sqrt(vector_norm / width)[:, None]
    vector_updated = vectors[0] - VECTOR_RATE * vector_update / jnp.maximum(1.0, vector_scale)

    results = []
    for grad, master, row_stat, old, summed in zip(grads, masters, rows_new, cols_old, sums):
        full_rows = grad.shape[0] * here.size
        columns = grad.shape[1]
        col_stat = decay * old[0] + (1.0 - decay) * summed[:columns] / full_rows
        row_mean = summed[2 * columns] / full_rows
        norm = row_mean * jnp.sum(summed[columns : 2 * columns] / col_stat)
        scale = jnp.sqrt(norm / (full_rows * columns))
        update = grad * lax.rsqrt(row_stat / row_mean)[:, None] * lax.rsqrt(col_stat)[None, :]
        updated = master[0] - RATE * update / jnp.maximum(1.0, scale)
        results += [grad[None], row_stat[None], col_stat[None], updated[None]]
    return (
        layer_outputs,
        input_grads,
        *results,
        vector_grad[None],
        vector_second[None],
        vector_updated[None],
    )


def solution(mesh):
    placed = (
        P("dp", None),
        P("dp", None),
        P("dp", None),
        P("section", "dp", None),
        P("section", "dp", None),
        P("section", "dp", None),
        P("section", "dp", None),
        P("section", None, "dp"),
        P("section", "dp"),
        P("section", None),
        P("section", "dp"),
        P("section", None),
        P("section", "dp"),
        P("section", None),
        P("section", "dp"),
        P("section", None),
        P("section", None, "dp"),
    )
    matrix = (
        P("section", "dp", None),
        P("section", "dp"),
        P("section", None),
        P("section", "dp", None),
    )
    return jax.shard_map(
        per_device,
        mesh=mesh,
        in_specs=placed,
        out_specs=(
            P("section", "dp", None),
            P("section", "dp", None),
            *matrix,
            *matrix,
            *matrix,
            *matrix,
            P("section", None, "dp"),
            P("section", None, "dp"),
            P("section", None, "dp"),
        ),
        check_vma=False,
    )
```

```python
import functools
import math

import jax
import jax.numpy as jnp
from jax import lax
from jax.experimental import pallas as pl
from jax.experimental.pallas import tpu as pltpu
from jax.sharding import PartitionSpec as P

HEADS = 16
HEAD_DIM = 64
PAIRS = HEADS // 2
UTTS = 3
STEP = 10

EPSILON = 1e-05
RATE = 0.04
VECTOR_RATE = 0.25
MASKED = -1e30
BF16 = jnp.bfloat16
F32 = jnp.float32
VMEM = pl.BlockSpec(memory_space=pltpu.VMEM)
HBM = pl.BlockSpec(memory_space=pl.ANY)
MIB = 1024 * 1024


def dot(left, right):
    return lax.dot_general(left, right, (((1,), (0,)), ((), ())), preferred_element_type=F32)


def dot_last(left, right):
    return lax.dot_general(left, right, (((1,), (1,)), ((), ())), preferred_element_type=F32)


def dot_first(left, right):
    return lax.dot_general(left, right, (((0,), (0,)), ((), ())), preferred_element_type=F32)


def moments(values):
    centred = values - jnp.mean(values, axis=-1, keepdims=True)
    spread = jnp.mean(centred * centred, axis=-1, keepdims=True)
    scale = lax.rsqrt(spread + EPSILON)
    return centred * scale, scale


def norm_back(grad, unit, scale, gain):
    inner = grad * gain
    first = jnp.mean(inner, axis=-1, keepdims=True)
    second = jnp.mean(inner * unit, axis=-1, keepdims=True)
    return scale * (inner - first - unit * second)


def fetch(pairs, sems):
    copies = [
        pltpu.make_async_copy(source, target, sems.at[index])
        for index, (source, target) in enumerate(pairs)
    ]
    for copy in copies:
        copy.start()
    return copies


def half_masks():
    lane = lax.broadcasted_iota(jnp.int32, (1, 128), 1)
    low = jnp.where(lane < HEAD_DIM, 1.0, 0.0)
    return low.astype(BF16), (1.0 - low).astype(BF16)


def two_heads(tile, masks):
    return jnp.concatenate([tile * masks[0], tile * masks[1]], axis=0)


def side_by_side(both):
    half = both.shape[0] // 2
    return jnp.concatenate([both[:half], both[half:]], axis=1)


def weights_of(both_queries, keys, visible):
    scores = jnp.where(visible, dot_last(both_queries, keys) * HEAD_DIM**-0.5, MASKED)
    shifted = jnp.exp(scores - jnp.max(scores, axis=-1, keepdims=True))
    return shifted / jnp.sum(shifted, axis=-1, keepdims=True)


def scalars():
    return pl.BlockSpec(memory_space=pltpu.SMEM)


def array(shape, kind):
    return jax.ShapeDtypeStruct(shape, kind)


def call(kernel, outs, args, in_specs, out_specs, scratch, flops, size, behind=(), limit=12):
    given = len(args)

    def body(*refs):
        kernel(*refs[:given], *refs[given + len(behind) :])

    return pl.pallas_call(
        body,
        out_shape=outs,
        in_specs=[*in_specs, *(HBM for unused in behind)],
        out_specs=out_specs,
        scratch_shapes=scratch,
        compiler_params=pltpu.CompilerParams(vmem_limit_bytes=limit * MIB),
        cost_estimate=pl.CostEstimate(flops=flops, bytes_accessed=size, transcendentals=0),
    )(*args, *behind)


def both_cores(core, near, far, whole, cuts):
    pairs = []
    for cut in cuts:
        pairs.append((near.at[cut], whole.at[cut[0], core, *cut[1:]]))
        pairs.append((far.at[cut], whole.at[cut[0], 1 - core, *cut[1:]]))
    return pairs


ALL = slice(None)


def quarters_of(core, near, far, whole, order):
    rows = whole.shape[3]
    pairs = []
    for at in order:
        pairs.append((near.at[:, pl.ds(at * rows, rows)], whole.at[at, :, core]))
        pairs.append((far.at[:, pl.ds(at * rows, rows)], whole.at[at, :, 1 - core]))
    return pairs


def quarters_scratch(width):
    return pltpu.VMEM((4, PAIRS, 2, width // HEADS, width), BF16)


def columns_cut(start, size):
    return (ALL, ALL, pl.ds(start, size))


def attend_kernel(core_ref, x_ref, mask_ref, vec_ref, near, far, a_ref, packed_ref, o_ref, x1_ref, c_ref, w, sems):
    count, width = x_ref.shape
    block = mask_ref.shape[1]
    step = 512
    copies = fetch(quarters_of(core_ref[0], near, far, w, range(4)), sems)
    unit, unused = moments(x_ref[...].astype(F32))
    a_ref[...] = (unit * vec_ref[0:1] + vec_ref[1:2]).astype(BF16)
    for third in range(3):
        copies[2 * third].wait()
        copies[2 * third + 1].wait()
        for cut in range(width // step):
            at = third * width + cut * step
            matrix = w[third, :, :, :, cut * step : (cut + 1) * step].reshape(width, step)
            result = dot(a_ref[...], matrix)
            if third != 1:
                row = 2 if third == 0 else 3
                result = result + vec_ref[row : row + 1, cut * step : (cut + 1) * step]
            packed_ref[:, at : at + step] = result.astype(BF16)
    masks = half_masks()
    for micro in range(count // block):
        rows = slice(micro * block, (micro + 1) * block)
        visible = mask_ref[micro] > 0.0
        visible = jnp.concatenate([visible, visible], axis=0)
        for at in range(0, width, 128):
            queries = packed_ref[rows, at : at + 128]
            keys = packed_ref[rows, at + width : at + width + 128]
            values = packed_ref[rows, at + 2 * width : at + 2 * width + 128]
            attend = weights_of(two_heads(queries, masks), keys, visible).astype(BF16)
            mixed = dot(side_by_side(attend), two_heads(values, masks))
            o_ref[rows, at : at + 128] = mixed.astype(BF16)
    copies[6].wait()
    copies[7].wait()
    for at in range(0, width, step):
        cut = slice(at, at + step)
        matrix = w[3, :, :, :, cut].reshape(width, step)
        x1_ref[:, cut] = x_ref[:, cut].astype(F32) + (dot(o_ref[...], matrix) + vec_ref[4:5, cut])
    unit, unused = moments(x1_ref[...])
    c_ref[...] = (unit * vec_ref[5:6] + vec_ref[6:7]).astype(BF16)


def whole_of(near):
    chips, rows, columns = near.shape
    return pltpu.VMEM((chips, 2, rows, columns), near.dtype)


def attend_block(core, x, mask, vec, pm):
    count, width = x.shape
    low = array((count, width), BF16)
    return call(
        attend_kernel,
        (low, array((count, 3 * width), BF16), low, array((count, width), F32), low),
        (core, x, mask, vec, *pm),
        [scalars()] + [VMEM] * 3 + [HBM] * 2,
        (VMEM,) * 5,
        [quarters_scratch(width), pltpu.SemaphoreType.DMA((8,))],
        8 * count * width * width,
        20 << 20,
        limit=32,
    )


def gelu_parts(values):
    cdf = 0.5 * (1.0 + lax.erf(values * math.sqrt(0.5)))
    slope = cdf + values * jnp.exp(-0.5 * values * values) * (1.0 / math.sqrt(2.0 * math.pi))
    return values * cdf, slope


def expand_kernel(core_ref, c_ref, vec_ref, near, far, hidden_ref, slope_hbm, w, slope, sems, out_sems):
    count, width = c_ref.shape
    step = 256
    quarters = w.shape[3] // width
    copies = fetch(
        both_cores(core_ref[0], near, far, w, [columns_cut(at * width, width) for at in range(quarters)]), sems
    )
    sent = []
    for quarter in range(quarters):
        copies[2 * quarter].wait()
        copies[2 * quarter + 1].wait()
        for cut in range(width // step):
            at = quarter * width + cut * step
            result = dot(c_ref[...], w[:, :, :, at : at + step].reshape(width, step))
            bias = vec_ref[8 + quarter : 9 + quarter, cut * step : (cut + 1) * step]
            hidden, rise = gelu_parts(result + bias)
            hidden_ref[:, at : at + step] = hidden.astype(BF16)
            slope[:, at : at + step] = rise
        at = slice(quarter * width, (quarter + 1) * width)
        copy = pltpu.make_async_copy(slope.at[:, at], slope_hbm.at[:, at], out_sems.at[quarter])
        copy.start()
        sent.append(copy)
    for copy in sent:
        copy.wait()


def expand_block(core, c, vec, e):
    count, width = c.shape
    hidden = 4 * width
    return call(
        expand_kernel,
        (array((count, hidden), BF16), array((count, hidden), F32)),
        (core, c, vec, *e),
        [scalars()] + [VMEM] * 2 + [HBM] * 2,
        (VMEM, HBM),
        [
            whole_of(e[0]),
            pltpu.VMEM((count, hidden), F32),
            pltpu.SemaphoreType.DMA((8,)),
            pltpu.SemaphoreType.DMA((4,)),
        ],
        2 * count * width * hidden,
        20 << 20,
        limit=32,
    )


def shrink_kernel(core_ref, x1_ref, hidden_ref, vec_ref, near, far, y_ref, low_ref, w, sems):
    chips, unused, rows, width = w.shape
    step = 512
    group = width // (2 * rows)
    copies = fetch(
        both_cores(core_ref[0], near, far, w, [(pl.ds(at, group),) for at in range(0, chips, group)]), sems
    )
    for index in range(chips // group):
        copies[2 * index].wait()
        copies[2 * index + 1].wait()
        left = hidden_ref[:, index * width : (index + 1) * width]
        for at in range(0, width, step):
            cut = slice(at, at + step)
            matrix = w[index * group : (index + 1) * group, :, :, cut].reshape(width, step)
            result = dot(left, matrix)
            if index == 0:
                y_ref[:, cut] = x1_ref[:, cut] + result
            elif index < chips // group - 1:
                y_ref[:, cut] += result
            else:
                total = y_ref[:, cut] + result + vec_ref[7:8, cut]
                y_ref[:, cut] = total
                low_ref[:, cut] = total.astype(BF16)


def shrink_block(core, x1, hidden, vec, s, behind=()):
    count, width = x1.shape
    return call(
        shrink_kernel,
        (array((count, width), F32), array((count, width), BF16)),
        (core, x1, hidden, vec, *s),
        [scalars()] + [VMEM] * 3 + [HBM] * 2,
        (VMEM, VMEM),
        [whole_of(s[0]), pltpu.SemaphoreType.DMA((8,))],
        8 * count * width * width,
        16 << 20,
        behind=behind,
        limit=28,
    )


def back_hidden_kernel(core_ref, dy_ref, x1_ref, vec_ref, s_near, s_far, e_near, e_far, slope_hbm, gf_ref, gu_ref, dx1_ref, gat_ref, sums_ref, bias_ref, ws, we, slope, dc, sems, slope_sems):
    chips, unused, rows, width = ws.shape
    group = width // (2 * rows)
    quarters = chips // group
    core = core_ref[0]
    pairs = []
    for index in range(quarters):
        at = pl.ds(index * width, width)
        pairs += both_cores(core, s_near, s_far, ws, [(pl.ds(index * group, group),)])
        pairs.append((slope_hbm.at[:, at], slope.at[:, at]))
        pairs += both_cores(core, e_near, e_far, we, [columns_cut(index * width, width)])
    copies = fetch(pairs, sems)
    gf_ref[...] = dy_ref[...].astype(BF16)
    step = 512
    for index in range(quarters):
        for copy in copies[5 * index : 5 * index + 3]:
            copy.wait()
        for near in range(group):
            matrix = ws[index * group + near].reshape(2 * rows, width)
            at = slice(index * width + near * 2 * rows, index * width + (near + 1) * 2 * rows)
            back = (dot_last(gf_ref[...], matrix) * slope[:, at]).astype(BF16)
            gu_ref[:, at] = back
            bias_ref[:, at] = jnp.sum(back.astype(F32), axis=0, keepdims=True)
        for copy in copies[5 * index + 3 : 5 * index + 5]:
            copy.wait()
        at = slice(index * width, (index + 1) * width)
        left = gu_ref[:, at]
        for half in range(2):
            matrix = we[half * (chips // 2) : (half + 1) * (chips // 2), :, :, at].reshape(step, width)
            to = slice(half * step, (half + 1) * step)
            result = dot_last(left, matrix)
            if index == 0:
                dc[:, to] = result
            else:
                dc[:, to] += result
    unit, scale = moments(x1_ref[...])
    grad = dc[...]
    back = dy_ref[...] + norm_back(grad, unit, scale, vec_ref[5:6])
    dx1_ref[...] = back
    gat_ref[...] = back.astype(BF16)
    sums_ref[...] = jnp.zeros_like(sums_ref)
    sums_ref[0:1] = jnp.sum(grad * unit, axis=0, keepdims=True)
    sums_ref[1:2] = jnp.sum(grad, axis=0, keepdims=True)
    sums_ref[2:3] = jnp.sum(gf_ref[...].astype(F32), axis=0, keepdims=True)
    sums_ref[3:4] = jnp.sum(gat_ref[...].astype(F32), axis=0, keepdims=True)


def back_hidden_block(core, dy, x1, vec, s, e, slope, behind):
    count, width = x1.shape
    hidden = slope.shape[1]
    return call(
        back_hidden_kernel,
        (
            array((count, width), BF16),
            array((count, hidden), BF16),
            array((count, width), F32),
            array((count, width), BF16),
            array((8, width), F32),
            array((1, hidden), F32),
        ),
        (core, dy, x1, vec, *s, *e, slope),
        [scalars()] + [VMEM] * 3 + [HBM] * 5,
        (VMEM,) * 6,
        [
            whole_of(s[0]),
            whole_of(e[0]),
            pltpu.VMEM((count, hidden), F32),
            pltpu.VMEM((count, width), F32),
            pltpu.SemaphoreType.DMA((20,)),
            pltpu.SemaphoreType.DMA((4,)),
        ],
        16 * count * width * width,
        32 << 20,
        behind,
        limit=48,
    )


def back_attend_kernel(core_ref, first_ref, x_ref, dx1_ref, gat_ref, packed_ref, mask_ref, vec_ref, two_ref, up_ref, near, far, gqkv_ref, dx_ref, low_ref, sums_ref, w, go, sems):
    count, width = x_ref.shape
    block = mask_ref.shape[1]
    step = 512
    copies = fetch(quarters_of(core_ref[0], near, far, w, (3, 0, 1, 2)), sems)
    masks = half_masks()
    factor = HEAD_DIM**-0.5
    copies[0].wait()
    copies[1].wait()
    chips = w.shape[1]
    for half in range(2):
        matrix = w[3, half * (chips // 2) : (half + 1) * (chips // 2)].reshape(step, width)
        go[:, half * step : (half + 1) * step] = dot_last(gat_ref[...], matrix).astype(BF16)
    for micro in range(count // block):
        rows = slice(micro * block, (micro + 1) * block)
        visible = mask_ref[micro] > 0.0
        visible = jnp.concatenate([visible, visible], axis=0)
        for at in range(0, width, 128):
            queries = two_heads(packed_ref[rows, at : at + 128], masks)
            keys = packed_ref[rows, at + width : at + width + 128]
            values = packed_ref[rows, at + 2 * width : at + 2 * width + 128]
            back = two_heads(go[rows, at : at + 128], masks)
            attend = weights_of(queries, keys, visible)
            slope = dot_last(back, values)
            inner = jnp.sum(attend * slope, axis=-1, keepdims=True)
            scores = (attend * (slope - inner)).astype(BF16)
            grad_q = dot(side_by_side(scores), two_heads(keys, masks)) * factor
            grad_k = dot_first(scores, queries) * factor
            grad_v = dot_first(attend.astype(BF16), back)
            gqkv_ref[rows, at : at + 128] = grad_q.astype(BF16)
            gqkv_ref[rows, at + width : at + width + 128] = grad_k.astype(BF16)
            gqkv_ref[rows, at + 2 * width : at + 2 * width + 128] = grad_v.astype(BF16)
    for copy in copies[2:]:
        copy.wait()
    for half in range(2):
        total = None
        for third in range(3):
            matrix = w[third, half * (chips // 2) : (half + 1) * (chips // 2)].reshape(step, width)
            result = dot_last(gqkv_ref[:, third * width : (third + 1) * width], matrix)
            total = result if total is None else total + result
        dx_ref[:, half * step : (half + 1) * step] = total
    unit, scale = moments(x_ref[...].astype(F32))
    grad = dx_ref[...]
    sums_ref[...] = jnp.zeros_like(sums_ref)
    sums_ref[0:1] = jnp.sum(grad * unit, axis=0, keepdims=True)
    sums_ref[1:2] = jnp.sum(grad, axis=0, keepdims=True)
    back = dx1_ref[...] + norm_back(grad, unit, scale, vec_ref[0:1])
    low = back.astype(BF16)
    low_ref[...] = low
    dx_ref[...] = jnp.where(first_ref[0] == 1, back, low.astype(F32))
    for row, third in ((2, 0), (3, 2)):
        part = gqkv_ref[:, third * width : (third + 1) * width]
        sums_ref[row : row + 1] = jnp.sum(part.astype(F32), axis=0, keepdims=True)
    sums_ref[4:5] = two_ref[3:4]
    sums_ref[5:8] = two_ref[0:3]
    for quarter in range(4):
        sums_ref[8 + quarter : 9 + quarter] = up_ref[:, quarter * width : (quarter + 1) * width]


def back_attend_block(core, first, x, dx1, gat, packed, mask, vec, two, up, pm, behind):
    count, width = x.shape
    return call(
        back_attend_kernel,
        (
            array((count, 3 * width), BF16),
            array((count, width), F32),
            array((count, width), BF16),
            array((16, width), F32),
        ),
        (core, first, x, dx1, gat, packed, mask, vec, two, up, *pm),
        [scalars()] * 2 + [VMEM] * 8 + [HBM] * 2,
        (VMEM,) * 4,
        [quarters_scratch(width), pltpu.VMEM((count, width), BF16), pltpu.SemaphoreType.DMA((8,))],
        12 * count * width * width,
        20 << 20,
        behind,
        limit=32,
    )


def incoming_kernel(first_ref, mail_ref, cotangent_ref, live_ref, out_ref, low_ref):
    targets = cotangent_ref[...].astype(F32) * live_ref[...]
    mail = mail_ref[...].astype(F32)
    out = jnp.where(first_ref[0] == 1, mail, targets)
    out_ref[...] = out
    low_ref[...] = out.astype(BF16)


def incoming_grad(first, mail, cotangent, live, behind):
    shape = cotangent.shape
    return call(
        incoming_kernel,
        (array(shape, F32), array(shape, BF16)),
        (first, mail, cotangent, live),
        [scalars()] + [VMEM] * 3,
        (VMEM, VMEM),
        [],
        0,
        10 * cotangent.size,
        behind,
    )


def shrink_grad_kernel(core_ref, near_ref, far_ref, right_ref, other_ref, out_ref):
    chips, rows, width = out_ref.shape
    for chip in range(chips):
        at = pl.ds(pl.multiple_of((2 * chip + core_ref[0]) * rows, rows), rows)
        total = dot_first(near_ref[:, at], right_ref[...]) + dot_first(far_ref[:, at], other_ref[...])
        out_ref[chip] = total.astype(BF16)


def shrink_grad(core, near, far, right, other, behind):
    tokens, hidden = near.shape
    width = right.shape[1]
    return call(
        shrink_grad_kernel,
        array((PAIRS, hidden // HEADS, width), BF16),
        (core, near, far, right, other),
        [scalars()] + [VMEM] * 4,
        VMEM,
        [],
        2 * tokens * width * hidden,
        12 << 20,
        behind,
        limit=24,
    )


def own_rows(core, near_ref, far_ref, turned):
    chips, unused, rows, both = turned.shape
    tokens = near_ref.shape[0]
    turned[:, :, :, :tokens] = near_ref[...].T.reshape(chips, 2, rows, tokens)
    turned[:, :, :, tokens:] = far_ref[...].T.reshape(chips, 2, rows, tokens)
    return turned[:, pl.ds(core, 1)].reshape(chips * rows, both)


def own_columns_grad(left, right_ref, other_ref, cut):
    right = jnp.concatenate([right_ref[:, cut], other_ref[:, cut]], axis=0)
    return dot(left, right).astype(BF16)


def expand_grad_kernel(core_ref, near_ref, far_ref, right_ref, other_ref, out_ref, turned):
    chips, rows, columns = out_ref.shape
    left = own_rows(core_ref[0], near_ref, far_ref, turned)
    step = 512
    for at in range(0, columns, step):
        cut = slice(at, at + step)
        out_ref[:, :, cut] = own_columns_grad(left, right_ref, other_ref, cut).reshape(chips, rows, step)


def turned_scratch(tokens, width):
    return pltpu.VMEM((PAIRS, 2, width // HEADS, 2 * tokens), BF16)


def expand_grad(core, near, far, right, other, behind):
    tokens, width = near.shape
    hidden = right.shape[1]
    return call(
        expand_grad_kernel,
        array((PAIRS, width // HEADS, hidden), BF16),
        (core, near, far, right, other),
        [scalars()] + [VMEM] * 4,
        VMEM,
        [turned_scratch(tokens, width)],
        2 * tokens * width * hidden,
        12 << 20,
        behind=behind,
        limit=24,
    )


def project_grad_kernel(core_ref, a_ref, a_far, packed_ref, packed_far, o_ref, o_far, gat_ref, gat_far, vec_ref, vec_far, out_ref, turned):
    chips, unused, width = out_ref.shape
    rows = width // HEADS
    core = core_ref[0]
    step = 512
    left = own_rows(core, a_ref, a_far, turned)
    for third in range(3):
        for at in range(0, width, step):
            result = own_columns_grad(left, packed_ref, packed_far, slice(third * width + at, third * width + at + step))
            out_ref[:, third * rows : (third + 1) * rows, at : at + step] = result.reshape(chips, rows, step)
    left = own_rows(core, o_ref, o_far, turned)
    for at in range(0, width, step):
        result = own_columns_grad(left, gat_ref, gat_far, slice(at, at + step))
        out_ref[:, 3 * rows : 4 * rows, at : at + step] = result.reshape(chips, rows, step)
    total = vec_ref[...] + vec_far[...]
    for chip in range(chips):
        pair = total[:, chip * 2 * rows : (chip + 1) * 2 * rows]
        turn = jnp.concatenate([pair[:, rows:], pair[:, :rows]], axis=1)
        own = jnp.where(core == 0, pair, turn)
        out_ref[chip, 4 * rows :, : 2 * rows] = own.astype(BF16)
        out_ref[chip, 4 * rows :, 2 * rows :] = jnp.zeros((own.shape[0], width - 2 * rows), BF16)


def project_grad(core, operands, behind):
    tokens, width = operands[0].shape
    rows = width // HEADS
    return call(
        project_grad_kernel,
        array((PAIRS, 4 * rows + 16, width), BF16),
        (core, *operands),
        [scalars()] + [VMEM] * len(operands),
        VMEM,
        [turned_scratch(tokens, width)],
        8 * tokens * width * width,
        12 << 20,
        behind=behind,
        limit=24,
    )


DECAY = 1.0 - STEP ** (-0.8)
LANES = 128


def sums_at(cuts, columns):
    lines = sum(blocks for first, rows, blocks in cuts) * columns // LANES
    return lines, 2 * lines, 2 * lines + 8


def turned_row(row):
    return jnp.sum(jnp.where(diagonal(row.shape[1]), row, 0.0), axis=1, keepdims=True)


def turned_column(column):
    return jnp.sum(jnp.where(diagonal(column.shape[0]), column, 0.0), axis=0, keepdims=True)


def diagonal(count):
    rows = lax.broadcasted_iota(jnp.int32, (count, count), 0)
    return rows == lax.broadcasted_iota(jnp.int32, (count, count), 1)


def finish_kernel(addends, cuts, with_vectors, *refs):
    parts = len(cuts)
    refs = list(refs)

    def take(count):
        taken = refs[:count]
        del refs[:count]
        return taken

    if addends > 1:
        (chips_ref, blocks), addend_refs = take(2), take(addends - 1)
    else:
        addend_refs = take(1)
    old_refs = take(parts)
    moment_refs = take(int(with_vectors))
    grad_refs, row_refs = take(parts), take(parts)
    vector_refs = take(2 * int(with_vectors))
    (sums_ref,) = take(1)
    if addends > 1:
        own, sems = refs
        for copy in fetch([(blocks.at[chips_ref[0]], own)], sems):
            copy.wait()
        addend_refs.append(own)
    columns = addend_refs[0].shape[1]
    norms, totals, vector_line = sums_at(cuts, columns)

    def sum_of(rows, cut):
        total = None
        for ref in addend_refs:
            value = ref[rows, cut].astype(F32)
            total = value if total is None else total + value
        return total

    sums_ref[totals : totals + 8] = jnp.zeros((8, LANES), F32)
    line = 0
    for part, (first, rows, blocks) in enumerate(cuts):
        row_sum = None
        for block in range(blocks):
            grad = sum_of(slice(first + block * rows, first + (block + 1) * rows), ALL)
            cut = slice(block * columns, (block + 1) * columns)
            grad_refs[part][:, cut] = grad
            square = grad * grad + 1e-30
            block_sum = jnp.sum(square, axis=1, keepdims=True)
            row_sum = block_sum if row_sum is None else row_sum + block_sum
            column_sum = jnp.sum(square, axis=0, keepdims=True)
            for at in range(columns // LANES):
                to = line + block * columns // LANES + at
                sums_ref[to : to + 1] = column_sum[:, at * LANES : (at + 1) * LANES]
        row_stat = DECAY * turned_row(old_refs[part][...]) + (1.0 - DECAY) * (row_sum / (blocks * columns))
        row_refs[part][...] = turned_column(row_stat)
        inverse = 1.0 / row_stat
        for block in range(blocks):
            grad = grad_refs[part][:, block * columns : (block + 1) * columns]
            column_sum = jnp.sum(grad * grad * inverse, axis=0, keepdims=True)
            for at in range(columns // LANES):
                to = norms + line + block * columns // LANES + at
                sums_ref[to : to + 1] = column_sum[:, at * LANES : (at + 1) * LANES]
        line += blocks * columns // LANES
        total = jnp.sum(row_stat, axis=0, keepdims=True)
        sums_ref[totals + part : totals + part + 1] = jnp.broadcast_to(total, (1, LANES))
    if with_vectors:
        last = cuts[-1][0] + cuts[-1][1] * cuts[-1][2]
        moment = moment_refs[0][...]
        count, wide = moment.shape
        grad = sum_of(slice(last, last + 16), slice(0, LANES))[:count, :wide]
        second = DECAY * moment + (1.0 - DECAY) * (grad * grad + 1e-30)
        vector_refs[0][...] = grad
        vector_refs[1][...] = second
        move = grad * lax.rsqrt(second)
        norm = jnp.sum(move * move, axis=1, keepdims=True)
        sums_ref[vector_line:] = jnp.zeros((16, LANES), F32)
        sums_ref[vector_line : vector_line + count] = jnp.broadcast_to(norm, (count, LANES))


def finish(parts, olds, cuts, moment, here, behind=()):
    columns = parts[-1].shape[1]
    rows = parts[-1].shape[0]
    outs = [array((count, blocks * columns), F32) for first, count, blocks in cuts]
    outs += [array((1, count), F32) for first, count, blocks in cuts]
    vectors = () if moment is None else (moment,)
    outs += [array(value.shape, F32) for value in vectors for unused in range(2)]
    outs += [array((sums_at(cuts, columns)[2] + 16 * len(vectors), LANES), F32)]
    args, specs, scratch = list(parts), [VMEM] * len(parts), []
    if len(parts) > 1:
        args, specs = [here.table, *parts], [scalars(), HBM] + [VMEM] * (len(parts) - 1)
        scratch = [pltpu.VMEM((rows, columns), parts[0].dtype), pltpu.SemaphoreType.DMA((1,))]
    args += list(olds) + list(vectors)
    specs += [VMEM] * (len(olds) + len(vectors))
    return call(
        functools.partial(finish_kernel, len(parts), cuts, bool(vectors)),
        tuple(outs),
        tuple(args),
        specs,
        (VMEM,) * len(outs),
        scratch,
        8 * rows * columns,
        8 * rows * columns,
        behind,
        16,
    )


def update_kernel(cuts, columns, full_rows, with_vectors, *refs):
    parts = len(cuts)
    refs = list(refs)

    def take(count):
        taken = refs[:count]
        del refs[:count]
        return taken

    grad_refs, master_refs, row_refs, old_refs = take(parts), take(parts), take(parts), take(parts)
    vector_refs = take(3 * int(with_vectors))
    (sums_ref,) = take(1)
    updated_refs, column_refs = take(parts), take(parts)
    norms, totals, vector_line = sums_at(cuts, columns)
    line = 0
    for part, (first, rows, blocks) in enumerate(cuts):
        wide = blocks * columns
        lines = wide // LANES
        square = jnp.concatenate([sums_ref[line + at : line + at + 1] for at in range(lines)], axis=1)
        weighted = jnp.concatenate(
            [sums_ref[norms + line + at : norms + line + at + 1] for at in range(lines)], axis=1
        )
        line += lines
        row_mean = sums_ref[totals + part : totals + part + 1, 0:1] / full_rows[part]
        col_stat = DECAY * old_refs[part][...] + (1.0 - DECAY) * (square / full_rows[part])
        column_refs[part][...] = col_stat
        norm = row_mean * jnp.sum(weighted / col_stat, axis=1, keepdims=True)
        scale = jnp.sqrt(norm / (full_rows[part] * wide))
        left = lax.rsqrt(turned_row(row_refs[part][...]) / row_mean) * (RATE / jnp.maximum(1.0, scale))
        updated_refs[part][...] = master_refs[part][...] - grad_refs[part][...] * left * lax.rsqrt(col_stat)
    if with_vectors:
        grad_ref, second_ref, vectors_ref = vector_refs
        count = grad_ref.shape[0]
        norm = sums_ref[vector_line : vector_line + count, 0:1]
        scale = jnp.sqrt(norm / columns)
        move = grad_ref[...] * lax.rsqrt(second_ref[...])
        refs[0][...] = vectors_ref[...] - VECTOR_RATE * move / jnp.maximum(1.0, scale)


def update(grads, masters, rows, olds, vectors, sums, cuts, columns, size, behind=()):
    outs = [array(grad.shape, F32) for grad in grads]
    outs += [array((1, grad.shape[1]), F32) for grad in grads]
    outs += [array(value.shape, F32) for value in vectors[2:]]
    args = (*grads, *masters, *rows, *olds, *vectors, sums)
    full_rows = tuple(grad.shape[0] * size for grad in grads)
    return call(
        functools.partial(update_kernel, cuts, columns, full_rows, bool(vectors)),
        tuple(outs),
        args,
        [VMEM] * len(args),
        (VMEM,) * len(outs),
        [],
        32 * grads[0].size,
        16 * grads[0].size,
        behind,
        16,
    )


class Place:
    def __init__(self):
        self.size = lax.axis_size("dp")
        self.chips = self.size // 2
        self.ring = list(range(0, self.chips, 2)) + list(range(self.chips - 1, 0, -2))
        self.small = self.size == HEADS
        index = lax.axis_index("dp")
        self.chip = index // 2
        self.core = index % 2 if self.small else jnp.zeros_like(index)
        where = [0] * self.chips
        for place, chip in enumerate(self.ring):
            where[chip] = place
        tables = [
            [self.ring[(where[chip] + offset) % self.chips] for offset in range(self.chips)]
            for chip in range(self.chips)
        ]
        self.table = lax.dynamic_index_in_dim(
            jnp.array(tables, jnp.int32), self.chip, 0, keepdims=False
        )

    def permute(self, array, target):
        pairs = []
        for chip in range(self.chips):
            for core in range(2):
                to_chip, to_core = target(chip, core)
                pairs.append((chip * 2 + core, to_chip * 2 + to_core))
        return lax.ppermute(array, "dp", pairs)

    def shift(self, array, by):
        where = {chip: place for place, chip in enumerate(self.ring)}
        return self.permute(
            array, lambda chip, core: (self.ring[(where[chip] + by) % self.chips], core)
        )

    def swap(self, array):
        return self.permute(array, lambda chip, core: (chip, 1 - core))

    def cross(self, array, mask):
        return self.permute(array, lambda chip, core: (chip ^ mask, core))

    def masks(self):
        return [1 << bit for bit in range(self.chips.bit_length() - 1)]


def section_shift(array, by):
    size = lax.axis_size("section")
    pairs = [(i, i + by) for i in range(size) if 0 <= i + by < size]
    return lax.ppermute(array, "section", pairs)


def place_kernel(plan, chips_ref, *refs):
    out, sems = refs[-2:]
    pairs = []
    for piece, (place, row) in zip(refs, plan):
        pairs.append((piece, out.at[chips_ref[place], pl.ds(row, piece.shape[0])]))
    for copy in fetch(pairs, sems):
        copy.wait()


def upper_rows(rows):
    return (rows // 2 + 15) // 16 * 16


def cut_kernel(count, *refs):
    sources, outs, sems = refs[: 2 * count], refs[2 * count : 4 * count], refs[-1]
    pairs = []
    for index, (source, out) in enumerate(zip(sources, outs)):
        start = 0 if index < count else source.shape[0] - out.shape[0]
        pairs.append((source.at[pl.ds(start, out.shape[0])], out))
    for copy in fetch(pairs, sems):
        copy.wait()


class RingGather:
    def __init__(self, cuts, here):
        self.here = here
        self.streams = [[(0, 0, cut)] for cut in cuts]
        self.ahead, self.behind = list(cuts), list(cuts)
        for step in range(1, here.chips // 2):
            for index, pieces in enumerate(self.streams):
                self.ahead[index] = here.shift(self.ahead[index], 1)
                self.behind[index] = here.shift(self.behind[index], -1)
                pieces += [(-step, 0, self.ahead[index]), (step, 0, self.behind[index])]

    def heads(self):
        return (*self.ahead, *self.behind)

    def finish(self, behind=()):
        here = self.here
        count = len(self.streams)
        half = here.chips // 2
        outs, size = [], 0
        for index, source in enumerate(self.heads()):
            rows, columns = source.shape
            upper = upper_rows(rows)
            outs.append(array((upper if index < count else rows - upper, columns), source.dtype))
            size += 2 * outs[-1].size
        cuts = call(
            functools.partial(cut_kernel, count),
            tuple(outs),
            self.heads(),
            [HBM] * (2 * count),
            (VMEM,) * (2 * count),
            [pltpu.SemaphoreType.DMA((2 * count,))],
            0,
            2 * size,
            behind,
        )
        plan, arrays, base = [], [], 0
        for index, pieces in enumerate(self.streams):
            rows = pieces[0][2].shape[0]
            pieces.append((half, 0, here.shift(cuts[index], 1)))
            pieces.append((half, upper_rows(rows), here.shift(cuts[count + index], -1)))
            for offset, row, piece in pieces:
                plan.append((offset % here.chips, base + row))
                arrays.append(piece)
            base += rows
        columns = arrays[0].shape[1]
        return call(
            functools.partial(place_kernel, tuple(plan)),
            array((here.chips, base, columns), arrays[0].dtype),
            (here.table, *arrays),
            [scalars()] + [HBM] * len(arrays),
            VMEM,
            [pltpu.SemaphoreType.DMA((len(arrays),))],
            0,
            4 * here.chips * base * columns,
            limit=16,
        )


def place_kernel(plan, chips_ref, *refs):
    out, sems = refs[-2:]
    pairs = []
    for piece, (place, row) in zip(refs, plan):
        pairs.append((piece, out.at[chips_ref[place], pl.ds(row, piece.shape[0])]))
    for copy in fetch(pairs, sems):
        copy.wait()


def pack_kernel(project_ref, merge_ref, vectors_ref, upper_ref, lower_ref):
    rows, width = merge_ref.shape
    count, wide = vectors_ref.shape
    vectors = jnp.concatenate([vectors_ref[...], jnp.zeros((16 - count, wide), F32)], axis=0).astype(BF16)
    vectors = jnp.concatenate([vectors, jnp.zeros((16, width - wide), BF16)], axis=1)
    whole = [project_ref[:, third * width : (third + 1) * width].astype(BF16) for third in range(3)]
    whole = jnp.concatenate([*whole, merge_ref[...].astype(BF16), vectors], axis=0)
    cut = upper_ref.shape[0]
    upper_ref[...] = whole[:cut]
    lower_ref[...] = whole[cut:]


def pack_rows(project, merge, vectors):
    rows = 4 * merge.shape[0] + 16
    width = merge.shape[1]
    cut = upper_rows(rows)
    return call(
        pack_kernel,
        (array((cut, width), BF16), array((rows - cut, width), BF16)),
        (project, merge, vectors),
        [VMEM] * 3,
        (VMEM, VMEM),
        [],
        0,
        2 << 20,
    )


def halves_kernel(whole_ref, upper_ref, lower_ref):
    half = whole_ref.shape[0] // 2
    upper_ref[...] = whole_ref[:half].astype(BF16)
    lower_ref[...] = whole_ref[half:].astype(BF16)


def halves_of(whole, behind):
    half = array((whole.shape[0] // 2, whole.shape[1]), BF16)
    return call(halves_kernel, (half, half), (whole,), [VMEM], (VMEM, VMEM), [], 0, 2 << 20, behind)


def vectors_of(near, far, core, wide):
    cuts = [part[:, -16:, :wide] for part in (near, far)]
    rows = jnp.where(core == 0, jnp.stack(cuts), jnp.stack(cuts[::-1]))
    return rows.transpose(2, 1, 0, 3).reshape(16, -1).astype(F32)


def gather_plainly(project, merge, expand, shrink, vectors):
    width = merge.shape[1]

    def whole_of_rows(rows):
        whole = lax.all_gather(rows.astype(BF16), "dp", axis=0, tiled=True)
        return whole.reshape(PAIRS, 2, -1, whole.shape[1])

    parts = [whole_of_rows(project[:, at * width : (at + 1) * width]) for at in range(3)]
    cuts = [jnp.concatenate([*parts, whole_of_rows(merge)], axis=2)]
    cuts += [whole_of_rows(expand), whole_of_rows(shrink)]
    rows = lax.all_gather(vectors.astype(BF16), "dp", axis=1, tiled=True)
    rows = jnp.pad(rows, ((0, 16 - vectors.shape[0]), (0, 0)))
    return *((cut[:, 0], cut[:, 1]) for cut in cuts), rows.astype(F32)


def far_kernel(half, chips_ref, blocks, upper_ref, lower_ref, sems):
    cut = upper_ref.shape[0]
    chip = chips_ref[half]
    pairs = [
        (blocks.at[chip, pl.ds(0, cut)], upper_ref),
        (blocks.at[chip, pl.ds(cut, lower_ref.shape[0])], lower_ref),
    ]
    for copy in fetch(pairs, sems):
        copy.wait()


def add_kernel(ahead_at, behind_at, chips_ref, blocks, ahead_got, behind_got, ahead_out, behind_out, ahead_ref, behind_ref, sems):
    pairs = [
        (blocks.at[chips_ref[ahead_at]], ahead_out),
        (blocks.at[chips_ref[behind_at]], behind_out),
        (ahead_got, ahead_ref),
        (behind_got, behind_ref),
    ]
    for copy in fetch(pairs, sems):
        copy.wait()
    rows = behind_out.shape[0]
    for got, out, cut in (
        (ahead_ref, ahead_out, pl.ds(0, ahead_ref.shape[0])),
        (behind_ref, behind_out, pl.ds(rows - behind_ref.shape[0], behind_ref.shape[0])),
    ):
        out[cut] = (out[cut].astype(F32) + got[...].astype(F32)).astype(BF16)


class RingSum:
    def __init__(self, blocks, here):
        self.blocks = blocks
        self.here = here
        self.step = here.chips // 2
        self.sent = None

    def round(self, *behind):
        here, blocks, step = self.here, self.blocks, self.step
        rows, columns = blocks.shape[1:]
        if self.sent is None:
            cut = upper_rows(rows)
            payload = call(
                functools.partial(far_kernel, step),
                (array((cut, columns), BF16), array((rows - cut, columns), BF16)),
                (here.table, blocks),
                [scalars(), HBM],
                (VMEM, VMEM),
                [pltpu.SemaphoreType.DMA((2,))],
                0,
                4 * rows * columns,
                behind,
            )
        else:
            whole = array((rows, columns), BF16)
            payload = call(
                functools.partial(add_kernel, step, here.chips - step),
                (whole, whole),
                (here.table, blocks, *self.sent),
                [scalars(), HBM, HBM, HBM],
                (VMEM, VMEM),
                [pltpu.VMEM(part.shape, BF16) for part in self.sent] + [pltpu.SemaphoreType.DMA((4,))],
                2 * rows * columns,
                12 * rows * columns,
                behind,
            )
        self.step -= 1
        self.sent = (here.shift(payload[0], 1), here.shift(payload[1], -1))
        return payload[0]

    def parts(self):
        return (self.blocks, *self.sent)


def small_sum(vector, here):
    if not here.small:
        return lax.psum(vector, "dp")
    vector = vector + here.swap(vector)
    for mask in here.masks():
        vector = vector + here.cross(vector, mask)
    return vector


def segments(lengths_row, count):
    ends = jnp.cumsum(lengths_row)
    places = jnp.arange(count, dtype=jnp.int32)
    return jnp.sum((places[:, None] >= ends[None, :]).astype(jnp.int32), axis=1)


def per_device(
    frames,
    lengths,
    cotangent,
    project_weight,
    merge_weight,
    expand_weight,
    shrink_weight,
    vectors,
    project_row,
    project_col,
    merge_row,
    merge_col,
    expand_row,
    expand_col,
    shrink_row,
    shrink_col,
    vector_moment,
):
    here = Place()
    core = here.core.reshape(1)
    is_first = lax.axis_index("section") == 0
    micro = lengths.shape[0]
    count, width = frames.shape
    block = count // micro
    segment = jax.vmap(lambda lengths_row: segments(lengths_row, block))(lengths)
    live = (segment < UTTS).astype(F32).reshape(count, 1)
    visible = (segment[:, :, None] == segment[:, None, :]).astype(F32)

    masters = (project_weight[0], merge_weight[0], expand_weight[0], shrink_weight[0])
    first = is_first.astype(jnp.int32).reshape(1)
    if here.small:
        pm_ring = RingGather(pack_rows(masters[0], masters[1], vectors[0]), here)
        e_cuts = halves_of(masters[2], pm_ring.heads())
        near = pm_ring.finish()
        e_ring = RingGather(e_cuts, here)
        pm = (near, here.swap(near))
        vec = vectors_of(*pm, here.core, vectors.shape[2])
        kept = attend_block(core, frames, visible, vec, pm)
        s_cuts = halves_of(masters[3], (*e_ring.heads(), kept[-1]))
        near = e_ring.finish()
        s_ring = RingGather(s_cuts, here)
        e = (near, here.swap(near))
        hidden, slope = expand_block(core, kept[-1], vec, e)
        near = s_ring.finish((hidden,))
        s = (near, here.swap(near))
    else:
        pm, e, s, vec = gather_plainly(*masters, vectors[0])
        kept = attend_block(core, frames, visible, vec, pm)
        hidden, slope = expand_block(core, kept[-1], vec, e)

    unused, low = shrink_block(core, kept[3], hidden, vec, s)
    start = jnp.where(is_first, frames, section_shift(low, 1))
    kept = attend_block(core, start, visible, vec, pm)
    normed, packed, mixed, middle, normed_two = kept
    hidden, slope = expand_block(core, normed_two, vec, e)

    incoming, unused = incoming_grad(jnp.zeros((1,), jnp.int32), frames, cotangent, live, ())
    unused, unused, back_middle, back_branch, sums_two, sums_up = back_hidden_block(
        core, incoming, middle, vec, s, e, slope, ()
    )
    unused, unused, low, unused = back_attend_block(
        core, first, start, back_middle, back_branch, packed, visible, vec, sums_two, sums_up, pm, ()
    )
    output, unused = shrink_block(core, middle, hidden, vec, s, (low,))
    incoming, low_incoming = incoming_grad(first, section_shift(low, -1), cotangent, live, (output,))
    swap = here.swap if here.small else lambda rows: rows

    shared = [swap(rows) for rows in (hidden, normed_two, normed, mixed)]
    behind = ()
    if here.small:
        shrink_ring = RingSum(
            shrink_grad(core, hidden, shared[0], low_incoming, swap(low_incoming), shared[1:]), here
        )
        behind = (shrink_ring.round(),)
    low_out, back_pre, back_middle, back_branch, sums_two, sums_up = back_hidden_block(
        core, incoming, middle, vec, s, e, slope, behind
    )
    if here.small:
        behind = (shrink_ring.round(back_branch),)
    back_packed, back_inputs, low, vector_sums = back_attend_block(
        core, first, start, back_middle, back_branch, packed, visible, vec, sums_two, sums_up, pm, behind
    )
    layer_outputs = output[None]
    input_grads = back_inputs[None]

    rows = masters[0].shape[0]
    shrink_cuts = ((0, masters[3].shape[0], 1),)
    expand_cuts = ((0, rows, 1),)
    both_cuts = ((0, rows, 3), (3 * rows, rows, 1))
    shrink_olds, expand_olds = (shrink_row,), (expand_row,)
    both_olds = (project_row, merge_row)
    moment = vector_moment[0]
    if here.small:
        last = shrink_ring.round(low)
        expand_ring = RingSum(
            expand_grad(core, normed_two, shared[1], back_pre, swap(back_pre), (last,)), here
        )
        last = expand_ring.round()
        last = shrink_ring.round(last)
        both_ring = RingSum(
            project_grad(
                core,
                (
                    normed,
                    shared[2],
                    back_packed,
                    swap(back_packed),
                    mixed,
                    shared[3],
                    back_branch,
                    swap(back_branch),
                    vector_sums,
                    swap(vector_sums),
                ),
                (last,),
            ),
            here,
        )
        last = both_ring.round()
        last = expand_ring.round(last)
        shrink_ends = finish(shrink_ring.parts(), shrink_olds, shrink_cuts, None, here, (last,))
        last = both_ring.round(shrink_ends[0])
        last = expand_ring.round(last)
        last = both_ring.round(last)
        last = expand_ring.round(last)
        last = both_ring.round(last)
        expand_ends = finish(expand_ring.parts(), expand_olds, expand_cuts, None, here, (last,))
        both_parts = both_ring.parts()
    else:

        def total(left, right):
            whole = dot_first(left, right).astype(BF16)
            return lax.psum_scatter(whole, "dp", scatter_dimension=0, tiled=True).astype(F32)

        shrink_ends = finish((total(hidden, low_out),), shrink_olds, shrink_cuts, None, here)
        expand_ends = finish((total(normed_two, back_pre),), expand_olds, expand_cuts, None, here)
        thirds = [total(normed, back_packed[:, at * width : (at + 1) * width]) for at in range(3)]
        vector_rows = lax.psum_scatter(vector_sums, "dp", scatter_dimension=1, tiled=True)
        vector_rows = jnp.pad(vector_rows, ((0, 0), (0, width - vector_rows.shape[1])))
        both_parts = (jnp.concatenate([*thirds, total(mixed, back_branch), vector_rows], axis=0),)
        last = vector_sums

    both_ends = finish(both_parts, both_olds, both_cuts, moment, here)
    ends = (shrink_ends, expand_ends, both_ends)
    sums = small_sum(jnp.concatenate([end[-1] for end in ends], axis=0), here)

    def updated(end, cuts, matrices, cols_old, columns, values):
        nonlocal sums
        count = len(cuts)
        lines = end[-1].shape[0]
        own, sums = sums[:lines], sums[lines:]
        grads, rows_new, vector_parts = end[:count], end[count : 2 * count], end[2 * count : -1]
        results = update(
            grads, matrices, rows_new, cols_old, (*vector_parts, *values), own, cuts, columns, here.size
        )
        outs = []
        for part in range(count):
            outs += [grads[part][None], rows_new[part], results[count + part], results[part][None]]
        return outs, (*vector_parts, *results[2 * count :])

    shrink_outs, unused = updated(shrink_ends, shrink_cuts, masters[3:], (shrink_col,), width, ())
    expand_outs, unused = updated(
        expand_ends, expand_cuts, masters[2:3], (expand_col,), 4 * width, ()
    )
    both_outs, vector_outs = updated(
        both_ends, both_cuts, masters[:2], (project_col, merge_col), width, (vectors[0],)
    )
    return (
        layer_outputs,
        input_grads,
        *both_outs,
        *expand_outs,
        *shrink_outs,
        *(rows[None] for rows in vector_outs),
    )


def solution(mesh):
    placed = (
        P("dp", None),
        P("dp", None),
        P("dp", None),
        P("section", "dp", None),
        P("section", "dp", None),
        P("section", "dp", None),
        P("section", "dp", None),
        P("section", None, "dp"),
        P("section", "dp"),
        P("section", None),
        P("section", "dp"),
        P("section", None),
        P("section", "dp"),
        P("section", None),
        P("section", "dp"),
        P("section", None),
        P("section", None, "dp"),
    )
    matrix = (
        P("section", "dp", None),
        P("section", "dp"),
        P("section", None),
        P("section", "dp", None),
    )
    return jax.shard_map(
        per_device,
        mesh=mesh,
        in_specs=placed,
        out_specs=(
            P("section", "dp", None),
            P("section", "dp", None),
            *matrix,
            *matrix,
            *matrix,
            *matrix,
            P("section", None, "dp"),
            P("section", None, "dp"),
            P("section", None, "dp"),
        ),
        check_vma=False,
    )
```

```python
import functools
import math

import jax
import jax.numpy as jnp
from jax import lax
from jax.experimental import pallas as pl
from jax.experimental.pallas import tpu as pltpu
from jax.sharding import PartitionSpec as P

HEADS = 16
HEAD_DIM = 64
PAIRS = HEADS // 2
UTTS = 3
STEP = 10

EPSILON = 1e-05
RATE = 0.04
VECTOR_RATE = 0.25
MASKED = -1e30
BF16 = jnp.bfloat16
F32 = jnp.float32
VMEM = pl.BlockSpec(memory_space=pltpu.VMEM)
HBM = pl.BlockSpec(memory_space=pl.ANY)
MIB = 1024 * 1024


def dot(left, right):
    return lax.dot_general(left, right, (((1,), (0,)), ((), ())), preferred_element_type=F32)


def dot_last(left, right):
    return lax.dot_general(left, right, (((1,), (1,)), ((), ())), preferred_element_type=F32)


def dot_first(left, right):
    return lax.dot_general(left, right, (((0,), (0,)), ((), ())), preferred_element_type=F32)


def moments(values):
    centred = values - jnp.mean(values, axis=-1, keepdims=True)
    spread = jnp.mean(centred * centred, axis=-1, keepdims=True)
    scale = lax.rsqrt(spread + EPSILON)
    return centred * scale, scale


def norm_back(grad, unit, scale, gain):
    inner = grad * gain
    first = jnp.mean(inner, axis=-1, keepdims=True)
    second = jnp.mean(inner * unit, axis=-1, keepdims=True)
    return scale * (inner - first - unit * second)


def fetch(pairs, sems):
    copies = [
        pltpu.make_async_copy(source, target, sems.at[index])
        for index, (source, target) in enumerate(pairs)
    ]
    for copy in copies:
        copy.start()
    return copies


def half_masks():
    lane = lax.broadcasted_iota(jnp.int32, (1, 128), 1)
    low = jnp.where(lane < HEAD_DIM, 1.0, 0.0)
    return low.astype(BF16), (1.0 - low).astype(BF16)


def two_heads(tile, masks):
    return jnp.concatenate([tile * masks[0], tile * masks[1]], axis=0)


def side_by_side(both):
    half = both.shape[0] // 2
    return jnp.concatenate([both[:half], both[half:]], axis=1)


def weights_of(both_queries, keys, visible):
    scores = jnp.where(visible, dot_last(both_queries, keys) * HEAD_DIM**-0.5, MASKED)
    shifted = jnp.exp(scores - jnp.max(scores, axis=-1, keepdims=True))
    return shifted / jnp.sum(shifted, axis=-1, keepdims=True)


def scalars():
    return pl.BlockSpec(memory_space=pltpu.SMEM)


def array(shape, kind):
    return jax.ShapeDtypeStruct(shape, kind)


def call(kernel, outs, args, in_specs, out_specs, scratch, flops, size, behind=(), limit=12, passing=()):
    given, skipped = len(args), len(behind) + len(passing)
    single = not isinstance(outs, tuple)
    results = (outs,) if single else outs
    result_specs = (out_specs,) if single else out_specs
    count = len(results)

    def body(*refs):
        kernel(*refs[:given], *refs[given + skipped :][:count], *refs[given + skipped + count + len(passing) :])

    returned = pl.pallas_call(
        body,
        out_shape=(*results, *(array(value.shape, value.dtype) for value in passing)),
        in_specs=[
            *in_specs,
            *(HBM for unused in range(skipped)),
        ],
        out_specs=(*result_specs, *(HBM for unused in passing)),
        scratch_shapes=scratch,
        input_output_aliases={given + len(behind) + at: count + at for at in range(len(passing))},
        compiler_params=pltpu.CompilerParams(vmem_limit_bytes=limit * MIB),
        cost_estimate=pl.CostEstimate(flops=flops, bytes_accessed=size, transcendentals=0),
    )(*args, *behind, *passing)
    own = returned[0] if single else tuple(returned[:count])
    return (own, tuple(returned[count:])) if passing else own


def both_cores(core, near, far, whole, cuts):
    pairs = []
    for cut in cuts:
        pairs.append((near.at[cut], whole.at[cut[0], core, *cut[1:]]))
        pairs.append((far.at[cut], whole.at[cut[0], 1 - core, *cut[1:]]))
    return pairs


ALL = slice(None)


def quarters_of(core, near, far, whole, order):
    rows = whole.shape[3]
    pairs = []
    for at in order:
        pairs.append((near.at[:, pl.ds(at * rows, rows)], whole.at[at, :, core]))
        pairs.append((far.at[:, pl.ds(at * rows, rows)], whole.at[at, :, 1 - core]))
    return pairs


def quarters_scratch(width):
    return pltpu.VMEM((4, PAIRS, 2, width // HEADS, width), BF16)


def columns_cut(start, size):
    return (ALL, ALL, pl.ds(start, size))


def attend_kernel(core_ref, x_ref, mask_ref, vec_ref, near, far, a_ref, packed_ref, o_ref, x1_ref, c_ref, w, sems):
    count, width = x_ref.shape
    block = mask_ref.shape[1]
    step = 512
    copies = fetch(quarters_of(core_ref[0], near, far, w, range(4)), sems)
    unit, unused = moments(x_ref[...].astype(F32))
    a_ref[...] = (unit * vec_ref[0:1] + vec_ref[1:2]).astype(BF16)
    for third in range(3):
        copies[2 * third].wait()
        copies[2 * third + 1].wait()
        for cut in range(width // step):
            at = third * width + cut * step
            matrix = w[third, :, :, :, cut * step : (cut + 1) * step].reshape(width, step)
            result = dot(a_ref[...], matrix)
            if third != 1:
                row = 2 if third == 0 else 3
                result = result + vec_ref[row : row + 1, cut * step : (cut + 1) * step]
            packed_ref[:, at : at + step] = result.astype(BF16)
    masks = half_masks()
    for micro in range(count // block):
        rows = slice(micro * block, (micro + 1) * block)
        visible = mask_ref[micro] > 0.0
        visible = jnp.concatenate([visible, visible], axis=0)
        for at in range(0, width, 128):
            queries = packed_ref[rows, at : at + 128]
            keys = packed_ref[rows, at + width : at + width + 128]
            values = packed_ref[rows, at + 2 * width : at + 2 * width + 128]
            attend = weights_of(two_heads(queries, masks), keys, visible).astype(BF16)
            mixed = dot(side_by_side(attend), two_heads(values, masks))
            o_ref[rows, at : at + 128] = mixed.astype(BF16)
    copies[6].wait()
    copies[7].wait()
    for at in range(0, width, step):
        cut = slice(at, at + step)
        matrix = w[3, :, :, :, cut].reshape(width, step)
        x1_ref[:, cut] = x_ref[:, cut].astype(F32) + (dot(o_ref[...], matrix) + vec_ref[4:5, cut])
    unit, unused = moments(x1_ref[...])
    c_ref[...] = (unit * vec_ref[5:6] + vec_ref[6:7]).astype(BF16)


def whole_of(near):
    chips, rows, columns = near.shape
    return pltpu.VMEM((chips, 2, rows, columns), near.dtype)


def attend_block(core, x, mask, vec, pm, behind=()):
    count, width = x.shape
    low = array((count, width), BF16)
    return call(
        attend_kernel,
        (low, array((count, 3 * width), BF16), low, array((count, width), F32), low),
        (core, x, mask, vec, *pm),
        [scalars()] + [VMEM] * 3 + [HBM] * 2,
        (VMEM,) * 5,
        [quarters_scratch(width), pltpu.SemaphoreType.DMA((8,))],
        8 * count * width * width,
        20 << 20,
        behind=behind,
        limit=32,
    )


def gelu_parts(values):
    cdf = 0.5 * (1.0 + lax.erf(values * math.sqrt(0.5)))
    slope = cdf + values * jnp.exp(-0.5 * values * values) * (1.0 / math.sqrt(2.0 * math.pi))
    return values * cdf, slope


def expand_kernel(core_ref, c_ref, vec_ref, near, far, hidden_ref, slope_hbm, w, slope, sems, out_sems):
    count, width = c_ref.shape
    step = 256
    quarters = w.shape[3] // width
    copies = fetch(
        both_cores(core_ref[0], near, far, w, [columns_cut(at * width, width) for at in range(quarters)]), sems
    )
    sent = []
    for quarter in range(quarters):
        copies[2 * quarter].wait()
        copies[2 * quarter + 1].wait()
        for cut in range(width // step):
            at = quarter * width + cut * step
            result = dot(c_ref[...], w[:, :, :, at : at + step].reshape(width, step))
            bias = vec_ref[8 + quarter : 9 + quarter, cut * step : (cut + 1) * step]
            hidden, rise = gelu_parts(result + bias)
            hidden_ref[:, at : at + step] = hidden.astype(BF16)
            slope[:, at : at + step] = rise
        at = slice(quarter * width, (quarter + 1) * width)
        copy = pltpu.make_async_copy(slope.at[:, at], slope_hbm.at[:, at], out_sems.at[quarter])
        copy.start()
        sent.append(copy)
    for copy in sent:
        copy.wait()


def expand_block(core, c, vec, e):
    count, width = c.shape
    hidden = 4 * width
    return call(
        expand_kernel,
        (array((count, hidden), BF16), array((count, hidden), F32)),
        (core, c, vec, *e),
        [scalars()] + [VMEM] * 2 + [HBM] * 2,
        (VMEM, HBM),
        [
            whole_of(e[0]),
            pltpu.VMEM((count, hidden), F32),
            pltpu.SemaphoreType.DMA((8,)),
            pltpu.SemaphoreType.DMA((4,)),
        ],
        2 * count * width * hidden,
        20 << 20,
        limit=32,
    )


def shrink_kernel(core_ref, x1_ref, hidden_ref, vec_ref, near, far, y_ref, low_ref, w, sems):
    chips, unused, rows, width = w.shape
    step = 512
    group = width // (2 * rows)
    copies = fetch(
        both_cores(core_ref[0], near, far, w, [(pl.ds(at, group),) for at in range(0, chips, group)]), sems
    )
    for index in range(chips // group):
        copies[2 * index].wait()
        copies[2 * index + 1].wait()
        left = hidden_ref[:, index * width : (index + 1) * width]
        for at in range(0, width, step):
            cut = slice(at, at + step)
            matrix = w[index * group : (index + 1) * group, :, :, cut].reshape(width, step)
            result = dot(left, matrix)
            if index == 0:
                y_ref[:, cut] = x1_ref[:, cut] + result
            elif index < chips // group - 1:
                y_ref[:, cut] += result
            else:
                total = y_ref[:, cut] + result + vec_ref[7:8, cut]
                y_ref[:, cut] = total
                low_ref[:, cut] = total.astype(BF16)


def shrink_block(core, x1, hidden, vec, s, behind=()):
    count, width = x1.shape
    return call(
        shrink_kernel,
        (array((count, width), F32), array((count, width), BF16)),
        (core, x1, hidden, vec, *s),
        [scalars()] + [VMEM] * 3 + [HBM] * 2,
        (VMEM, VMEM),
        [whole_of(s[0]), pltpu.SemaphoreType.DMA((8,))],
        8 * count * width * width,
        16 << 20,
        behind=behind,
        limit=28,
    )


def back_hidden_kernel(core_ref, dy_ref, x1_ref, vec_ref, s_near, s_far, e_near, e_far, slope_hbm, gf_ref, gu_ref, dx1_ref, gat_ref, sums_ref, bias_ref, ws, we, slope, dc, sems, slope_sems):
    chips, unused, rows, width = ws.shape
    group = width // (2 * rows)
    quarters = chips // group
    core = core_ref[0]
    pairs = []
    for index in range(quarters):
        at = pl.ds(index * width, width)
        pairs += both_cores(core, s_near, s_far, ws, [(pl.ds(index * group, group),)])
        pairs.append((slope_hbm.at[:, at], slope.at[:, at]))
        pairs += both_cores(core, e_near, e_far, we, [columns_cut(index * width, width)])
    copies = fetch(pairs, sems)
    gf_ref[...] = dy_ref[...].astype(BF16)
    step = 512
    for index in range(quarters):
        for copy in copies[5 * index : 5 * index + 3]:
            copy.wait()
        for near in range(group):
            matrix = ws[index * group + near].reshape(2 * rows, width)
            at = slice(index * width + near * 2 * rows, index * width + (near + 1) * 2 * rows)
            back = (dot_last(gf_ref[...], matrix) * slope[:, at]).astype(BF16)
            gu_ref[:, at] = back
            bias_ref[:, at] = jnp.sum(back.astype(F32), axis=0, keepdims=True)
        for copy in copies[5 * index + 3 : 5 * index + 5]:
            copy.wait()
        at = slice(index * width, (index + 1) * width)
        left = gu_ref[:, at]
        for half in range(2):
            matrix = we[half * (chips // 2) : (half + 1) * (chips // 2), :, :, at].reshape(step, width)
            to = slice(half * step, (half + 1) * step)
            result = dot_last(left, matrix)
            if index == 0:
                dc[:, to] = result
            else:
                dc[:, to] += result
    unit, scale = moments(x1_ref[...])
    grad = dc[...]
    back = dy_ref[...] + norm_back(grad, unit, scale, vec_ref[5:6])
    dx1_ref[...] = back
    gat_ref[...] = back.astype(BF16)
    sums_ref[...] = jnp.zeros_like(sums_ref)
    sums_ref[0:1] = jnp.sum(grad * unit, axis=0, keepdims=True)
    sums_ref[1:2] = jnp.sum(grad, axis=0, keepdims=True)
    sums_ref[2:3] = jnp.sum(gf_ref[...].astype(F32), axis=0, keepdims=True)
    sums_ref[3:4] = jnp.sum(gat_ref[...].astype(F32), axis=0, keepdims=True)


def back_hidden_block(core, dy, x1, vec, s, e, slope, behind):
    count, width = x1.shape
    hidden = slope.shape[1]
    return call(
        back_hidden_kernel,
        (
            array((count, width), BF16),
            array((count, hidden), BF16),
            array((count, width), F32),
            array((count, width), BF16),
            array((8, width), F32),
            array((1, hidden), F32),
        ),
        (core, dy, x1, vec, *s, *e, slope),
        [scalars()] + [VMEM] * 3 + [HBM] * 5,
        (VMEM,) * 6,
        [
            whole_of(s[0]),
            whole_of(e[0]),
            pltpu.VMEM((count, hidden), F32),
            pltpu.VMEM((count, width), F32),
            pltpu.SemaphoreType.DMA((20,)),
            pltpu.SemaphoreType.DMA((4,)),
        ],
        16 * count * width * width,
        32 << 20,
        behind,
        limit=48,
    )


def back_attend_kernel(core_ref, first_ref, x_ref, dx1_ref, gat_ref, packed_ref, mask_ref, vec_ref, two_ref, up_ref, near, far, gqkv_ref, dx_ref, low_ref, sums_ref, w, go, sems):
    count, width = x_ref.shape
    block = mask_ref.shape[1]
    step = 512
    copies = fetch(quarters_of(core_ref[0], near, far, w, (3, 0, 1, 2)), sems)
    masks = half_masks()
    factor = HEAD_DIM**-0.5
    copies[0].wait()
    copies[1].wait()
    chips = w.shape[1]
    for half in range(2):
        matrix = w[3, half * (chips // 2) : (half + 1) * (chips // 2)].reshape(step, width)
        go[:, half * step : (half + 1) * step] = dot_last(gat_ref[...], matrix).astype(BF16)
    for micro in range(count // block):
        rows = slice(micro * block, (micro + 1) * block)
        visible = mask_ref[micro] > 0.0
        visible = jnp.concatenate([visible, visible], axis=0)
        for at in range(0, width, 128):
            queries = two_heads(packed_ref[rows, at : at + 128], masks)
            keys = packed_ref[rows, at + width : at + width + 128]
            values = packed_ref[rows, at + 2 * width : at + 2 * width + 128]
            back = two_heads(go[rows, at : at + 128], masks)
            attend = weights_of(queries, keys, visible)
            slope = dot_last(back, values)
            inner = jnp.sum(attend * slope, axis=-1, keepdims=True)
            scores = (attend * (slope - inner)).astype(BF16)
            grad_q = dot(side_by_side(scores), two_heads(keys, masks)) * factor
            grad_k = dot_first(scores, queries) * factor
            grad_v = dot_first(attend.astype(BF16), back)
            gqkv_ref[rows, at : at + 128] = grad_q.astype(BF16)
            gqkv_ref[rows, at + width : at + width + 128] = grad_k.astype(BF16)
            gqkv_ref[rows, at + 2 * width : at + 2 * width + 128] = grad_v.astype(BF16)
    for copy in copies[2:]:
        copy.wait()
    for half in range(2):
        total = None
        for third in range(3):
            matrix = w[third, half * (chips // 2) : (half + 1) * (chips // 2)].reshape(step, width)
            result = dot_last(gqkv_ref[:, third * width : (third + 1) * width], matrix)
            total = result if total is None else total + result
        dx_ref[:, half * step : (half + 1) * step] = total
    unit, scale = moments(x_ref[...].astype(F32))
    grad = dx_ref[...]
    sums_ref[...] = jnp.zeros_like(sums_ref)
    sums_ref[0:1] = jnp.sum(grad * unit, axis=0, keepdims=True)
    sums_ref[1:2] = jnp.sum(grad, axis=0, keepdims=True)
    back = dx1_ref[...] + norm_back(grad, unit, scale, vec_ref[0:1])
    low = back.astype(BF16)
    low_ref[...] = low
    dx_ref[...] = jnp.where(first_ref[0] == 1, back, low.astype(F32))
    for row, third in ((2, 0), (3, 2)):
        part = gqkv_ref[:, third * width : (third + 1) * width]
        sums_ref[row : row + 1] = jnp.sum(part.astype(F32), axis=0, keepdims=True)
    sums_ref[4:5] = two_ref[3:4]
    sums_ref[5:8] = two_ref[0:3]
    for quarter in range(4):
        sums_ref[8 + quarter : 9 + quarter] = up_ref[:, quarter * width : (quarter + 1) * width]


def back_attend_block(core, first, x, dx1, gat, packed, mask, vec, two, up, pm, behind):
    count, width = x.shape
    return call(
        back_attend_kernel,
        (
            array((count, 3 * width), BF16),
            array((count, width), F32),
            array((count, width), BF16),
            array((16, width), F32),
        ),
        (core, first, x, dx1, gat, packed, mask, vec, two, up, *pm),
        [scalars()] * 2 + [VMEM] * 8 + [HBM] * 2,
        (VMEM,) * 4,
        [quarters_scratch(width), pltpu.VMEM((count, width), BF16), pltpu.SemaphoreType.DMA((8,))],
        12 * count * width * width,
        20 << 20,
        behind,
        limit=32,
    )


def incoming_kernel(first_ref, mail_ref, cotangent_ref, live_ref, out_ref, low_ref):
    targets = cotangent_ref[...].astype(F32) * live_ref[...]
    mail = mail_ref[...].astype(F32)
    out = jnp.where(first_ref[0] == 1, mail, targets)
    out_ref[...] = out
    low_ref[...] = out.astype(BF16)


def incoming_grad(first, mail, cotangent, live, behind):
    shape = cotangent.shape
    return call(
        incoming_kernel,
        (array(shape, F32), array(shape, BF16)),
        (first, mail, cotangent, live),
        [scalars()] + [VMEM] * 3,
        (VMEM, VMEM),
        [],
        0,
        10 * cotangent.size,
        behind,
    )


def shrink_grad_kernel(core_ref, near_ref, far_ref, right_ref, other_ref, out_ref):
    chips, rows, width = out_ref.shape
    for chip in range(chips):
        at = pl.ds(pl.multiple_of((2 * chip + core_ref[0]) * rows, rows), rows)
        total = dot_first(near_ref[:, at], right_ref[...]) + dot_first(far_ref[:, at], other_ref[...])
        out_ref[chip] = total.astype(BF16)


def shrink_grad(core, near, far, right, other, behind):
    tokens, hidden = near.shape
    width = right.shape[1]
    return call(
        shrink_grad_kernel,
        array((PAIRS, hidden // HEADS, width), BF16),
        (core, near, far, right, other),
        [scalars()] + [VMEM] * 4,
        VMEM,
        [],
        2 * tokens * width * hidden,
        12 << 20,
        behind,
        limit=24,
    )


def own_rows(core, near_ref, far_ref, turned):
    chips, unused, rows, both = turned.shape
    tokens = near_ref.shape[0]
    turned[:, :, :, :tokens] = near_ref[...].T.reshape(chips, 2, rows, tokens)
    turned[:, :, :, tokens:] = far_ref[...].T.reshape(chips, 2, rows, tokens)
    return turned[:, pl.ds(core, 1)].reshape(chips * rows, both)


def own_columns_grad(left, right_ref, other_ref, cut):
    right = jnp.concatenate([right_ref[:, cut], other_ref[:, cut]], axis=0)
    return dot(left, right).astype(BF16)


def expand_grad_kernel(core_ref, near_ref, far_ref, right_ref, other_ref, out_ref, turned):
    chips, rows, columns = out_ref.shape
    left = own_rows(core_ref[0], near_ref, far_ref, turned)
    step = 512
    for at in range(0, columns, step):
        cut = slice(at, at + step)
        out_ref[:, :, cut] = own_columns_grad(left, right_ref, other_ref, cut).reshape(chips, rows, step)


def turned_scratch(tokens, width):
    return pltpu.VMEM((PAIRS, 2, width // HEADS, 2 * tokens), BF16)


def expand_grad(core, near, far, right, other, behind):
    tokens, width = near.shape
    hidden = right.shape[1]
    return call(
        expand_grad_kernel,
        array((PAIRS, width // HEADS, hidden), BF16),
        (core, near, far, right, other),
        [scalars()] + [VMEM] * 4,
        VMEM,
        [turned_scratch(tokens, width)],
        2 * tokens * width * hidden,
        12 << 20,
        behind=behind,
        limit=24,
    )


def project_grad_kernel(core_ref, a_ref, a_far, packed_ref, packed_far, o_ref, o_far, gat_ref, gat_far, vec_ref, vec_far, out_ref, turned):
    chips, unused, width = out_ref.shape
    rows = width // HEADS
    core = core_ref[0]
    step = 512
    left = own_rows(core, a_ref, a_far, turned)
    for third in range(3):
        for at in range(0, width, step):
            result = own_columns_grad(left, packed_ref, packed_far, slice(third * width + at, third * width + at + step))
            out_ref[:, third * rows : (third + 1) * rows, at : at + step] = result.reshape(chips, rows, step)
    left = own_rows(core, o_ref, o_far, turned)
    for at in range(0, width, step):
        result = own_columns_grad(left, gat_ref, gat_far, slice(at, at + step))
        out_ref[:, 3 * rows : 4 * rows, at : at + step] = result.reshape(chips, rows, step)
    total = vec_ref[...] + vec_far[...]
    for chip in range(chips):
        pair = total[:, chip * 2 * rows : (chip + 1) * 2 * rows]
        turn = jnp.concatenate([pair[:, rows:], pair[:, :rows]], axis=1)
        own = jnp.where(core == 0, pair, turn)
        out_ref[chip, 4 * rows :, : 2 * rows] = own.astype(BF16)
        out_ref[chip, 4 * rows :, 2 * rows :] = jnp.zeros((own.shape[0], width - 2 * rows), BF16)


def project_grad(core, operands, behind):
    tokens, width = operands[0].shape
    rows = width // HEADS
    return call(
        project_grad_kernel,
        array((PAIRS, 4 * rows + 16, width), BF16),
        (core, *operands),
        [scalars()] + [VMEM] * len(operands),
        VMEM,
        [turned_scratch(tokens, width)],
        8 * tokens * width * width,
        12 << 20,
        behind=behind,
        limit=24,
    )


DECAY = 1.0 - STEP ** (-0.8)
LANES = 128


def sums_at(cuts, columns):
    lines = sum(blocks for first, rows, blocks in cuts) * columns // LANES
    return lines, 2 * lines, 2 * lines + 8


def turned_row(row):
    return jnp.sum(jnp.where(diagonal(row.shape[1]), row, 0.0), axis=1, keepdims=True)


def turned_column(column):
    return jnp.sum(jnp.where(diagonal(column.shape[0]), column, 0.0), axis=0, keepdims=True)


def diagonal(count):
    rows = lax.broadcasted_iota(jnp.int32, (count, count), 0)
    return rows == lax.broadcasted_iota(jnp.int32, (count, count), 1)


def finish_kernel(addends, cuts, with_vectors, *refs):
    parts = len(cuts)
    refs = list(refs)

    def take(count):
        taken = refs[:count]
        del refs[:count]
        return taken

    if addends > 1:
        (chips_ref, blocks), addend_refs = take(2), take(addends - 1)
    else:
        addend_refs = take(1)
    old_refs = take(parts)
    moment_refs = take(int(with_vectors))
    grad_refs, row_refs = take(parts), take(parts)
    vector_refs = take(2 * int(with_vectors))
    (sums_ref,) = take(1)
    if addends > 1:
        own, sems = refs
        for copy in fetch([(blocks.at[chips_ref[0]], own)], sems):
            copy.wait()
        addend_refs.append(own)
    columns = addend_refs[0].shape[1]
    norms, totals, vector_line = sums_at(cuts, columns)

    def sum_of(rows, cut):
        total = None
        for ref in addend_refs:
            value = ref[rows, cut].astype(F32)
            total = value if total is None else total + value
        return total

    sums_ref[totals : totals + 8] = jnp.zeros((8, LANES), F32)
    line = 0
    for part, (first, rows, blocks) in enumerate(cuts):
        row_sum = None
        for block in range(blocks):
            grad = sum_of(slice(first + block * rows, first + (block + 1) * rows), ALL)
            cut = slice(block * columns, (block + 1) * columns)
            grad_refs[part][:, cut] = grad
            square = grad * grad + 1e-30
            block_sum = jnp.sum(square, axis=1, keepdims=True)
            row_sum = block_sum if row_sum is None else row_sum + block_sum
            column_sum = jnp.sum(square, axis=0, keepdims=True)
            for at in range(columns // LANES):
                to = line + block * columns // LANES + at
                sums_ref[to : to + 1] = column_sum[:, at * LANES : (at + 1) * LANES]
        row_stat = DECAY * turned_row(old_refs[part][...]) + (1.0 - DECAY) * (row_sum / (blocks * columns))
        row_refs[part][...] = turned_column(row_stat)
        inverse = 1.0 / row_stat
        for block in range(blocks):
            grad = grad_refs[part][:, block * columns : (block + 1) * columns]
            column_sum = jnp.sum(grad * grad * inverse, axis=0, keepdims=True)
            for at in range(columns // LANES):
                to = norms + line + block * columns // LANES + at
                sums_ref[to : to + 1] = column_sum[:, at * LANES : (at + 1) * LANES]
        line += blocks * columns // LANES
        total = jnp.sum(row_stat, axis=0, keepdims=True)
        sums_ref[totals + part : totals + part + 1] = jnp.broadcast_to(total, (1, LANES))
    if with_vectors:
        last = cuts[-1][0] + cuts[-1][1] * cuts[-1][2]
        moment = moment_refs[0][...]
        count, wide = moment.shape
        grad = sum_of(slice(last, last + 16), slice(0, LANES))[:count, :wide]
        second = DECAY * moment + (1.0 - DECAY) * (grad * grad + 1e-30)
        vector_refs[0][...] = grad
        vector_refs[1][...] = second
        move = grad * lax.rsqrt(second)
        norm = jnp.sum(move * move, axis=1, keepdims=True)
        sums_ref[vector_line:] = jnp.zeros((16, LANES), F32)
        sums_ref[vector_line : vector_line + count] = jnp.broadcast_to(norm, (count, LANES))


def finish(parts, olds, cuts, moment, here, behind=()):
    columns = parts[-1].shape[1]
    rows = parts[-1].shape[0]
    outs = [array((count, blocks * columns), F32) for first, count, blocks in cuts]
    outs += [array((1, count), F32) for first, count, blocks in cuts]
    vectors = () if moment is None else (moment,)
    outs += [array(value.shape, F32) for value in vectors for unused in range(2)]
    outs += [array((sums_at(cuts, columns)[2] + 16 * len(vectors), LANES), F32)]
    args, specs, scratch = list(parts), [VMEM] * len(parts), []
    if len(parts) > 1:
        args, specs = [here.table, *parts], [scalars(), HBM] + [VMEM] * (len(parts) - 1)
        scratch = [pltpu.VMEM((rows, columns), parts[0].dtype), pltpu.SemaphoreType.DMA((1,))]
    args += list(olds) + list(vectors)
    specs += [VMEM] * (len(olds) + len(vectors))
    return call(
        functools.partial(finish_kernel, len(parts), cuts, bool(vectors)),
        tuple(outs),
        tuple(args),
        specs,
        (VMEM,) * len(outs),
        scratch,
        8 * rows * columns,
        8 * rows * columns,
        behind,
        16,
    )


def update_kernel(cuts, columns, full_rows, with_vectors, *refs):
    parts = len(cuts)
    refs = list(refs)

    def take(count):
        taken = refs[:count]
        del refs[:count]
        return taken

    grad_refs, master_refs, row_refs, old_refs = take(parts), take(parts), take(parts), take(parts)
    vector_refs = take(3 * int(with_vectors))
    (sums_ref,) = take(1)
    updated_refs, column_refs = take(parts), take(parts)
    norms, totals, vector_line = sums_at(cuts, columns)
    line = 0
    for part, (first, rows, blocks) in enumerate(cuts):
        wide = blocks * columns
        lines = wide // LANES
        square = jnp.concatenate([sums_ref[line + at : line + at + 1] for at in range(lines)], axis=1)
        weighted = jnp.concatenate(
            [sums_ref[norms + line + at : norms + line + at + 1] for at in range(lines)], axis=1
        )
        line += lines
        row_mean = sums_ref[totals + part : totals + part + 1, 0:1] / full_rows[part]
        col_stat = DECAY * old_refs[part][...] + (1.0 - DECAY) * (square / full_rows[part])
        column_refs[part][...] = col_stat
        norm = row_mean * jnp.sum(weighted / col_stat, axis=1, keepdims=True)
        scale = jnp.sqrt(norm / (full_rows[part] * wide))
        left = lax.rsqrt(turned_row(row_refs[part][...]) / row_mean) * (RATE / jnp.maximum(1.0, scale))
        updated_refs[part][...] = master_refs[part][...] - grad_refs[part][...] * left * lax.rsqrt(col_stat)
    if with_vectors:
        grad_ref, second_ref, vectors_ref = vector_refs
        count = grad_ref.shape[0]
        norm = sums_ref[vector_line : vector_line + count, 0:1]
        scale = jnp.sqrt(norm / columns)
        move = grad_ref[...] * lax.rsqrt(second_ref[...])
        refs[0][...] = vectors_ref[...] - VECTOR_RATE * move / jnp.maximum(1.0, scale)


def update(grads, masters, rows, olds, vectors, sums, cuts, columns, size, behind=()):
    outs = [array(grad.shape, F32) for grad in grads]
    outs += [array((1, grad.shape[1]), F32) for grad in grads]
    outs += [array(value.shape, F32) for value in vectors[2:]]
    args = (*grads, *masters, *rows, *olds, *vectors, sums)
    full_rows = tuple(grad.shape[0] * size for grad in grads)
    return call(
        functools.partial(update_kernel, cuts, columns, full_rows, bool(vectors)),
        tuple(outs),
        args,
        [VMEM] * len(args),
        (VMEM,) * len(outs),
        [],
        32 * grads[0].size,
        16 * grads[0].size,
        behind,
        16,
    )


class Place:
    def __init__(self):
        self.size = lax.axis_size("dp")
        self.chips = self.size // 2
        self.ring = list(range(0, self.chips, 2)) + list(range(self.chips - 1, 0, -2))
        self.small = self.size == HEADS
        index = lax.axis_index("dp")
        self.chip = index // 2
        self.core = index % 2 if self.small else jnp.zeros_like(index)
        where = [0] * self.chips
        for place, chip in enumerate(self.ring):
            where[chip] = place
        tables = [
            [self.ring[(where[chip] + offset) % self.chips] for offset in range(self.chips)]
            for chip in range(self.chips)
        ]
        self.table = lax.dynamic_index_in_dim(
            jnp.array(tables, jnp.int32), self.chip, 0, keepdims=False
        )

    def permute(self, array, target):
        pairs = []
        for chip in range(self.chips):
            for core in range(2):
                to_chip, to_core = target(chip, core)
                pairs.append((chip * 2 + core, to_chip * 2 + to_core))
        return lax.ppermute(array, "dp", pairs)

    def shift(self, array, by):
        where = {chip: place for place, chip in enumerate(self.ring)}
        return self.permute(
            array, lambda chip, core: (self.ring[(where[chip] + by) % self.chips], core)
        )

    def swap(self, array):
        return self.permute(array, lambda chip, core: (chip, 1 - core))

    def cross(self, array, mask):
        return self.permute(array, lambda chip, core: (chip ^ mask, core))

    def masks(self):
        return [1 << bit for bit in range(self.chips.bit_length() - 1)]


def section_shift(array, by):
    size = lax.axis_size("section")
    pairs = [(i, i + by) for i in range(size) if 0 <= i + by < size]
    return lax.ppermute(array, "section", pairs)


def upper_rows(rows):
    return (rows // 2 + 15) // 16 * 16


def gate_kernel():
    pass


def gated(arrays, behind):
    return call(gate_kernel, (), (), [], (), [], 0, 1 << 10, behind, passing=arrays)[1]


class RingGather:
    def __init__(self, own, here):
        self.here = here
        self.rows, self.columns = own.shape
        self.pieces = [(0, 0, own)]
        self.ahead = self.behind = own
        self.step = 0
        self.round()

    def round(self, behind=(), passing=()):
        here = self.here
        self.step += 1
        if behind or passing:
            self.ahead, self.behind, *passing = gated((self.ahead, self.behind, *passing), behind)
            if self.step > 1:
                self.pieces[-2:] = [
                    (1 - self.step, 0, self.ahead),
                    (self.step - 1, 0, self.behind),
                ]
        if self.step < here.chips // 2:
            self.ahead = here.shift(self.ahead, 1)
            self.behind = here.shift(self.behind, -1)
            self.pieces += [(-self.step, 0, self.ahead), (self.step, 0, self.behind)]
        else:
            cut = upper_rows(self.rows)
            self.ahead = here.shift(self.ahead[:cut], 1)
            self.behind = here.shift(self.behind[cut:], -1)
            self.pieces += [(self.step, 0, self.ahead), (self.step, cut, self.behind)]
        return passing

    def heads(self):
        return self.ahead, self.behind


def placed(rings, here, behind=()):
    plan, arrays, base = [], [], 0
    for ring in rings:
        for offset, row, piece in ring.pieces:
            plan.append((offset % here.chips, base + row))
            arrays.append(piece)
        base += ring.rows
    columns = arrays[0].shape[1]
    return call(
        functools.partial(place_kernel, tuple(plan)),
        array((here.chips, base, columns), arrays[0].dtype),
        (here.table, *arrays),
        [scalars()] + [HBM] * len(arrays),
        VMEM,
        [pltpu.SemaphoreType.DMA((len(arrays),))],
        0,
        4 * here.chips * base * columns,
        behind,
        56,
    )


def place_kernel(plan, chips_ref, *refs):
    out, sems = refs[-2:]
    pairs = []
    for piece, (place, row) in zip(refs, plan):
        pairs.append((piece, out.at[chips_ref[place], pl.ds(row, piece.shape[0])]))
    for copy in fetch(pairs, sems):
        copy.wait()


def pack_kernel(project_ref, merge_ref, vectors_ref, expand_ref, out_ref, expand_out):
    rows, width = merge_ref.shape
    for third in range(3):
        out_ref[third * rows : (third + 1) * rows] = project_ref[:, third * width : (third + 1) * width].astype(BF16)
    out_ref[3 * rows : 4 * rows] = merge_ref[...].astype(BF16)
    count, wide = vectors_ref.shape
    vectors = jnp.concatenate([vectors_ref[...], jnp.zeros((16 - count, wide), F32)], axis=0)
    out_ref[4 * rows :] = jnp.concatenate(
        [vectors.astype(BF16), jnp.zeros((16, width - wide), BF16)], axis=1
    )
    expand_out[...] = expand_ref[...].astype(BF16)


def pack_rows(project, merge, vectors, expand):
    rows, width = merge.shape
    return call(
        pack_kernel,
        (array((4 * rows + 16, width), BF16), array(expand.shape, BF16)),
        (project, merge, vectors, expand),
        [VMEM] * 4,
        (VMEM, VMEM),
        [],
        0,
        2 << 20,
    )


def half_kernel(side, whole_ref, out_ref):
    rows = out_ref.shape[0]
    out_ref[...] = whole_ref[side * rows : (side + 1) * rows].astype(BF16)


def half_of(whole, side, behind):
    half = array((whole.shape[0] // 2, whole.shape[1]), BF16)
    return call(functools.partial(half_kernel, side), half, (whole,), [VMEM], VMEM, [], 0, 2 << 20, behind)


def vectors_of(near, far, core, wide):
    cuts = [part[:, -16:, :wide] for part in (near, far)]
    rows = jnp.where(core == 0, jnp.stack(cuts), jnp.stack(cuts[::-1]))
    return rows.transpose(2, 1, 0, 3).reshape(16, -1).astype(F32)


def gather_plainly(project, merge, expand, shrink, vectors):
    width = merge.shape[1]

    def whole_of_rows(rows):
        whole = lax.all_gather(rows.astype(BF16), "dp", axis=0, tiled=True)
        return whole.reshape(PAIRS, 2, -1, whole.shape[1])

    parts = [whole_of_rows(project[:, at * width : (at + 1) * width]) for at in range(3)]
    cuts = [jnp.concatenate([*parts, whole_of_rows(merge)], axis=2)]
    cuts += [whole_of_rows(expand), whole_of_rows(shrink)]
    rows = lax.all_gather(vectors.astype(BF16), "dp", axis=1, tiled=True)
    rows = jnp.pad(rows, ((0, 16 - vectors.shape[0]), (0, 0)))
    return *((cut[:, 0], cut[:, 1]) for cut in cuts), rows.astype(F32)


def far_kernel(half, chips_ref, blocks, upper_ref, lower_ref, sems):
    cut = upper_ref.shape[0]
    chip = chips_ref[half]
    pairs = [
        (blocks.at[chip, pl.ds(0, cut)], upper_ref),
        (blocks.at[chip, pl.ds(cut, lower_ref.shape[0])], lower_ref),
    ]
    for copy in fetch(pairs, sems):
        copy.wait()


def add_kernel(ahead_at, behind_at, chips_ref, blocks, ahead_got, behind_got, ahead_out, behind_out, ahead_ref, behind_ref, sems):
    pairs = [
        (blocks.at[chips_ref[ahead_at]], ahead_out),
        (blocks.at[chips_ref[behind_at]], behind_out),
        (ahead_got, ahead_ref),
        (behind_got, behind_ref),
    ]
    for copy in fetch(pairs, sems):
        copy.wait()
    rows = behind_out.shape[0]
    for got, out, cut in (
        (ahead_ref, ahead_out, pl.ds(0, ahead_ref.shape[0])),
        (behind_ref, behind_out, pl.ds(rows - behind_ref.shape[0], behind_ref.shape[0])),
    ):
        out[cut] = (out[cut].astype(F32) + got[...].astype(F32)).astype(BF16)


class RingSum:
    def __init__(self, blocks, here):
        self.blocks = blocks
        self.here = here
        self.step = here.chips // 2
        self.sent = None

    def round(self, *behind, passing=()):
        here, blocks, step = self.here, self.blocks, self.step
        rows, columns = blocks.shape[1:]
        if self.sent is None:
            cut = upper_rows(rows)
            payload = call(
                functools.partial(far_kernel, step),
                (array((cut, columns), BF16), array((rows - cut, columns), BF16)),
                (here.table, blocks),
                [scalars(), HBM],
                (VMEM, VMEM),
                [pltpu.SemaphoreType.DMA((2,))],
                0,
                4 * rows * columns,
                behind,
            )
        else:
            whole = array((rows, columns), BF16)
            payload = call(
                functools.partial(add_kernel, step, here.chips - step),
                (whole, whole),
                (here.table, blocks, *self.sent),
                [scalars(), HBM, HBM, HBM],
                (VMEM, VMEM),
                [pltpu.VMEM(part.shape, BF16) for part in self.sent] + [pltpu.SemaphoreType.DMA((4,))],
                2 * rows * columns,
                12 * rows * columns,
                behind,
                passing=passing,
            )
            if passing:
                payload, passing = payload
        self.step -= 1
        self.sent = (here.shift(payload[0], 1), here.shift(payload[1], -1))
        return (payload[0], *passing)

    def parts(self):
        return (self.blocks, *self.sent)


def small_sum(vector, here):
    if not here.small:
        return lax.psum(vector, "dp")
    vector = vector + here.swap(vector)
    near = [here.cross(vector, mask) for mask in (1, 2, 3)]
    vector = (vector + near[0]) + (near[1] + near[2])
    for mask in here.masks()[2:]:
        vector = vector + here.cross(vector, mask)
    return vector


def segments(lengths_row, count):
    ends = jnp.cumsum(lengths_row)
    places = jnp.arange(count, dtype=jnp.int32)
    return jnp.sum((places[:, None] >= ends[None, :]).astype(jnp.int32), axis=1)


def per_device(
    frames,
    lengths,
    cotangent,
    project_weight,
    merge_weight,
    expand_weight,
    shrink_weight,
    vectors,
    project_row,
    project_col,
    merge_row,
    merge_col,
    expand_row,
    expand_col,
    shrink_row,
    shrink_col,
    vector_moment,
):
    here = Place()
    core = here.core.reshape(1)
    is_first = lax.axis_index("section") == 0
    micro = lengths.shape[0]
    count, width = frames.shape
    block = count // micro
    segment = jax.vmap(lambda lengths_row: segments(lengths_row, block))(lengths)
    live = (segment < UTTS).astype(F32).reshape(count, 1)
    visible = (segment[:, :, None] == segment[:, None, :]).astype(F32)

    masters = (project_weight[0], merge_weight[0], expand_weight[0], shrink_weight[0])
    first = is_first.astype(jnp.int32).reshape(1)
    if here.small:
        pm_rows, e_rows = pack_rows(masters[0], masters[1], vectors[0], masters[2])
        pm_ring, e_ring = RingGather(pm_rows, here), RingGather(e_rows, here)
        pm_ring.round()
        pm_ring.round(e_ring.heads())
        e_ring.round()
        upper_ring = RingGather(half_of(masters[3], 0, pm_ring.heads()), here)
        pm_ring.round(e_ring.heads())
        e_ring.round()
        lower_ring = RingGather(half_of(masters[3], 1, e_ring.heads()), here)
        e_ring.round(upper_ring.heads())
        upper_ring.round()
        upper_ring.round(lower_ring.heads())
        lower_ring.round()
        upper_ring.round(lower_ring.heads())
        lower_ring.round()
        lower_ring.round()
        near = placed([pm_ring], here)
        pm = (near, here.swap(near))
        vec = vectors_of(*pm, here.core, vectors.shape[2])
        near = placed([e_ring], here)
        e = (near, here.swap(near))
        near = placed([upper_ring, lower_ring], here)
        s = (near, here.swap(near))
        kept = attend_block(core, frames, visible, vec, pm, (near,))
        hidden, slope = expand_block(core, kept[-1], vec, e)
    else:
        pm, e, s, vec = gather_plainly(*masters, vectors[0])
        kept = attend_block(core, frames, visible, vec, pm)
        hidden, slope = expand_block(core, kept[-1], vec, e)

    unused, low = shrink_block(core, kept[3], hidden, vec, s)
    start = jnp.where(is_first, frames, section_shift(low, 1))
    kept = attend_block(core, start, visible, vec, pm)
    normed, packed, mixed, middle, normed_two = kept
    hidden, slope = expand_block(core, normed_two, vec, e)

    incoming, unused = incoming_grad(jnp.zeros((1,), jnp.int32), frames, cotangent, live, ())
    unused, unused, back_middle, back_branch, sums_two, sums_up = back_hidden_block(
        core, incoming, middle, vec, s, e, slope, ()
    )
    unused, unused, low, unused = back_attend_block(
        core, first, start, back_middle, back_branch, packed, visible, vec, sums_two, sums_up, pm, ()
    )
    output, unused = shrink_block(core, middle, hidden, vec, s, (low,))
    incoming, low_incoming = incoming_grad(first, section_shift(low, -1), cotangent, live, (output,))
    swap = here.swap if here.small else lambda rows: rows

    shared = [swap(rows) for rows in (hidden, normed_two, normed, mixed)]
    behind = ()
    if here.small:
        shrink_ring = RingSum(
            shrink_grad(core, hidden, shared[0], low_incoming, swap(low_incoming), shared[1:]), here
        )
        behind = shrink_ring.round()
    low_out, back_pre, back_middle, back_branch, sums_two, sums_up = back_hidden_block(
        core, incoming, middle, vec, s, e, slope, behind
    )
    if here.small:
        last, back_pre, back_branch = shrink_ring.round(passing=(back_pre, back_branch))
        behind = (last,)
    back_packed, back_inputs, low, vector_sums = back_attend_block(
        core, first, start, back_middle, back_branch, packed, visible, vec, sums_two, sums_up, pm, behind
    )
    layer_outputs = output[None]
    input_grads = back_inputs[None]

    rows = masters[0].shape[0]
    shrink_cuts = ((0, masters[3].shape[0], 1),)
    expand_cuts = ((0, rows, 1),)
    both_cuts = ((0, rows, 3), (3 * rows, rows, 1))
    shrink_olds, expand_olds = (shrink_row,), (expand_row,)
    both_olds = (project_row, merge_row)
    moment = vector_moment[0]
    if here.small:
        last, back_packed, vector_sums = shrink_ring.round(passing=(back_packed, vector_sums))
        expand_ring = RingSum(
            expand_grad(core, normed_two, shared[1], back_pre, swap(back_pre), (last,)), here
        )
        (last,) = expand_ring.round()
        (last,) = shrink_ring.round(last)
        both_ring = RingSum(
            project_grad(
                core,
                (
                    normed,
                    shared[2],
                    back_packed,
                    swap(back_packed),
                    mixed,
                    shared[3],
                    back_branch,
                    swap(back_branch),
                    vector_sums,
                    swap(vector_sums),
                ),
                (last,),
            ),
            here,
        )
        (last,) = both_ring.round()
        (last,) = expand_ring.round(last)
        shrink_ends = finish(shrink_ring.parts(), shrink_olds, shrink_cuts, None, here, (last,))
        (last,) = both_ring.round(shrink_ends[0])
        (last,) = expand_ring.round(last)
        (last,) = both_ring.round(last)
        (last,) = expand_ring.round(last)
        (last,) = both_ring.round(last)
        expand_ends = finish(expand_ring.parts(), expand_olds, expand_cuts, None, here, (last,))
        both_parts = both_ring.parts()
    else:

        def total(left, right):
            whole = dot_first(left, right).astype(BF16)
            return lax.psum_scatter(whole, "dp", scatter_dimension=0, tiled=True).astype(F32)

        shrink_ends = finish((total(hidden, low_out),), shrink_olds, shrink_cuts, None, here)
        expand_ends = finish((total(normed_two, back_pre),), expand_olds, expand_cuts, None, here)
        thirds = [total(normed, back_packed[:, at * width : (at + 1) * width]) for at in range(3)]
        vector_rows = lax.psum_scatter(vector_sums, "dp", scatter_dimension=1, tiled=True)
        vector_rows = jnp.pad(vector_rows, ((0, 0), (0, width - vector_rows.shape[1])))
        both_parts = (jnp.concatenate([*thirds, total(mixed, back_branch), vector_rows], axis=0),)
        last = vector_sums

    both_ends = finish(both_parts, both_olds, both_cuts, moment, here)
    ends = (shrink_ends, expand_ends, both_ends)
    sums = small_sum(jnp.concatenate([end[-1] for end in ends], axis=0), here)

    def updated(end, cuts, matrices, cols_old, columns, values):
        nonlocal sums
        count = len(cuts)
        lines = end[-1].shape[0]
        own, sums = sums[:lines], sums[lines:]
        grads, rows_new, vector_parts = end[:count], end[count : 2 * count], end[2 * count : -1]
        results = update(
            grads, matrices, rows_new, cols_old, (*vector_parts, *values), own, cuts, columns, here.size
        )
        outs = []
        for part in range(count):
            outs += [grads[part][None], rows_new[part], results[count + part], results[part][None]]
        return outs, (*vector_parts, *results[2 * count :])

    shrink_outs, unused = updated(shrink_ends, shrink_cuts, masters[3:], (shrink_col,), width, ())
    expand_outs, unused = updated(
        expand_ends, expand_cuts, masters[2:3], (expand_col,), 4 * width, ()
    )
    both_outs, vector_outs = updated(
        both_ends, both_cuts, masters[:2], (project_col, merge_col), width, (vectors[0],)
    )
    return (
        layer_outputs,
        input_grads,
        *both_outs,
        *expand_outs,
        *shrink_outs,
        *(rows[None] for rows in vector_outs),
    )


def solution(mesh):
    placed = (
        P("dp", None),
        P("dp", None),
        P("dp", None),
        P("section", "dp", None),
        P("section", "dp", None),
        P("section", "dp", None),
        P("section", "dp", None),
        P("section", None, "dp"),
        P("section", "dp"),
        P("section", None),
        P("section", "dp"),
        P("section", None),
        P("section", "dp"),
        P("section", None),
        P("section", "dp"),
        P("section", None),
        P("section", None, "dp"),
    )
    matrix = (
        P("section", "dp", None),
        P("section", "dp"),
        P("section", None),
        P("section", "dp", None),
    )
    return jax.shard_map(
        per_device,
        mesh=mesh,
        in_specs=placed,
        out_specs=(
            P("section", "dp", None),
            P("section", "dp", None),
            *matrix,
            *matrix,
            *matrix,
            *matrix,
            P("section", None, "dp"),
            P("section", None, "dp"),
            P("section", None, "dp"),
        ),
        check_vma=False,
    )
```

```python
import functools
import math

import jax
import jax.numpy as jnp
from jax import lax
from jax.experimental import pallas as pl
from jax.experimental.pallas import tpu as pltpu
from jax.sharding import PartitionSpec as P

HEADS = 16
HEAD_DIM = 64
PAIRS = HEADS // 2
UTTS = 3
STEP = 10

EPSILON = 1e-05
RATE = 0.04
VECTOR_RATE = 0.25
MASKED = -1e30
BF16 = jnp.bfloat16
F32 = jnp.float32
VMEM = pl.BlockSpec(memory_space=pltpu.VMEM)
HBM = pl.BlockSpec(memory_space=pl.ANY)
MIB = 1024 * 1024


def dot(left, right):
    return lax.dot_general(left, right, (((1,), (0,)), ((), ())), preferred_element_type=F32)


def dot_last(left, right):
    return lax.dot_general(left, right, (((1,), (1,)), ((), ())), preferred_element_type=F32)


def dot_first(left, right):
    return lax.dot_general(left, right, (((0,), (0,)), ((), ())), preferred_element_type=F32)


def moments(values):
    centred = values - jnp.mean(values, axis=-1, keepdims=True)
    spread = jnp.mean(centred * centred, axis=-1, keepdims=True)
    scale = lax.rsqrt(spread + EPSILON)
    return centred * scale, scale


def norm_back(grad, unit, scale, gain):
    inner = grad * gain
    first = jnp.mean(inner, axis=-1, keepdims=True)
    second = jnp.mean(inner * unit, axis=-1, keepdims=True)
    return scale * (inner - first - unit * second)


def fetch(pairs, sems):
    copies = [
        pltpu.make_async_copy(source, target, sems.at[index])
        for index, (source, target) in enumerate(pairs)
    ]
    for copy in copies:
        copy.start()
    return copies


def half_masks():
    lane = lax.broadcasted_iota(jnp.int32, (1, 128), 1)
    low = jnp.where(lane < HEAD_DIM, 1.0, 0.0)
    return low.astype(BF16), (1.0 - low).astype(BF16)


def two_heads(tile, masks):
    return jnp.concatenate([tile * masks[0], tile * masks[1]], axis=0)


def side_by_side(both):
    half = both.shape[0] // 2
    return jnp.concatenate([both[:half], both[half:]], axis=1)


def weights_of(scores, visible):
    scores = jnp.where(visible, scores * HEAD_DIM**-0.5, MASKED)
    shifted = jnp.exp(scores - jnp.max(scores, axis=-1, keepdims=True))
    return shifted / jnp.sum(shifted, axis=-1, keepdims=True)


def scalars():
    return pl.BlockSpec(memory_space=pltpu.SMEM)


def array(shape, kind):
    return jax.ShapeDtypeStruct(shape, kind)


def call(kernel, outs, args, in_specs, out_specs, scratch, flops, size, behind=(), limit=12, passing=()):
    given, skipped = len(args), len(behind) + len(passing)
    single = not isinstance(outs, tuple)
    results = (outs,) if single else outs
    result_specs = (out_specs,) if single else out_specs
    count = len(results)

    def body(*refs):
        kernel(*refs[:given], *refs[given + skipped :][:count], *refs[given + skipped + count + len(passing) :])

    returned = pl.pallas_call(
        body,
        out_shape=(*results, *(array(value.shape, value.dtype) for value in passing)),
        in_specs=[
            *in_specs,
            *(HBM for unused in range(skipped)),
        ],
        out_specs=(*result_specs, *(HBM for unused in passing)),
        scratch_shapes=scratch,
        input_output_aliases={given + len(behind) + at: count + at for at in range(len(passing))},
        compiler_params=pltpu.CompilerParams(vmem_limit_bytes=limit * MIB),
        cost_estimate=pl.CostEstimate(flops=flops, bytes_accessed=size, transcendentals=0),
    )(*args, *behind, *passing)
    own = returned[0] if single else tuple(returned[:count])
    return (own, tuple(returned[count:])) if passing else own


def both_cores(core, near, far, whole, cuts):
    pairs = []
    for cut in cuts:
        pairs.append((near.at[cut], whole.at[cut[0], core, *cut[1:]]))
        pairs.append((far.at[cut], whole.at[cut[0], 1 - core, *cut[1:]]))
    return pairs


ALL = slice(None)


def quarters_of(core, near, far, whole, order):
    rows = whole.shape[3]
    pairs = []
    for at in order:
        pairs.append((near.at[:, pl.ds(at * rows, rows)], whole.at[at, :, core]))
        pairs.append((far.at[:, pl.ds(at * rows, rows)], whole.at[at, :, 1 - core]))
    return pairs


def quarters_scratch(width):
    return pltpu.VMEM((4, PAIRS, 2, width // HEADS, width), BF16)


def columns_cut(start, size):
    return (ALL, ALL, pl.ds(start, size))


def attend_kernel(core_ref, x_ref, mask_ref, vec_ref, near, far, a_ref, packed_ref, o_ref, x1_ref, c_ref, w, sems):
    count, width = x_ref.shape
    block = mask_ref.shape[1]
    step = 512
    copies = fetch(quarters_of(core_ref[0], near, far, w, range(4)), sems)
    unit, unused = moments(x_ref[...].astype(F32))
    a_ref[...] = (unit * vec_ref[0:1] + vec_ref[1:2]).astype(BF16)
    for third in range(3):
        copies[2 * third].wait()
        copies[2 * third + 1].wait()
        for cut in range(width // step):
            at = third * width + cut * step
            matrix = w[third, :, :, :, cut * step : (cut + 1) * step].reshape(width, step)
            result = dot(a_ref[...], matrix)
            if third != 1:
                row = 2 if third == 0 else 3
                result = result + vec_ref[row : row + 1, cut * step : (cut + 1) * step]
            packed_ref[:, at : at + step] = result.astype(BF16)
    masks = half_masks()
    for micro in range(count // block):
        rows = slice(micro * block, (micro + 1) * block)
        visible = mask_ref[micro] > 0.0
        visible = jnp.concatenate([visible, visible], axis=0)
        for at in range(0, width, 128):
            queries = packed_ref[rows, at : at + 128]
            keys = packed_ref[rows, at + width : at + width + 128]
            values = packed_ref[rows, at + 2 * width : at + 2 * width + 128]
            attend = weights_of(dot_last(two_heads(queries, masks), keys), visible).astype(BF16)
            mixed = dot(side_by_side(attend), two_heads(values, masks))
            o_ref[rows, at : at + 128] = mixed.astype(BF16)
    copies[6].wait()
    copies[7].wait()
    for at in range(0, width, step):
        cut = slice(at, at + step)
        matrix = w[3, :, :, :, cut].reshape(width, step)
        x1_ref[:, cut] = x_ref[:, cut].astype(F32) + (dot(o_ref[...], matrix) + vec_ref[4:5, cut])
    unit, unused = moments(x1_ref[...])
    c_ref[...] = (unit * vec_ref[5:6] + vec_ref[6:7]).astype(BF16)


def whole_of(near):
    chips, rows, columns = near.shape
    return pltpu.VMEM((chips, 2, rows, columns), near.dtype)


def attend_block(core, x, mask, vec, pm, behind=()):
    count, width = x.shape
    low = array((count, width), BF16)
    return call(
        attend_kernel,
        (low, array((count, 3 * width), BF16), low, array((count, width), F32), low),
        (core, x, mask, vec, *pm),
        [scalars()] + [VMEM] * 3 + [HBM] * 2,
        (VMEM,) * 5,
        [quarters_scratch(width), pltpu.SemaphoreType.DMA((8,))],
        8 * count * width * width,
        20 << 20,
        behind=behind,
        limit=32,
    )


def gelu_parts(values):
    cdf = 0.5 * (1.0 + lax.erf(values * math.sqrt(0.5)))
    slope = cdf + values * jnp.exp(-0.5 * values * values) * (1.0 / math.sqrt(2.0 * math.pi))
    return values * cdf, slope


def expand_kernel(core_ref, c_ref, vec_ref, near, far, hidden_ref, slope_hbm, w, slope, sems, out_sems):
    count, width = c_ref.shape
    step = 256
    quarters = w.shape[3] // width
    copies = fetch(
        both_cores(core_ref[0], near, far, w, [columns_cut(at * width, width) for at in range(quarters)]), sems
    )
    sent = []
    for quarter in range(quarters):
        copies[2 * quarter].wait()
        copies[2 * quarter + 1].wait()
        for cut in range(width // step):
            at = quarter * width + cut * step
            result = dot(c_ref[...], w[:, :, :, at : at + step].reshape(width, step))
            bias = vec_ref[8 + quarter : 9 + quarter, cut * step : (cut + 1) * step]
            hidden, rise = gelu_parts(result + bias)
            hidden_ref[:, at : at + step] = hidden.astype(BF16)
            slope[:, at : at + step] = rise
        at = slice(quarter * width, (quarter + 1) * width)
        copy = pltpu.make_async_copy(slope.at[:, at], slope_hbm.at[:, at], out_sems.at[quarter])
        copy.start()
        sent.append(copy)
    for copy in sent:
        copy.wait()


def expand_block(core, c, vec, e):
    count, width = c.shape
    hidden = 4 * width
    return call(
        expand_kernel,
        (array((count, hidden), BF16), array((count, hidden), F32)),
        (core, c, vec, *e),
        [scalars()] + [VMEM] * 2 + [HBM] * 2,
        (VMEM, HBM),
        [
            whole_of(e[0]),
            pltpu.VMEM((count, hidden), F32),
            pltpu.SemaphoreType.DMA((8,)),
            pltpu.SemaphoreType.DMA((4,)),
        ],
        2 * count * width * hidden,
        20 << 20,
        limit=32,
    )


def shrink_kernel(core_ref, x1_ref, hidden_ref, vec_ref, near, far, y_ref, low_ref, w, sems):
    chips, unused, rows, width = w.shape
    step = 512
    group = width // (2 * rows)
    copies = fetch(
        both_cores(core_ref[0], near, far, w, [(pl.ds(at, group),) for at in range(0, chips, group)]), sems
    )
    for index in range(chips // group):
        copies[2 * index].wait()
        copies[2 * index + 1].wait()
        left = hidden_ref[:, index * width : (index + 1) * width]
        for at in range(0, width, step):
            cut = slice(at, at + step)
            matrix = w[index * group : (index + 1) * group, :, :, cut].reshape(width, step)
            result = dot(left, matrix)
            if index == 0:
                y_ref[:, cut] = x1_ref[:, cut] + result
            elif index < chips // group - 1:
                y_ref[:, cut] += result
            else:
                total = y_ref[:, cut] + result + vec_ref[7:8, cut]
                y_ref[:, cut] = total
                low_ref[:, cut] = total.astype(BF16)


def shrink_block(core, x1, hidden, vec, s, behind=()):
    count, width = x1.shape
    return call(
        shrink_kernel,
        (array((count, width), F32), array((count, width), BF16)),
        (core, x1, hidden, vec, *s),
        [scalars()] + [VMEM] * 3 + [HBM] * 2,
        (VMEM, VMEM),
        [whole_of(s[0]), pltpu.SemaphoreType.DMA((8,))],
        8 * count * width * width,
        16 << 20,
        behind=behind,
        limit=28,
    )


def back_hidden_kernel(core_ref, dy_ref, x1_ref, vec_ref, s_near, s_far, e_near, e_far, slope_hbm, gf_ref, gu_ref, dx1_ref, gat_ref, sums_ref, bias_ref, ws, we, slope, dc, sems, slope_sems):
    chips, unused, rows, width = ws.shape
    group = width // (2 * rows)
    quarters = chips // group
    core = core_ref[0]
    pairs = []
    for index in range(quarters):
        at = pl.ds(index * width, width)
        pairs += both_cores(core, s_near, s_far, ws, [(pl.ds(index * group, group),)])
        pairs.append((slope_hbm.at[:, at], slope.at[:, at]))
        pairs += both_cores(core, e_near, e_far, we, [columns_cut(index * width, width)])
    copies = fetch(pairs, sems)
    gf_ref[...] = dy_ref[...].astype(BF16)
    step = 512
    for index in range(quarters):
        for copy in copies[5 * index : 5 * index + 3]:
            copy.wait()
        for near in range(group):
            matrix = ws[index * group + near].reshape(2 * rows, width)
            at = slice(index * width + near * 2 * rows, index * width + (near + 1) * 2 * rows)
            back = (dot_last(gf_ref[...], matrix) * slope[:, at]).astype(BF16)
            gu_ref[:, at] = back
            bias_ref[:, at] = jnp.sum(back.astype(F32), axis=0, keepdims=True)
        for copy in copies[5 * index + 3 : 5 * index + 5]:
            copy.wait()
        at = slice(index * width, (index + 1) * width)
        left = gu_ref[:, at]
        for half in range(2):
            matrix = we[half * (chips // 2) : (half + 1) * (chips // 2), :, :, at].reshape(step, width)
            to = slice(half * step, (half + 1) * step)
            result = dot_last(left, matrix)
            if index == 0:
                dc[:, to] = result
            else:
                dc[:, to] += result
    unit, scale = moments(x1_ref[...])
    grad = dc[...]
    back = dy_ref[...] + norm_back(grad, unit, scale, vec_ref[5:6])
    dx1_ref[...] = back
    gat_ref[...] = back.astype(BF16)
    sums_ref[...] = jnp.zeros_like(sums_ref)
    sums_ref[0:1] = jnp.sum(grad * unit, axis=0, keepdims=True)
    sums_ref[1:2] = jnp.sum(grad, axis=0, keepdims=True)
    sums_ref[2:3] = jnp.sum(gf_ref[...].astype(F32), axis=0, keepdims=True)
    sums_ref[3:4] = jnp.sum(gat_ref[...].astype(F32), axis=0, keepdims=True)


def back_hidden_block(core, dy, x1, vec, s, e, slope, behind):
    count, width = x1.shape
    hidden = slope.shape[1]
    return call(
        back_hidden_kernel,
        (
            array((count, width), BF16),
            array((count, hidden), BF16),
            array((count, width), F32),
            array((count, width), BF16),
            array((8, width), F32),
            array((1, hidden), F32),
        ),
        (core, dy, x1, vec, *s, *e, slope),
        [scalars()] + [VMEM] * 3 + [HBM] * 5,
        (VMEM,) * 6,
        [
            whole_of(s[0]),
            whole_of(e[0]),
            pltpu.VMEM((count, hidden), F32),
            pltpu.VMEM((count, width), F32),
            pltpu.SemaphoreType.DMA((20,)),
            pltpu.SemaphoreType.DMA((4,)),
        ],
        16 * count * width * width,
        32 << 20,
        behind,
        limit=48,
    )


def back_attend_kernel(core_ref, first_ref, x_ref, dx1_ref, gat_ref, packed_ref, mask_ref, vec_ref, two_ref, up_ref, near, far, gqkv_ref, dx_ref, low_ref, sums_ref, w, go, sems):
    count, width = x_ref.shape
    block = mask_ref.shape[1]
    step = 512
    copies = fetch(quarters_of(core_ref[0], near, far, w, (3, 0, 1, 2)), sems)
    masks = half_masks()
    factor = HEAD_DIM**-0.5
    copies[0].wait()
    copies[1].wait()
    chips = w.shape[1]
    for half in range(2):
        matrix = w[3, half * (chips // 2) : (half + 1) * (chips // 2)].reshape(step, width)
        go[:, half * step : (half + 1) * step] = dot_last(gat_ref[...], matrix).astype(BF16)
    tiles = range(0, width, 128)
    for micro in range(count // block):
        rows = slice(micro * block, (micro + 1) * block)
        visible = mask_ref[micro] > 0.0
        visible = jnp.concatenate([visible, visible], axis=0)
        queries = [two_heads(packed_ref[rows, at : at + 128], masks) for at in tiles]
        keys = [packed_ref[rows, at + width : at + width + 128] for at in tiles]
        values = [packed_ref[rows, at + 2 * width : at + 2 * width + 128] for at in tiles]
        back = [two_heads(go[rows, at : at + 128], masks) for at in tiles]
        scores = [dot_last(query, key) for query, key in zip(queries, keys)]
        slopes = [dot_last(grad, value) for grad, value in zip(back, values)]
        attend = [weights_of(score, visible) for score in scores]
        low = [weight.astype(BF16) for weight in attend]
        inner = [jnp.sum(weight * slope, axis=-1, keepdims=True) for weight, slope in zip(attend, slopes)]
        scores = [
            (weight * (slope - total)).astype(BF16)
            for weight, slope, total in zip(attend, slopes, inner)
        ]
        grad_q = [dot(side_by_side(score), two_heads(key, masks)) for score, key in zip(scores, keys)]
        grad_k = [dot_first(score, query) for score, query in zip(scores, queries)]
        grad_v = [dot_first(weight, grad) for weight, grad in zip(low, back)]
        for at, one, two, three in zip(tiles, grad_q, grad_k, grad_v):
            gqkv_ref[rows, at : at + 128] = (one * factor).astype(BF16)
            gqkv_ref[rows, at + width : at + width + 128] = (two * factor).astype(BF16)
            gqkv_ref[rows, at + 2 * width : at + 2 * width + 128] = three.astype(BF16)
    for copy in copies[2:]:
        copy.wait()
    for half in range(2):
        total = None
        for third in range(3):
            matrix = w[third, half * (chips // 2) : (half + 1) * (chips // 2)].reshape(step, width)
            result = dot_last(gqkv_ref[:, third * width : (third + 1) * width], matrix)
            total = result if total is None else total + result
        dx_ref[:, half * step : (half + 1) * step] = total
    unit, scale = moments(x_ref[...].astype(F32))
    grad = dx_ref[...]
    sums_ref[...] = jnp.zeros_like(sums_ref)
    sums_ref[0:1] = jnp.sum(grad * unit, axis=0, keepdims=True)
    sums_ref[1:2] = jnp.sum(grad, axis=0, keepdims=True)
    back = dx1_ref[...] + norm_back(grad, unit, scale, vec_ref[0:1])
    low = back.astype(BF16)
    low_ref[...] = low
    dx_ref[...] = jnp.where(first_ref[0] == 1, back, low.astype(F32))
    for row, third in ((2, 0), (3, 2)):
        part = gqkv_ref[:, third * width : (third + 1) * width]
        sums_ref[row : row + 1] = jnp.sum(part.astype(F32), axis=0, keepdims=True)
    sums_ref[4:5] = two_ref[3:4]
    sums_ref[5:8] = two_ref[0:3]
    for quarter in range(4):
        sums_ref[8 + quarter : 9 + quarter] = up_ref[:, quarter * width : (quarter + 1) * width]


def back_attend_block(core, first, x, dx1, gat, packed, mask, vec, two, up, pm, behind):
    count, width = x.shape
    return call(
        back_attend_kernel,
        (
            array((count, 3 * width), BF16),
            array((count, width), F32),
            array((count, width), BF16),
            array((16, width), F32),
        ),
        (core, first, x, dx1, gat, packed, mask, vec, two, up, *pm),
        [scalars()] * 2 + [VMEM] * 8 + [HBM] * 2,
        (VMEM,) * 4,
        [quarters_scratch(width), pltpu.VMEM((count, width), BF16), pltpu.SemaphoreType.DMA((8,))],
        12 * count * width * width,
        20 << 20,
        behind,
        limit=32,
    )


def incoming_kernel(first_ref, mail_ref, cotangent_ref, live_ref, out_ref, low_ref):
    targets = cotangent_ref[...].astype(F32) * live_ref[...]
    mail = mail_ref[...].astype(F32)
    out = jnp.where(first_ref[0] == 1, mail, targets)
    out_ref[...] = out
    low_ref[...] = out.astype(BF16)


def incoming_grad(first, mail, cotangent, live, behind):
    shape = cotangent.shape
    return call(
        incoming_kernel,
        (array(shape, F32), array(shape, BF16)),
        (first, mail, cotangent, live),
        [scalars()] + [VMEM] * 3,
        (VMEM, VMEM),
        [],
        0,
        10 * cotangent.size,
        behind,
    )


def shrink_grad_kernel(core_ref, near_ref, far_ref, right_ref, other_ref, out_ref):
    chips, rows, width = out_ref.shape
    for chip in range(chips):
        at = pl.ds(pl.multiple_of((2 * chip + core_ref[0]) * rows, rows), rows)
        total = dot_first(near_ref[:, at], right_ref[...]) + dot_first(far_ref[:, at], other_ref[...])
        out_ref[chip] = total.astype(BF16)


def shrink_grad(core, near, far, right, other, behind):
    tokens, hidden = near.shape
    width = right.shape[1]
    return call(
        shrink_grad_kernel,
        array((PAIRS, hidden // HEADS, width), BF16),
        (core, near, far, right, other),
        [scalars()] + [VMEM] * 4,
        VMEM,
        [],
        2 * tokens * width * hidden,
        12 << 20,
        behind,
        limit=24,
    )


def own_rows(core, near_ref, far_ref, turned):
    chips, unused, rows, both = turned.shape
    tokens = near_ref.shape[0]
    turned[:, :, :, :tokens] = near_ref[...].T.reshape(chips, 2, rows, tokens)
    turned[:, :, :, tokens:] = far_ref[...].T.reshape(chips, 2, rows, tokens)
    return turned[:, pl.ds(core, 1)].reshape(chips * rows, both)


def own_columns_grad(left, right_ref, other_ref, cut):
    right = jnp.concatenate([right_ref[:, cut], other_ref[:, cut]], axis=0)
    return dot(left, right).astype(BF16)


def expand_grad_kernel(core_ref, near_ref, far_ref, right_ref, other_ref, out_ref, turned):
    chips, rows, columns = out_ref.shape
    left = own_rows(core_ref[0], near_ref, far_ref, turned)
    step = 512
    for at in range(0, columns, step):
        cut = slice(at, at + step)
        out_ref[:, :, cut] = own_columns_grad(left, right_ref, other_ref, cut).reshape(chips, rows, step)


def turned_scratch(tokens, width):
    return pltpu.VMEM((PAIRS, 2, width // HEADS, 2 * tokens), BF16)


def expand_grad(core, near, far, right, other, behind):
    tokens, width = near.shape
    hidden = right.shape[1]
    return call(
        expand_grad_kernel,
        array((PAIRS, width // HEADS, hidden), BF16),
        (core, near, far, right, other),
        [scalars()] + [VMEM] * 4,
        VMEM,
        [turned_scratch(tokens, width)],
        2 * tokens * width * hidden,
        12 << 20,
        behind=behind,
        limit=24,
    )


def project_grad_kernel(core_ref, a_ref, a_far, packed_ref, packed_far, o_ref, o_far, gat_ref, gat_far, vec_ref, vec_far, out_ref, turned):
    chips, unused, width = out_ref.shape
    rows = width // HEADS
    core = core_ref[0]
    step = 512
    left = own_rows(core, a_ref, a_far, turned)
    for third in range(3):
        for at in range(0, width, step):
            result = own_columns_grad(left, packed_ref, packed_far, slice(third * width + at, third * width + at + step))
            out_ref[:, third * rows : (third + 1) * rows, at : at + step] = result.reshape(chips, rows, step)
    left = own_rows(core, o_ref, o_far, turned)
    for at in range(0, width, step):
        result = own_columns_grad(left, gat_ref, gat_far, slice(at, at + step))
        out_ref[:, 3 * rows : 4 * rows, at : at + step] = result.reshape(chips, rows, step)
    total = vec_ref[...] + vec_far[...]
    for chip in range(chips):
        pair = total[:, chip * 2 * rows : (chip + 1) * 2 * rows]
        turn = jnp.concatenate([pair[:, rows:], pair[:, :rows]], axis=1)
        own = jnp.where(core == 0, pair, turn)
        out_ref[chip, 4 * rows :, : 2 * rows] = own.astype(BF16)
        out_ref[chip, 4 * rows :, 2 * rows :] = jnp.zeros((own.shape[0], width - 2 * rows), BF16)


def project_grad(core, operands, behind):
    tokens, width = operands[0].shape
    rows = width // HEADS
    return call(
        project_grad_kernel,
        array((PAIRS, 4 * rows + 16, width), BF16),
        (core, *operands),
        [scalars()] + [VMEM] * len(operands),
        VMEM,
        [turned_scratch(tokens, width)],
        8 * tokens * width * width,
        12 << 20,
        behind=behind,
        limit=24,
    )


DECAY = 1.0 - STEP ** (-0.8)
LANES = 128


def sums_at(cuts, columns):
    lines = sum(blocks for first, rows, blocks in cuts) * columns // LANES
    return lines, 2 * lines, 2 * lines + 8


def turned_row(row):
    return jnp.sum(jnp.where(diagonal(row.shape[1]), row, 0.0), axis=1, keepdims=True)


def turned_column(column):
    return jnp.sum(jnp.where(diagonal(column.shape[0]), column, 0.0), axis=0, keepdims=True)


def diagonal(count):
    rows = lax.broadcasted_iota(jnp.int32, (count, count), 0)
    return rows == lax.broadcasted_iota(jnp.int32, (count, count), 1)


def finish_kernel(addends, cuts, with_vectors, *refs):
    parts = len(cuts)
    refs = list(refs)

    def take(count):
        taken = refs[:count]
        del refs[:count]
        return taken

    if addends > 1:
        (chips_ref, blocks), addend_refs = take(2), take(addends - 1)
    else:
        addend_refs = take(1)
    old_refs = take(parts)
    moment_refs = take(int(with_vectors))
    grad_refs, row_refs, over_refs = take(parts), take(parts), take(parts)
    vector_refs = take(2 * int(with_vectors))
    (sums_ref,) = take(1)
    if addends > 1:
        own, sems = refs
        for copy in fetch([(blocks.at[chips_ref[0]], own)], sems):
            copy.wait()
        addend_refs.append(own)
    columns = addend_refs[0].shape[1]
    norms, totals, vector_line = sums_at(cuts, columns)

    def sum_of(rows, cut):
        total = None
        for ref in addend_refs:
            value = ref[rows, cut].astype(F32)
            total = value if total is None else total + value
        return total

    sums_ref[totals : totals + 8] = jnp.zeros((8, LANES), F32)
    line = 0
    for part, (first, rows, blocks) in enumerate(cuts):
        row_sum = None
        for block in range(blocks):
            grad = sum_of(slice(first + block * rows, first + (block + 1) * rows), ALL)
            cut = slice(block * columns, (block + 1) * columns)
            grad_refs[part][:, cut] = grad
            square = grad * grad + 1e-30
            block_sum = jnp.sum(square, axis=1, keepdims=True)
            row_sum = block_sum if row_sum is None else row_sum + block_sum
            column_sum = jnp.sum(square, axis=0, keepdims=True)
            for at in range(columns // LANES):
                to = line + block * columns // LANES + at
                sums_ref[to : to + 1] = column_sum[:, at * LANES : (at + 1) * LANES]
        row_stat = DECAY * turned_row(old_refs[part][...]) + (1.0 - DECAY) * (row_sum / (blocks * columns))
        row_refs[part][...] = turned_column(row_stat)
        root = lax.rsqrt(row_stat)
        for block in range(blocks):
            grad = grad_refs[part][:, block * columns : (block + 1) * columns]
            over = grad * root
            over_refs[part][:, block * columns : (block + 1) * columns] = over
            column_sum = jnp.sum(over * over, axis=0, keepdims=True)
            for at in range(columns // LANES):
                to = norms + line + block * columns // LANES + at
                sums_ref[to : to + 1] = column_sum[:, at * LANES : (at + 1) * LANES]
        line += blocks * columns // LANES
        total = jnp.sum(row_stat, axis=0, keepdims=True)
        sums_ref[totals + part : totals + part + 1] = jnp.broadcast_to(total, (1, LANES))
    if with_vectors:
        last = cuts[-1][0] + cuts[-1][1] * cuts[-1][2]
        moment = moment_refs[0][...]
        count, wide = moment.shape
        grad = sum_of(slice(last, last + 16), slice(0, LANES))[:count, :wide]
        second = DECAY * moment + (1.0 - DECAY) * (grad * grad + 1e-30)
        vector_refs[0][...] = grad
        vector_refs[1][...] = second
        move = grad * lax.rsqrt(second)
        norm = jnp.sum(move * move, axis=1, keepdims=True)
        sums_ref[vector_line:] = jnp.zeros((16, LANES), F32)
        sums_ref[vector_line : vector_line + count] = jnp.broadcast_to(norm, (count, LANES))


def finish(parts, olds, cuts, moment, here, behind=()):
    columns = parts[-1].shape[1]
    rows = parts[-1].shape[0]
    outs = [array((count, blocks * columns), F32) for first, count, blocks in cuts]
    outs += [array((1, count), F32) for first, count, blocks in cuts]
    outs += outs[: len(cuts)]
    vectors = () if moment is None else (moment,)
    outs += [array(value.shape, F32) for value in vectors for unused in range(2)]
    outs += [array((sums_at(cuts, columns)[2] + 16 * len(vectors), LANES), F32)]
    args, specs, scratch = list(parts), [VMEM] * len(parts), []
    if len(parts) > 1:
        args, specs = [here.table, *parts], [scalars(), HBM] + [VMEM] * (len(parts) - 1)
        scratch = [pltpu.VMEM((rows, columns), parts[0].dtype), pltpu.SemaphoreType.DMA((1,))]
    args += list(olds) + list(vectors)
    specs += [VMEM] * (len(olds) + len(vectors))
    return call(
        functools.partial(finish_kernel, len(parts), cuts, bool(vectors)),
        tuple(outs),
        tuple(args),
        specs,
        (VMEM,) * len(outs),
        scratch,
        8 * rows * columns,
        8 * rows * columns,
        behind,
        16,
    )


def update_kernel(chunks, full_rows, *refs):
    refs = list(refs)

    def take(count):
        taken = refs[:count]
        del refs[:count]
        return taken

    operands = []
    for cuts, columns, with_vectors in chunks:
        operands.append([take(len(cuts)) for unused in range(3)] + [take(3 * int(with_vectors))])
    (sums_ref,) = take(1)
    base = 0
    for (cuts, columns, with_vectors), operand in zip(chunks, operands):
        over_refs, master_refs, old_refs, vector_refs = operand
        updated_refs, column_refs = take(len(cuts)), take(len(cuts))
        norms, totals, vector_line = sums_at(cuts, columns)

        def lanes(start, count):
            return jnp.concatenate([sums_ref[start + at : start + at + 1] for at in range(count)], axis=1)

        line = base
        for part, (first, rows, blocks) in enumerate(cuts):
            wide = blocks * columns
            lines = wide // LANES
            square, weighted = lanes(line, lines), lanes(norms + line, lines)
            line += lines
            count = full_rows[rows]
            row_mean = sums_ref[base + totals + part : base + totals + part + 1, 0:1] / count
            col_stat = DECAY * old_refs[part][...] + (1.0 - DECAY) * (square / count)
            column_refs[part][...] = col_stat
            norm = row_mean * jnp.sum(weighted / col_stat, axis=1, keepdims=True)
            scale = jnp.sqrt(norm / (count * wide))
            rate = jnp.sqrt(row_mean) * (RATE / jnp.maximum(1.0, scale))
            updated_refs[part][...] = master_refs[part][...] - over_refs[part][...] * (rate * lax.rsqrt(col_stat))
        if with_vectors:
            grad_ref, second_ref, vectors_ref = vector_refs
            count = grad_ref.shape[0]
            norm = sums_ref[base + vector_line : base + vector_line + count, 0:1]
            scale = jnp.sqrt(norm / columns)
            move = grad_ref[...] * lax.rsqrt(second_ref[...])
            (updated_ref,) = take(1)
            updated_ref[...] = vectors_ref[...] - VECTOR_RATE * move / jnp.maximum(1.0, scale)
        base += vector_line + 16 * int(with_vectors)


def update(chunks, operands, sums, size):
    outs, args = [], []
    for grads, masters, olds, vectors in operands:
        outs += [array(grad.shape, F32) for grad in grads]
        outs += [array((1, grad.shape[1]), F32) for grad in grads]
        outs += [array(value.shape, F32) for value in vectors[2:]]
        args += [*grads, *masters, *olds, *vectors]
    full_rows = {grad.shape[0]: grad.shape[0] * size for operand in operands for grad in operand[0]}
    results = call(
        functools.partial(update_kernel, chunks, full_rows),
        tuple(outs),
        (*args, sums),
        [VMEM] * (len(args) + 1),
        (VMEM,) * len(outs),
        [],
        8 << 20,
        10 << 20,
        limit=24,
    )
    split = []
    for grads, masters, olds, vectors in operands:
        count = 2 * len(grads) + len(vectors[2:])
        split.append(results[:count])
        results = results[count:]
    return split


class Place:
    def __init__(self):
        self.size = lax.axis_size("dp")
        self.chips = self.size // 2
        self.ring = list(range(0, self.chips, 2)) + list(range(self.chips - 1, 0, -2))
        self.small = self.size == HEADS
        index = lax.axis_index("dp")
        self.chip = index // 2
        self.core = index % 2 if self.small else jnp.zeros_like(index)
        where = [0] * self.chips
        for place, chip in enumerate(self.ring):
            where[chip] = place
        tables = [
            [self.ring[(where[chip] + offset) % self.chips] for offset in range(self.chips)]
            for chip in range(self.chips)
        ]
        self.table = lax.dynamic_index_in_dim(
            jnp.array(tables, jnp.int32), self.chip, 0, keepdims=False
        )

    def permute(self, array, target):
        pairs = []
        for chip in range(self.chips):
            for core in range(2):
                to_chip, to_core = target(chip, core)
                pairs.append((chip * 2 + core, to_chip * 2 + to_core))
        return lax.ppermute(array, "dp", pairs)

    def shift(self, array, by):
        where = {chip: place for place, chip in enumerate(self.ring)}
        return self.permute(
            array, lambda chip, core: (self.ring[(where[chip] + by) % self.chips], core)
        )

    def swap(self, array):
        return self.permute(array, lambda chip, core: (chip, 1 - core))

    def cross(self, array, mask):
        return self.permute(array, lambda chip, core: (chip ^ mask, core))

    def masks(self):
        return [1 << bit for bit in range(self.chips.bit_length() - 1)]


def section_shift(array, by):
    size = lax.axis_size("section")
    pairs = [(i, i + by) for i in range(size) if 0 <= i + by < size]
    return lax.ppermute(array, "section", pairs)


def upper_rows(rows):
    return (rows // 2 + 15) // 16 * 16


def gate_kernel():
    pass


def gated(arrays, behind):
    return call(gate_kernel, (), (), [], (), [], 0, 1 << 10, behind, passing=arrays)[1]


class RingGather:
    def __init__(self, own, here):
        self.here = here
        self.rows, self.columns = own.shape
        self.pieces = [(0, 0, own)]
        self.ahead = self.behind = own
        self.step = 0
        self.round()

    def round(self, behind=(), passing=()):
        here = self.here
        self.step += 1
        if behind or passing:
            self.ahead, self.behind, *passing = gated((self.ahead, self.behind, *passing), behind)
            if self.step > 1:
                self.pieces[-2:] = [
                    (1 - self.step, 0, self.ahead),
                    (self.step - 1, 0, self.behind),
                ]
        if self.step < here.chips // 2:
            self.ahead = here.shift(self.ahead, 1)
            self.behind = here.shift(self.behind, -1)
            self.pieces += [(-self.step, 0, self.ahead), (self.step, 0, self.behind)]
        else:
            cut = upper_rows(self.rows)
            self.ahead = here.shift(self.ahead[:cut], 1)
            self.behind = here.shift(self.behind[cut:], -1)
            self.pieces += [(self.step, 0, self.ahead), (self.step, cut, self.behind)]
        return passing

    def heads(self):
        return self.ahead, self.behind


def placed(rings, here, behind=()):
    plan, arrays, base = [], [], 0
    for ring in rings:
        for offset, row, piece in ring.pieces:
            plan.append((offset % here.chips, base + row))
            arrays.append(piece)
        base += ring.rows
    columns = arrays[0].shape[1]
    return call(
        functools.partial(place_kernel, tuple(plan)),
        array((here.chips, base, columns), arrays[0].dtype),
        (here.table, *arrays),
        [scalars()] + [HBM] * len(arrays),
        VMEM,
        [pltpu.SemaphoreType.DMA((len(arrays),))],
        0,
        4 * here.chips * base * columns,
        behind,
        56 if len(rings) == 1 else 30,
    )


def place_kernel(plan, chips_ref, *refs):
    out, sems = refs[-2:]
    pairs = []
    for piece, (place, row) in zip(refs, plan):
        pairs.append((piece, out.at[chips_ref[place], pl.ds(row, piece.shape[0])]))
    for copy in fetch(pairs, sems):
        copy.wait()


def pack_kernel(project_hbm, merge_hbm, vectors_ref, expand_hbm, out_ref, expand_out, project_ref, merge_ref, expand_ref, sems):
    copies = fetch([(project_hbm, project_ref), (merge_hbm, merge_ref), (expand_hbm, expand_ref)], sems)
    rows, width = merge_ref.shape
    count, wide = vectors_ref.shape
    vectors = jnp.concatenate([vectors_ref[...], jnp.zeros((16 - count, wide), F32)], axis=0)
    out_ref[4 * rows :] = jnp.concatenate(
        [vectors.astype(BF16), jnp.zeros((16, width - wide), BF16)], axis=1
    )
    copies[0].wait()
    for third in range(3):
        out_ref[third * rows : (third + 1) * rows] = project_ref[:, third * width : (third + 1) * width].astype(BF16)
    copies[1].wait()
    out_ref[3 * rows : 4 * rows] = merge_ref[...].astype(BF16)
    copies[2].wait()
    expand_out[...] = expand_ref[...].astype(BF16)


def pack_rows(project, merge, vectors, expand):
    rows, width = merge.shape
    return call(
        pack_kernel,
        (array((4 * rows + 16, width), BF16), array(expand.shape, BF16)),
        (project, merge, vectors, expand),
        [HBM, HBM, VMEM, HBM],
        (VMEM, VMEM),
        [pltpu.VMEM(part.shape, F32) for part in (project, merge, expand)] + [pltpu.SemaphoreType.DMA((3,))],
        0,
        2 << 20,
        limit=56,
    )


def half_kernel(side, whole_ref, out_ref):
    rows = out_ref.shape[0]
    out_ref[...] = whole_ref[side * rows : (side + 1) * rows].astype(BF16)


def half_of(whole, side, behind):
    half = array((whole.shape[0] // 2, whole.shape[1]), BF16)
    return call(functools.partial(half_kernel, side), half, (whole,), [VMEM], VMEM, [], 0, 2 << 20, behind)


def vectors_of(near, far, core, wide):
    cuts = [part[:, -16:, :wide] for part in (near, far)]
    rows = jnp.where(core == 0, jnp.stack(cuts), jnp.stack(cuts[::-1]))
    return rows.transpose(2, 1, 0, 3).reshape(16, -1).astype(F32)


def gather_plainly(project, merge, expand, shrink, vectors):
    width = merge.shape[1]

    def whole_of_rows(rows):
        whole = lax.all_gather(rows.astype(BF16), "dp", axis=0, tiled=True)
        return whole.reshape(PAIRS, 2, -1, whole.shape[1])

    parts = [whole_of_rows(project[:, at * width : (at + 1) * width]) for at in range(3)]
    cuts = [jnp.concatenate([*parts, whole_of_rows(merge)], axis=2)]
    cuts += [whole_of_rows(expand), whole_of_rows(shrink)]
    rows = lax.all_gather(vectors.astype(BF16), "dp", axis=1, tiled=True)
    rows = jnp.pad(rows, ((0, 16 - vectors.shape[0]), (0, 0)))
    return *((cut[:, 0], cut[:, 1]) for cut in cuts), rows.astype(F32)


def far_kernel(half, chips_ref, blocks, upper_ref, lower_ref, sems):
    cut = upper_ref.shape[0]
    chip = chips_ref[half]
    pairs = [
        (blocks.at[chip, pl.ds(0, cut)], upper_ref),
        (blocks.at[chip, pl.ds(cut, lower_ref.shape[0])], lower_ref),
    ]
    for copy in fetch(pairs, sems):
        copy.wait()


def add_kernel(ahead_at, behind_at, chips_ref, blocks, ahead_got, behind_got, ahead_out, behind_out, ahead_ref, behind_ref, sems):
    pairs = [
        (blocks.at[chips_ref[ahead_at]], ahead_out),
        (blocks.at[chips_ref[behind_at]], behind_out),
        (ahead_got, ahead_ref),
        (behind_got, behind_ref),
    ]
    for copy in fetch(pairs, sems):
        copy.wait()
    rows = behind_out.shape[0]
    for got, out, cut in (
        (ahead_ref, ahead_out, pl.ds(0, ahead_ref.shape[0])),
        (behind_ref, behind_out, pl.ds(rows - behind_ref.shape[0], behind_ref.shape[0])),
    ):
        out[cut] = (out[cut].astype(F32) + got[...].astype(F32)).astype(BF16)


class RingSum:
    def __init__(self, blocks, here):
        self.blocks = blocks
        self.here = here
        self.step = here.chips // 2
        self.sent = None

    def round(self, *behind, passing=()):
        here, blocks, step = self.here, self.blocks, self.step
        rows, columns = blocks.shape[1:]
        if self.sent is None:
            cut = upper_rows(rows)
            payload = call(
                functools.partial(far_kernel, step),
                (array((cut, columns), BF16), array((rows - cut, columns), BF16)),
                (here.table, blocks),
                [scalars(), HBM],
                (VMEM, VMEM),
                [pltpu.SemaphoreType.DMA((2,))],
                0,
                4 * rows * columns,
                behind,
            )
        else:
            whole = array((rows, columns), BF16)
            payload = call(
                functools.partial(add_kernel, step, here.chips - step),
                (whole, whole),
                (here.table, blocks, *self.sent),
                [scalars(), HBM, HBM, HBM],
                (VMEM, VMEM),
                [pltpu.VMEM(part.shape, BF16) for part in self.sent] + [pltpu.SemaphoreType.DMA((4,))],
                2 * rows * columns,
                12 * rows * columns,
                behind,
                passing=passing,
            )
            if passing:
                payload, passing = payload
        self.step -= 1
        self.sent = (here.shift(payload[0], 1), here.shift(payload[1], -1))
        return (payload[0], *passing)

    def parts(self):
        return (self.blocks, *self.sent)


def small_sum(vector, here):
    if not here.small:
        return lax.psum(vector, "dp")
    vector = vector + here.swap(vector)
    near = [here.cross(vector, mask) for mask in (1, 2, 3)]
    vector = (vector + near[0]) + (near[1] + near[2])
    for mask in here.masks()[2:]:
        vector = vector + here.cross(vector, mask)
    return vector


def segments(lengths_row, count):
    ends = jnp.cumsum(lengths_row)
    places = jnp.arange(count, dtype=jnp.int32)
    return jnp.sum((places[:, None] >= ends[None, :]).astype(jnp.int32), axis=1)


def per_device(
    frames,
    lengths,
    cotangent,
    project_weight,
    merge_weight,
    expand_weight,
    shrink_weight,
    vectors,
    project_row,
    project_col,
    merge_row,
    merge_col,
    expand_row,
    expand_col,
    shrink_row,
    shrink_col,
    vector_moment,
):
    here = Place()
    core = here.core.reshape(1)
    is_first = lax.axis_index("section") == 0
    micro = lengths.shape[0]
    count, width = frames.shape
    block = count // micro
    segment = jax.vmap(lambda lengths_row: segments(lengths_row, block))(lengths)
    live = (segment < UTTS).astype(F32).reshape(count, 1)
    visible = (segment[:, :, None] == segment[:, None, :]).astype(F32)

    masters = (project_weight[0], merge_weight[0], expand_weight[0], shrink_weight[0])
    first = is_first.astype(jnp.int32).reshape(1)
    if here.small:
        pm_rows, e_rows = pack_rows(masters[0], masters[1], vectors[0], masters[2])
        pm_ring, e_ring = RingGather(pm_rows, here), RingGather(e_rows, here)
        pm_ring.round()
        pm_ring.round(e_ring.heads())
        e_ring.round()
        upper_ring = RingGather(half_of(masters[3], 0, pm_ring.heads()), here)
        pm_ring.round(e_ring.heads())
        e_ring.round()
        lower_ring = RingGather(half_of(masters[3], 1, e_ring.heads()), here)
        e_ring.round(upper_ring.heads())
        upper_ring.round()
        upper_ring.round(lower_ring.heads())
        lower_ring.round()
        upper_ring.round(lower_ring.heads())
        lower_ring.round()
        lower_ring.round()
        near = placed([pm_ring], here)
        pm = (near, here.swap(near))
        vec = vectors_of(*pm, here.core, vectors.shape[2])
        near = placed([e_ring], here)
        e = (near, here.swap(near))
        near = placed([upper_ring, lower_ring], here)
        s = (near, here.swap(near))
        kept = attend_block(core, frames, visible, vec, pm, (near,))
        hidden, slope = expand_block(core, kept[-1], vec, e)
    else:
        pm, e, s, vec = gather_plainly(*masters, vectors[0])
        kept = attend_block(core, frames, visible, vec, pm)
        hidden, slope = expand_block(core, kept[-1], vec, e)

    unused, low = shrink_block(core, kept[3], hidden, vec, s)
    start = jnp.where(is_first, frames, section_shift(low, 1))
    kept = attend_block(core, start, visible, vec, pm)
    normed, packed, mixed, middle, normed_two = kept
    hidden, slope = expand_block(core, normed_two, vec, e)

    incoming, unused = incoming_grad(jnp.zeros((1,), jnp.int32), frames, cotangent, live, ())
    unused, unused, back_middle, back_branch, sums_two, sums_up = back_hidden_block(
        core, incoming, middle, vec, s, e, slope, ()
    )
    unused, unused, low, unused = back_attend_block(
        core, first, start, back_middle, back_branch, packed, visible, vec, sums_two, sums_up, pm, ()
    )
    output, unused = shrink_block(core, middle, hidden, vec, s, (low,))
    incoming, low_incoming = incoming_grad(first, section_shift(low, -1), cotangent, live, (output,))
    swap = here.swap if here.small else lambda rows: rows

    shared = [swap(rows) for rows in (hidden, normed_two, normed, mixed)]
    behind = ()
    if here.small:
        shrink_ring = RingSum(
            shrink_grad(core, hidden, shared[0], low_incoming, swap(low_incoming), shared[1:]), here
        )
        shrink_ring.round()
        behind = shrink_ring.round()
    low_out, back_pre, back_middle, back_branch, sums_two, sums_up = back_hidden_block(
        core, incoming, middle, vec, s, e, slope, behind
    )
    if here.small:
        last, back_pre, back_branch = shrink_ring.round(passing=(back_pre, back_branch))
        behind = (last,)
    back_packed, back_inputs, low, vector_sums = back_attend_block(
        core, first, start, back_middle, back_branch, packed, visible, vec, sums_two, sums_up, pm, behind
    )
    layer_outputs = output[None]
    input_grads = back_inputs[None]

    rows = masters[0].shape[0]
    shrink_cuts = ((0, masters[3].shape[0], 1),)
    expand_cuts = ((0, rows, 1),)
    both_cuts = ((0, rows, 3), (3 * rows, rows, 1))
    shrink_olds, expand_olds = (shrink_row,), (expand_row,)
    both_olds = (project_row, merge_row)
    moment = vector_moment[0]
    if here.small:
        last, back_packed, vector_sums = shrink_ring.round(passing=(back_packed, vector_sums))
        expand_ring = RingSum(
            expand_grad(core, normed_two, shared[1], back_pre, swap(back_pre), (last,)), here
        )
        (last,) = expand_ring.round()
        both_ring = RingSum(
            project_grad(
                core,
                (
                    normed,
                    shared[2],
                    back_packed,
                    swap(back_packed),
                    mixed,
                    shared[3],
                    back_branch,
                    swap(back_branch),
                    vector_sums,
                    swap(vector_sums),
                ),
                (last,),
            ),
            here,
        )
        (last,) = both_ring.round()
        (last,) = expand_ring.round(last)
        shrink_ends = finish(shrink_ring.parts(), shrink_olds, shrink_cuts, None, here, (last,))
        (last,) = both_ring.round(shrink_ends[0])
        (last,) = expand_ring.round(last)
        (last,) = both_ring.round(last)
        (last,) = expand_ring.round(last)
        (last,) = both_ring.round(last)
        expand_ends = finish(expand_ring.parts(), expand_olds, expand_cuts, None, here, (last,))
        both_parts = both_ring.parts()
    else:

        def total(left, right):
            whole = dot_first(left, right).astype(BF16)
            return lax.psum_scatter(whole, "dp", scatter_dimension=0, tiled=True).astype(F32)

        shrink_ends = finish((total(hidden, low_out),), shrink_olds, shrink_cuts, None, here)
        expand_ends = finish((total(normed_two, back_pre),), expand_olds, expand_cuts, None, here)
        thirds = [total(normed, back_packed[:, at * width : (at + 1) * width]) for at in range(3)]
        vector_rows = lax.psum_scatter(vector_sums, "dp", scatter_dimension=1, tiled=True)
        vector_rows = jnp.pad(vector_rows, ((0, 0), (0, width - vector_rows.shape[1])))
        both_parts = (jnp.concatenate([*thirds, total(mixed, back_branch), vector_rows], axis=0),)
        last = vector_sums

    both_ends = finish(both_parts, both_olds, both_cuts, moment, here)
    ends = (shrink_ends, expand_ends, both_ends)
    sums = small_sum(jnp.concatenate([end[-1] for end in ends], axis=0), here)
    chunks = ((shrink_cuts, width, False), (expand_cuts, 4 * width, False), (both_cuts, width, True))
    matrices = (masters[3:], masters[2:3], masters[:2])
    cols_old = ((shrink_col,), (expand_col,), (project_col, merge_col))
    operands = []
    for (cuts, columns, with_vectors), end, masters_own, olds in zip(chunks, ends, matrices, cols_old):
        count = len(cuts)
        values = (*end[3 * count : -1], vectors[0]) if with_vectors else ()
        operands.append((end[2 * count : 3 * count], masters_own, olds, values))
    outs = []
    for end, operand, results in zip(ends, operands, update(chunks, operands, sums, here.size)):
        count, values = len(operand[0]), operand[-1]
        own = []
        for part in range(count):
            own += [end[part][None], end[count + part], results[count + part], results[part][None]]
        outs.append(own)
        vector_outs = (*values[:2], *results[2 * count :])
    shrink_outs, expand_outs, both_outs = outs
    return (
        layer_outputs,
        input_grads,
        *both_outs,
        *expand_outs,
        *shrink_outs,
        *(rows[None] for rows in vector_outs),
    )


def solution(mesh):
    placed = (
        P("dp", None),
        P("dp", None),
        P("dp", None),
        P("section", "dp", None),
        P("section", "dp", None),
        P("section", "dp", None),
        P("section", "dp", None),
        P("section", None, "dp"),
        P("section", "dp"),
        P("section", None),
        P("section", "dp"),
        P("section", None),
        P("section", "dp"),
        P("section", None),
        P("section", "dp"),
        P("section", None),
        P("section", None, "dp"),
    )
    matrix = (
        P("section", "dp", None),
        P("section", "dp"),
        P("section", None),
        P("section", "dp", None),
    )
    return jax.shard_map(
        per_device,
        mesh=mesh,
        in_specs=placed,
        out_specs=(
            P("section", "dp", None),
            P("section", "dp", None),
            *matrix,
            *matrix,
            *matrix,
            *matrix,
            P("section", None, "dp"),
            P("section", None, "dp"),
            P("section", None, "dp"),
        ),
        check_vma=False,
    )
```

```python
import functools
import math

import jax
import jax.numpy as jnp
from jax import lax
from jax.experimental import pallas as pl
from jax.experimental.pallas import tpu as pltpu
from jax.sharding import PartitionSpec as P

HEADS = 16
HEAD_DIM = 64
PAIRS = HEADS // 2
UTTS = 3
STEP = 10

EPSILON = 1e-05
RATE = 0.04
VECTOR_RATE = 0.25
MASKED = -1e30
BF16 = jnp.bfloat16
F32 = jnp.float32
VMEM = pl.BlockSpec(memory_space=pltpu.VMEM)
HBM = pl.BlockSpec(memory_space=pl.ANY)
MIB = 1024 * 1024


def dot(left, right):
    return lax.dot_general(left, right, (((1,), (0,)), ((), ())), preferred_element_type=F32)


def dot_last(left, right):
    return lax.dot_general(left, right, (((1,), (1,)), ((), ())), preferred_element_type=F32)


def dot_first(left, right):
    return lax.dot_general(left, right, (((0,), (0,)), ((), ())), preferred_element_type=F32)


def moments(values):
    centred = values - jnp.mean(values, axis=-1, keepdims=True)
    spread = jnp.mean(centred * centred, axis=-1, keepdims=True)
    scale = lax.rsqrt(spread + EPSILON)
    return centred * scale, scale


def norm_back(grad, unit, scale, gain):
    inner = grad * gain
    first = jnp.mean(inner, axis=-1, keepdims=True)
    second = jnp.mean(inner * unit, axis=-1, keepdims=True)
    return scale * (inner - first - unit * second)


def fetch(pairs, sems):
    copies = [
        pltpu.make_async_copy(source, target, sems.at[index])
        for index, (source, target) in enumerate(pairs)
    ]
    for copy in copies:
        copy.start()
    return copies


def half_masks():
    lane = lax.broadcasted_iota(jnp.int32, (1, 128), 1)
    low = jnp.where(lane < HEAD_DIM, 1.0, 0.0)
    return low.astype(BF16), (1.0 - low).astype(BF16)


def two_heads(tile, masks):
    return jnp.concatenate([tile * masks[0], tile * masks[1]], axis=0)


def side_by_side(both):
    half = both.shape[0] // 2
    return jnp.concatenate([both[:half], both[half:]], axis=1)


def weights_of(scores, visible):
    scores = jnp.where(visible, scores * HEAD_DIM**-0.5, MASKED)
    shifted = jnp.exp(scores - jnp.max(scores, axis=-1, keepdims=True))
    return shifted / jnp.sum(shifted, axis=-1, keepdims=True)


def scalars():
    return pl.BlockSpec(memory_space=pltpu.SMEM)


def array(shape, kind):
    return jax.ShapeDtypeStruct(shape, kind)


def call(kernel, outs, args, in_specs, out_specs, scratch, flops, size, behind=(), limit=12, passing=()):
    given, skipped = len(args), len(behind) + len(passing)
    single = not isinstance(outs, tuple)
    results = (outs,) if single else outs
    result_specs = (out_specs,) if single else out_specs
    count = len(results)

    def body(*refs):
        kernel(*refs[:given], *refs[given + skipped :][:count], *refs[given + skipped + count + len(passing) :])

    returned = pl.pallas_call(
        body,
        out_shape=(*results, *(array(value.shape, value.dtype) for value in passing)),
        in_specs=[
            *in_specs,
            *(HBM for unused in range(skipped)),
        ],
        out_specs=(*result_specs, *(HBM for unused in passing)),
        scratch_shapes=scratch,
        input_output_aliases={given + len(behind) + at: count + at for at in range(len(passing))},
        compiler_params=pltpu.CompilerParams(vmem_limit_bytes=limit * MIB),
        cost_estimate=pl.CostEstimate(flops=flops, bytes_accessed=size, transcendentals=0),
    )(*args, *behind, *passing)
    own = returned[0] if single else tuple(returned[:count])
    return (own, tuple(returned[count:])) if passing else own


def both_cores(core, near, far, whole, cuts):
    pairs = []
    for cut in cuts:
        pairs.append((near.at[cut], whole.at[cut[0], core, *cut[1:]]))
        pairs.append((far.at[cut], whole.at[cut[0], 1 - core, *cut[1:]]))
    return pairs


ALL = slice(None)


def quarters_of(core, near, far, whole, order):
    rows = whole.shape[3]
    pairs = []
    for at in order:
        pairs.append((near.at[:, pl.ds(at * rows, rows)], whole.at[at, :, core]))
        pairs.append((far.at[:, pl.ds(at * rows, rows)], whole.at[at, :, 1 - core]))
    return pairs


def quarters_scratch(width):
    return pltpu.VMEM((4, PAIRS, 2, width // HEADS, width), BF16)


def columns_cut(start, size):
    return (ALL, ALL, pl.ds(start, size))


def attend_kernel(core_ref, x_ref, mask_ref, vec_ref, near, far, a_ref, packed_ref, o_ref, x1_ref, c_ref, w, sems):
    count, width = x_ref.shape
    block = mask_ref.shape[1]
    step = 512
    copies = fetch(quarters_of(core_ref[0], near, far, w, range(4)), sems)
    unit, unused = moments(x_ref[...].astype(F32))
    a_ref[...] = (unit * vec_ref[0:1] + vec_ref[1:2]).astype(BF16)
    for third in range(3):
        copies[2 * third].wait()
        copies[2 * third + 1].wait()
        for cut in range(width // step):
            at = third * width + cut * step
            matrix = w[third, :, :, :, cut * step : (cut + 1) * step].reshape(width, step)
            result = dot(a_ref[...], matrix)
            if third != 1:
                row = 2 if third == 0 else 3
                result = result + vec_ref[row : row + 1, cut * step : (cut + 1) * step]
            packed_ref[:, at : at + step] = result.astype(BF16)
    masks = half_masks()
    for micro in range(count // block):
        rows = slice(micro * block, (micro + 1) * block)
        visible = mask_ref[micro] > 0.0
        visible = jnp.concatenate([visible, visible], axis=0)
        for at in range(0, width, 128):
            queries = packed_ref[rows, at : at + 128]
            keys = packed_ref[rows, at + width : at + width + 128]
            values = packed_ref[rows, at + 2 * width : at + 2 * width + 128]
            attend = weights_of(dot_last(two_heads(queries, masks), keys), visible).astype(BF16)
            mixed = dot(side_by_side(attend), two_heads(values, masks))
            o_ref[rows, at : at + 128] = mixed.astype(BF16)
    copies[6].wait()
    copies[7].wait()
    for at in range(0, width, step):
        cut = slice(at, at + step)
        matrix = w[3, :, :, :, cut].reshape(width, step)
        x1_ref[:, cut] = x_ref[:, cut].astype(F32) + (dot(o_ref[...], matrix) + vec_ref[4:5, cut])
    unit, unused = moments(x1_ref[...])
    c_ref[...] = (unit * vec_ref[5:6] + vec_ref[6:7]).astype(BF16)


def whole_of(near):
    chips, rows, columns = near.shape
    return pltpu.VMEM((chips, 2, rows, columns), near.dtype)


def attend_block(core, x, mask, vec, pm, behind=()):
    count, width = x.shape
    low = array((count, width), BF16)
    return call(
        attend_kernel,
        (low, array((count, 3 * width), BF16), low, array((count, width), F32), low),
        (core, x, mask, vec, *pm),
        [scalars()] + [VMEM] * 3 + [HBM] * 2,
        (VMEM,) * 5,
        [quarters_scratch(width), pltpu.SemaphoreType.DMA((8,))],
        8 * count * width * width,
        20 << 20,
        behind=behind,
        limit=32,
    )


def gelu_parts(values):
    cdf = 0.5 * (1.0 + lax.erf(values * math.sqrt(0.5)))
    slope = cdf + values * jnp.exp(-0.5 * values * values) * (1.0 / math.sqrt(2.0 * math.pi))
    return values * cdf, slope


def expand_kernel(core_ref, c_ref, vec_ref, near, far, hidden_ref, slope_hbm, w, slope, sems, out_sems):
    count, width = c_ref.shape
    step = 256
    quarters = w.shape[3] // width
    copies = fetch(
        both_cores(core_ref[0], near, far, w, [columns_cut(at * width, width) for at in range(quarters)]), sems
    )
    sent = []
    for quarter in range(quarters):
        copies[2 * quarter].wait()
        copies[2 * quarter + 1].wait()
        for cut in range(width // step):
            at = quarter * width + cut * step
            result = dot(c_ref[...], w[:, :, :, at : at + step].reshape(width, step))
            bias = vec_ref[8 + quarter : 9 + quarter, cut * step : (cut + 1) * step]
            hidden, rise = gelu_parts(result + bias)
            hidden_ref[:, at : at + step] = hidden.astype(BF16)
            slope[:, at : at + step] = rise
        at = slice(quarter * width, (quarter + 1) * width)
        copy = pltpu.make_async_copy(slope.at[:, at], slope_hbm.at[:, at], out_sems.at[quarter])
        copy.start()
        sent.append(copy)
    for copy in sent:
        copy.wait()


def expand_block(core, c, vec, e):
    count, width = c.shape
    hidden = 4 * width
    return call(
        expand_kernel,
        (array((count, hidden), BF16), array((count, hidden), F32)),
        (core, c, vec, *e),
        [scalars()] + [VMEM] * 2 + [HBM] * 2,
        (VMEM, HBM),
        [
            whole_of(e[0]),
            pltpu.VMEM((count, hidden), F32),
            pltpu.SemaphoreType.DMA((8,)),
            pltpu.SemaphoreType.DMA((4,)),
        ],
        2 * count * width * hidden,
        20 << 20,
        limit=32,
    )


def shrink_kernel(core_ref, x1_ref, hidden_ref, vec_ref, near, far, y_ref, low_ref, w, sems):
    chips, unused, rows, width = w.shape
    step = 512
    group = width // (2 * rows)
    copies = fetch(
        both_cores(core_ref[0], near, far, w, [(pl.ds(at, group),) for at in range(0, chips, group)]), sems
    )
    for index in range(chips // group):
        copies[2 * index].wait()
        copies[2 * index + 1].wait()
        left = hidden_ref[:, index * width : (index + 1) * width]
        for at in range(0, width, step):
            cut = slice(at, at + step)
            matrix = w[index * group : (index + 1) * group, :, :, cut].reshape(width, step)
            result = dot(left, matrix)
            if index == 0:
                y_ref[:, cut] = x1_ref[:, cut] + result
            elif index < chips // group - 1:
                y_ref[:, cut] += result
            else:
                total = y_ref[:, cut] + result + vec_ref[7:8, cut]
                y_ref[:, cut] = total
                low_ref[:, cut] = total.astype(BF16)


def shrink_block(core, x1, hidden, vec, s, behind=()):
    count, width = x1.shape
    return call(
        shrink_kernel,
        (array((count, width), F32), array((count, width), BF16)),
        (core, x1, hidden, vec, *s),
        [scalars()] + [VMEM] * 3 + [HBM] * 2,
        (VMEM, VMEM),
        [whole_of(s[0]), pltpu.SemaphoreType.DMA((8,))],
        8 * count * width * width,
        16 << 20,
        behind=behind,
        limit=28,
    )


def back_hidden_kernel(core_ref, dy_ref, x1_ref, vec_ref, s_near, s_far, e_near, e_far, slope_hbm, gf_ref, gu_ref, dx1_ref, gat_ref, sums_ref, bias_ref, ws, we, slope, dc, sems, slope_sems):
    chips, unused, rows, width = ws.shape
    group = width // (2 * rows)
    quarters = chips // group
    core = core_ref[0]
    pairs = []
    for index in range(quarters):
        at = pl.ds(index * width, width)
        pairs += both_cores(core, s_near, s_far, ws, [(pl.ds(index * group, group),)])
        pairs.append((slope_hbm.at[:, at], slope.at[:, at]))
        pairs += both_cores(core, e_near, e_far, we, [columns_cut(index * width, width)])
    copies = fetch(pairs, sems)
    gf_ref[...] = dy_ref[...].astype(BF16)
    step = 512
    for index in range(quarters):
        for copy in copies[5 * index : 5 * index + 3]:
            copy.wait()
        for near in range(group):
            matrix = ws[index * group + near].reshape(2 * rows, width)
            at = slice(index * width + near * 2 * rows, index * width + (near + 1) * 2 * rows)
            back = (dot_last(gf_ref[...], matrix) * slope[:, at]).astype(BF16)
            gu_ref[:, at] = back
            bias_ref[:, at] = jnp.sum(back.astype(F32), axis=0, keepdims=True)
        for copy in copies[5 * index + 3 : 5 * index + 5]:
            copy.wait()
        at = slice(index * width, (index + 1) * width)
        left = gu_ref[:, at]
        for half in range(2):
            matrix = we[half * (chips // 2) : (half + 1) * (chips // 2), :, :, at].reshape(step, width)
            to = slice(half * step, (half + 1) * step)
            result = dot_last(left, matrix)
            if index == 0:
                dc[:, to] = result
            else:
                dc[:, to] += result
    unit, scale = moments(x1_ref[...])
    grad = dc[...]
    back = dy_ref[...] + norm_back(grad, unit, scale, vec_ref[5:6])
    dx1_ref[...] = back
    gat_ref[...] = back.astype(BF16)
    sums_ref[...] = jnp.zeros_like(sums_ref)
    sums_ref[0:1] = jnp.sum(grad * unit, axis=0, keepdims=True)
    sums_ref[1:2] = jnp.sum(grad, axis=0, keepdims=True)
    sums_ref[2:3] = jnp.sum(gf_ref[...].astype(F32), axis=0, keepdims=True)
    sums_ref[3:4] = jnp.sum(gat_ref[...].astype(F32), axis=0, keepdims=True)


def back_hidden_block(core, dy, x1, vec, s, e, slope, behind):
    count, width = x1.shape
    hidden = slope.shape[1]
    return call(
        back_hidden_kernel,
        (
            array((count, width), BF16),
            array((count, hidden), BF16),
            array((count, width), F32),
            array((count, width), BF16),
            array((8, width), F32),
            array((1, hidden), F32),
        ),
        (core, dy, x1, vec, *s, *e, slope),
        [scalars()] + [VMEM] * 3 + [HBM] * 5,
        (VMEM,) * 6,
        [
            whole_of(s[0]),
            whole_of(e[0]),
            pltpu.VMEM((count, hidden), F32),
            pltpu.VMEM((count, width), F32),
            pltpu.SemaphoreType.DMA((20,)),
            pltpu.SemaphoreType.DMA((4,)),
        ],
        16 * count * width * width,
        32 << 20,
        behind,
        limit=44,
    )


def back_attend_kernel(core_ref, first_ref, x_ref, dx1_ref, gat_ref, packed_ref, mask_ref, vec_ref, two_ref, up_ref, near, far, gqkv_ref, dx_ref, low_ref, sums_ref, w, go, sems):
    count, width = x_ref.shape
    block = mask_ref.shape[1]
    step = 512
    copies = fetch(quarters_of(core_ref[0], near, far, w, (3, 0, 1, 2)), sems)
    masks = half_masks()
    factor = HEAD_DIM**-0.5
    copies[0].wait()
    copies[1].wait()
    chips = w.shape[1]
    for half in range(2):
        matrix = w[3, half * (chips // 2) : (half + 1) * (chips // 2)].reshape(step, width)
        go[:, half * step : (half + 1) * step] = dot_last(gat_ref[...], matrix).astype(BF16)
    tiles = range(0, width, 128)
    for micro in range(count // block):
        rows = slice(micro * block, (micro + 1) * block)
        visible = mask_ref[micro] > 0.0
        visible = jnp.concatenate([visible, visible], axis=0)
        queries = [two_heads(packed_ref[rows, at : at + 128], masks) for at in tiles]
        keys = [packed_ref[rows, at + width : at + width + 128] for at in tiles]
        values = [packed_ref[rows, at + 2 * width : at + 2 * width + 128] for at in tiles]
        back = [two_heads(go[rows, at : at + 128], masks) for at in tiles]
        scores = [dot_last(query, key) for query, key in zip(queries, keys)]
        slopes = [dot_last(grad, value) for grad, value in zip(back, values)]
        attend = [weights_of(score, visible) for score in scores]
        low = [weight.astype(BF16) for weight in attend]
        inner = [jnp.sum(weight * slope, axis=-1, keepdims=True) for weight, slope in zip(attend, slopes)]
        scores = [
            (weight * (slope - total)).astype(BF16)
            for weight, slope, total in zip(attend, slopes, inner)
        ]
        grad_q = [dot(side_by_side(score), two_heads(key, masks)) for score, key in zip(scores, keys)]
        grad_k = [dot_first(score, query) for score, query in zip(scores, queries)]
        grad_v = [dot_first(weight, grad) for weight, grad in zip(low, back)]
        for at, one, two, three in zip(tiles, grad_q, grad_k, grad_v):
            gqkv_ref[rows, at : at + 128] = (one * factor).astype(BF16)
            gqkv_ref[rows, at + width : at + width + 128] = (two * factor).astype(BF16)
            gqkv_ref[rows, at + 2 * width : at + 2 * width + 128] = three.astype(BF16)
    for copy in copies[2:]:
        copy.wait()
    for half in range(2):
        total = None
        for third in range(3):
            matrix = w[third, half * (chips // 2) : (half + 1) * (chips // 2)].reshape(step, width)
            result = dot_last(gqkv_ref[:, third * width : (third + 1) * width], matrix)
            total = result if total is None else total + result
        dx_ref[:, half * step : (half + 1) * step] = total
    unit, scale = moments(x_ref[...].astype(F32))
    grad = dx_ref[...]
    sums_ref[...] = jnp.zeros_like(sums_ref)
    sums_ref[0:1] = jnp.sum(grad * unit, axis=0, keepdims=True)
    sums_ref[1:2] = jnp.sum(grad, axis=0, keepdims=True)
    back = dx1_ref[...] + norm_back(grad, unit, scale, vec_ref[0:1])
    low = back.astype(BF16)
    low_ref[...] = low
    dx_ref[...] = jnp.where(first_ref[0] == 1, back, low.astype(F32))
    for row, third in ((2, 0), (3, 2)):
        part = gqkv_ref[:, third * width : (third + 1) * width]
        sums_ref[row : row + 1] = jnp.sum(part.astype(F32), axis=0, keepdims=True)
    sums_ref[4:5] = two_ref[3:4]
    sums_ref[5:8] = two_ref[0:3]
    for quarter in range(4):
        sums_ref[8 + quarter : 9 + quarter] = up_ref[:, quarter * width : (quarter + 1) * width]


def back_attend_block(core, first, x, dx1, gat, packed, mask, vec, two, up, pm, behind):
    count, width = x.shape
    return call(
        back_attend_kernel,
        (
            array((count, 3 * width), BF16),
            array((count, width), F32),
            array((count, width), BF16),
            array((16, width), F32),
        ),
        (core, first, x, dx1, gat, packed, mask, vec, two, up, *pm),
        [scalars()] * 2 + [VMEM] * 8 + [HBM] * 2,
        (VMEM,) * 4,
        [quarters_scratch(width), pltpu.VMEM((count, width), BF16), pltpu.SemaphoreType.DMA((8,))],
        12 * count * width * width,
        20 << 20,
        behind,
        limit=32,
    )


def incoming_kernel(first_ref, mail_ref, cotangent_ref, live_ref, out_ref, low_ref):
    targets = cotangent_ref[...].astype(F32) * live_ref[...]
    mail = mail_ref[...].astype(F32)
    out = jnp.where(first_ref[0] == 1, mail, targets)
    out_ref[...] = out
    low_ref[...] = out.astype(BF16)


def incoming_grad(first, mail, cotangent, live, behind):
    shape = cotangent.shape
    return call(
        incoming_kernel,
        (array(shape, F32), array(shape, BF16)),
        (first, mail, cotangent, live),
        [scalars()] + [VMEM] * 3,
        (VMEM, VMEM),
        [],
        0,
        10 * cotangent.size,
        behind,
    )


def shrink_grad_kernel(core_ref, near_ref, far_ref, right_ref, other_ref, out_ref):
    chips, rows, width = out_ref.shape
    for chip in range(chips):
        at = pl.ds(pl.multiple_of((2 * chip + core_ref[0]) * rows, rows), rows)
        total = dot_first(near_ref[:, at], right_ref[...]) + dot_first(far_ref[:, at], other_ref[...])
        out_ref[chip] = total.astype(BF16)


def shrink_far_kernel(half, chips_ref, core_ref, near_ref, far_ref, right_ref, other_ref, upper_ref, lower_ref):
    cut, lower = upper_ref.shape[0], lower_ref.shape[0]
    at = (2 * chips_ref[half] + core_ref[0]) * (cut + lower)
    for start, out in ((0, upper_ref), (cut, lower_ref)):
        rows = pl.ds(pl.multiple_of(at + start, cut), out.shape[0])
        total = dot_first(near_ref[:, rows], right_ref[...]) + dot_first(far_ref[:, rows], other_ref[...])
        out[...] = total.astype(BF16)


def shrink_far(here, core, near, far, right, other, behind):
    tokens, hidden = near.shape
    width = right.shape[1]
    half = array((hidden // HEADS // 2, width), BF16)
    return call(
        functools.partial(shrink_far_kernel, here.chips // 2),
        (half, half),
        (here.table, core, near, far, right, other),
        [scalars()] * 2 + [VMEM] * 4,
        (VMEM, VMEM),
        [],
        2 * tokens * width * hidden // PAIRS,
        5 << 20,
        behind,
        24,
    )


def shrink_grad(core, near, far, right, other, behind):
    tokens, hidden = near.shape
    width = right.shape[1]
    return call(
        shrink_grad_kernel,
        array((PAIRS, hidden // HEADS, width), BF16),
        (core, near, far, right, other),
        [scalars()] + [VMEM] * 4,
        VMEM,
        [],
        2 * tokens * width * hidden,
        12 << 20,
        behind,
        limit=24,
    )


def own_rows(core, near_ref, far_ref, turned):
    chips, unused, rows, both = turned.shape
    tokens = near_ref.shape[0]
    turned[:, :, :, :tokens] = near_ref[...].T.reshape(chips, 2, rows, tokens)
    turned[:, :, :, tokens:] = far_ref[...].T.reshape(chips, 2, rows, tokens)
    return turned[:, pl.ds(core, 1)].reshape(chips * rows, both)


def own_columns_grad(left, right_ref, other_ref, cut):
    right = jnp.concatenate([right_ref[:, cut], other_ref[:, cut]], axis=0)
    return dot(left, right).astype(BF16)


def expand_grad_kernel(core_ref, near_ref, far_ref, right_ref, other_ref, out_ref, turned):
    chips, rows, columns = out_ref.shape
    left = own_rows(core_ref[0], near_ref, far_ref, turned)
    step = 512
    for at in range(0, columns, step):
        cut = slice(at, at + step)
        out_ref[:, :, cut] = own_columns_grad(left, right_ref, other_ref, cut).reshape(chips, rows, step)


def turned_scratch(tokens, width):
    return pltpu.VMEM((PAIRS, 2, width // HEADS, 2 * tokens), BF16)


def expand_grad(core, near, far, right, other, behind):
    tokens, width = near.shape
    hidden = right.shape[1]
    return call(
        expand_grad_kernel,
        array((PAIRS, width // HEADS, hidden), BF16),
        (core, near, far, right, other),
        [scalars()] + [VMEM] * 4,
        VMEM,
        [turned_scratch(tokens, width)],
        2 * tokens * width * hidden,
        12 << 20,
        behind=behind,
        limit=24,
    )


def project_grad_kernel(core_ref, a_ref, a_far, packed_ref, packed_far, o_ref, o_far, gat_ref, gat_far, vec_ref, vec_far, out_ref, turned):
    chips, unused, width = out_ref.shape
    rows = width // HEADS
    core = core_ref[0]
    step = 512
    left = own_rows(core, a_ref, a_far, turned)
    for third in range(3):
        for at in range(0, width, step):
            result = own_columns_grad(left, packed_ref, packed_far, slice(third * width + at, third * width + at + step))
            out_ref[:, third * rows : (third + 1) * rows, at : at + step] = result.reshape(chips, rows, step)
    left = own_rows(core, o_ref, o_far, turned)
    for at in range(0, width, step):
        result = own_columns_grad(left, gat_ref, gat_far, slice(at, at + step))
        out_ref[:, 3 * rows : 4 * rows, at : at + step] = result.reshape(chips, rows, step)
    total = vec_ref[...] + vec_far[...]
    for chip in range(chips):
        pair = total[:, chip * 2 * rows : (chip + 1) * 2 * rows]
        turn = jnp.concatenate([pair[:, rows:], pair[:, :rows]], axis=1)
        own = jnp.where(core == 0, pair, turn)
        out_ref[chip, 4 * rows :, : 2 * rows] = own.astype(BF16)
        out_ref[chip, 4 * rows :, 2 * rows :] = jnp.zeros((own.shape[0], width - 2 * rows), BF16)


def project_grad(core, operands, behind):
    tokens, width = operands[0].shape
    rows = width // HEADS
    return call(
        project_grad_kernel,
        array((PAIRS, 4 * rows + 16, width), BF16),
        (core, *operands),
        [scalars()] + [VMEM] * len(operands),
        VMEM,
        [turned_scratch(tokens, width)],
        8 * tokens * width * width,
        12 << 20,
        behind=behind,
        limit=24,
    )


DECAY = 1.0 - STEP ** (-0.8)
LANES = 128


def sums_at(cuts, columns):
    lines = sum(blocks for first, rows, blocks in cuts) * columns // LANES
    return lines, 2 * lines, 2 * lines + 8


def turned_row(row):
    return jnp.sum(jnp.where(diagonal(row.shape[1]), row, 0.0), axis=1, keepdims=True)


def turned_column(column):
    return jnp.sum(jnp.where(diagonal(column.shape[0]), column, 0.0), axis=0, keepdims=True)


def diagonal(count):
    rows = lax.broadcasted_iota(jnp.int32, (count, count), 0)
    return rows == lax.broadcasted_iota(jnp.int32, (count, count), 1)


def finish_kernel(addends, cuts, with_vectors, *refs):
    parts = len(cuts)
    refs = list(refs)

    def take(count):
        taken = refs[:count]
        del refs[:count]
        return taken

    if addends > 1:
        (chips_ref, blocks), addend_refs = take(2), take(addends - 1)
    else:
        addend_refs = take(1)
    old_refs = take(parts)
    moment_refs = take(int(with_vectors))
    grad_refs, row_refs, over_refs = take(parts), take(parts), take(parts)
    vector_refs = take(2 * int(with_vectors))
    (sums_ref,) = take(1)
    if addends > 1:
        own, sems = refs
        for copy in fetch([(blocks.at[chips_ref[0]], own)], sems):
            copy.wait()
        addend_refs.append(own)
    columns = addend_refs[0].shape[1]
    norms, totals, vector_line = sums_at(cuts, columns)

    def sum_of(rows, cut):
        total = None
        for ref in addend_refs:
            value = ref[rows, cut].astype(F32)
            total = value if total is None else total + value
        return total

    sums_ref[totals : totals + 8] = jnp.zeros((8, LANES), F32)
    line = 0
    for part, (first, rows, blocks) in enumerate(cuts):
        row_sum = None
        for block in range(blocks):
            grad = sum_of(slice(first + block * rows, first + (block + 1) * rows), ALL)
            cut = slice(block * columns, (block + 1) * columns)
            grad_refs[part][:, cut] = grad
            square = grad * grad + 1e-30
            block_sum = jnp.sum(square, axis=1, keepdims=True)
            row_sum = block_sum if row_sum is None else row_sum + block_sum
            column_sum = jnp.sum(square, axis=0, keepdims=True)
            for at in range(columns // LANES):
                to = line + block * columns // LANES + at
                sums_ref[to : to + 1] = column_sum[:, at * LANES : (at + 1) * LANES]
        row_stat = DECAY * turned_row(old_refs[part][...]) + (1.0 - DECAY) * (row_sum / (blocks * columns))
        row_refs[part][...] = turned_column(row_stat)
        root = lax.rsqrt(row_stat)
        for block in range(blocks):
            grad = grad_refs[part][:, block * columns : (block + 1) * columns]
            over = grad * root
            over_refs[part][:, block * columns : (block + 1) * columns] = over
            column_sum = jnp.sum(over * over, axis=0, keepdims=True)
            for at in range(columns // LANES):
                to = norms + line + block * columns // LANES + at
                sums_ref[to : to + 1] = column_sum[:, at * LANES : (at + 1) * LANES]
        line += blocks * columns // LANES
        total = jnp.sum(row_stat, axis=0, keepdims=True)
        sums_ref[totals + part : totals + part + 1] = jnp.broadcast_to(total, (1, LANES))
    if with_vectors:
        last = cuts[-1][0] + cuts[-1][1] * cuts[-1][2]
        moment = moment_refs[0][...]
        count, wide = moment.shape
        grad = sum_of(slice(last, last + 16), slice(0, LANES))[:count, :wide]
        second = DECAY * moment + (1.0 - DECAY) * (grad * grad + 1e-30)
        vector_refs[0][...] = grad
        vector_refs[1][...] = second
        move = grad * lax.rsqrt(second)
        norm = jnp.sum(move * move, axis=1, keepdims=True)
        sums_ref[vector_line:] = jnp.zeros((16, LANES), F32)
        sums_ref[vector_line : vector_line + count] = jnp.broadcast_to(norm, (count, LANES))


def finish(parts, olds, cuts, moment, here, behind=()):
    columns = parts[-1].shape[1]
    rows = parts[-1].shape[0]
    outs = [array((count, blocks * columns), F32) for first, count, blocks in cuts]
    outs += [array((1, count), F32) for first, count, blocks in cuts]
    outs += outs[: len(cuts)]
    vectors = () if moment is None else (moment,)
    outs += [array(value.shape, F32) for value in vectors for unused in range(2)]
    outs += [array((sums_at(cuts, columns)[2] + 16 * len(vectors), LANES), F32)]
    args, specs, scratch = list(parts), [VMEM] * len(parts), []
    if len(parts) > 1:
        args, specs = [here.table, *parts], [scalars(), HBM] + [VMEM] * (len(parts) - 1)
        scratch = [pltpu.VMEM((rows, columns), parts[0].dtype), pltpu.SemaphoreType.DMA((1,))]
    args += list(olds) + list(vectors)
    specs += [VMEM] * (len(olds) + len(vectors))
    return call(
        functools.partial(finish_kernel, len(parts), cuts, bool(vectors)),
        tuple(outs),
        tuple(args),
        specs,
        (VMEM,) * len(outs),
        scratch,
        8 * rows * columns,
        8 * rows * columns,
        behind,
        16,
    )


def update_kernel(chunks, full_rows, *refs):
    refs = list(refs)

    def take(count):
        taken = refs[:count]
        del refs[:count]
        return taken

    operands = []
    for cuts, columns, with_vectors in chunks:
        operands.append([take(len(cuts)) for unused in range(3)] + [take(3 * int(with_vectors))])
    (sums_ref,) = take(1)
    base = 0
    for (cuts, columns, with_vectors), operand in zip(chunks, operands):
        over_refs, master_refs, old_refs, vector_refs = operand
        updated_refs, column_refs = take(len(cuts)), take(len(cuts))
        norms, totals, vector_line = sums_at(cuts, columns)

        def lanes(start, count):
            return jnp.concatenate([sums_ref[start + at : start + at + 1] for at in range(count)], axis=1)

        line = base
        for part, (first, rows, blocks) in enumerate(cuts):
            wide = blocks * columns
            lines = wide // LANES
            square, weighted = lanes(line, lines), lanes(norms + line, lines)
            line += lines
            count = full_rows[rows]
            row_mean = sums_ref[base + totals + part : base + totals + part + 1, 0:1] / count
            col_stat = DECAY * old_refs[part][...] + (1.0 - DECAY) * (square / count)
            column_refs[part][...] = col_stat
            norm = row_mean * jnp.sum(weighted / col_stat, axis=1, keepdims=True)
            scale = jnp.sqrt(norm / (count * wide))
            rate = jnp.sqrt(row_mean) * (RATE / jnp.maximum(1.0, scale))
            updated_refs[part][...] = master_refs[part][...] - over_refs[part][...] * (rate * lax.rsqrt(col_stat))
        if with_vectors:
            grad_ref, second_ref, vectors_ref = vector_refs
            count = grad_ref.shape[0]
            norm = sums_ref[base + vector_line : base + vector_line + count, 0:1]
            scale = jnp.sqrt(norm / columns)
            move = grad_ref[...] * lax.rsqrt(second_ref[...])
            (updated_ref,) = take(1)
            updated_ref[...] = vectors_ref[...] - VECTOR_RATE * move / jnp.maximum(1.0, scale)
        base += vector_line + 16 * int(with_vectors)


def update(chunks, operands, sums, size):
    outs, args = [], []
    for grads, masters, olds, vectors in operands:
        outs += [array(grad.shape, F32) for grad in grads]
        outs += [array((1, grad.shape[1]), F32) for grad in grads]
        outs += [array(value.shape, F32) for value in vectors[2:]]
        args += [*grads, *masters, *olds, *vectors]
    full_rows = {grad.shape[0]: grad.shape[0] * size for operand in operands for grad in operand[0]}
    results = call(
        functools.partial(update_kernel, chunks, full_rows),
        tuple(outs),
        (*args, sums),
        [VMEM] * (len(args) + 1),
        (VMEM,) * len(outs),
        [],
        8 << 20,
        10 << 20,
        limit=24,
    )
    split = []
    for grads, masters, olds, vectors in operands:
        count = 2 * len(grads) + len(vectors[2:])
        split.append(results[:count])
        results = results[count:]
    return split


class Place:
    def __init__(self):
        self.size = lax.axis_size("dp")
        self.chips = self.size // 2
        self.ring = list(range(0, self.chips, 2)) + list(range(self.chips - 1, 0, -2))
        self.small = self.size == HEADS
        index = lax.axis_index("dp")
        self.chip = index // 2
        self.core = index % 2 if self.small else jnp.zeros_like(index)
        where = [0] * self.chips
        for place, chip in enumerate(self.ring):
            where[chip] = place
        tables = [
            [self.ring[(where[chip] + offset) % self.chips] for offset in range(self.chips)]
            for chip in range(self.chips)
        ]
        self.table = lax.dynamic_index_in_dim(
            jnp.array(tables, jnp.int32), self.chip, 0, keepdims=False
        )

    def permute(self, array, target):
        pairs = []
        for chip in range(self.chips):
            for core in range(2):
                to_chip, to_core = target(chip, core)
                pairs.append((chip * 2 + core, to_chip * 2 + to_core))
        return lax.ppermute(array, "dp", pairs)

    def shift(self, array, by):
        where = {chip: place for place, chip in enumerate(self.ring)}
        return self.permute(
            array, lambda chip, core: (self.ring[(where[chip] + by) % self.chips], core)
        )

    def swap(self, array):
        return self.permute(array, lambda chip, core: (chip, 1 - core))

    def cross(self, array, mask):
        return self.permute(array, lambda chip, core: (chip ^ mask, core))

    def masks(self):
        return [1 << bit for bit in range(self.chips.bit_length() - 1)]


def section_shift(array, by):
    size = lax.axis_size("section")
    pairs = [(i, i + by) for i in range(size) if 0 <= i + by < size]
    return lax.ppermute(array, "section", pairs)


def upper_rows(rows):
    return (rows // 2 + 15) // 16 * 16


def gate_kernel():
    pass


def gated(arrays, behind):
    return call(gate_kernel, (), (), [], (), [], 0, 1 << 10, behind, passing=arrays)[1]


class RingGather:
    def __init__(self, own, here):
        self.here = here
        self.rows, self.columns = own.shape
        self.pieces = [(0, 0, own)]
        self.ahead = self.behind = own
        self.step = 0
        self.round()

    def round(self, behind=(), passing=()):
        here = self.here
        self.step += 1
        if behind or passing:
            self.ahead, self.behind, *passing = gated((self.ahead, self.behind, *passing), behind)
            if self.step > 1:
                self.pieces[-2:] = [
                    (1 - self.step, 0, self.ahead),
                    (self.step - 1, 0, self.behind),
                ]
        if self.step < here.chips // 2:
            self.ahead = here.shift(self.ahead, 1)
            self.behind = here.shift(self.behind, -1)
            self.pieces += [(-self.step, 0, self.ahead), (self.step, 0, self.behind)]
        else:
            cut = upper_rows(self.rows)
            self.ahead = here.shift(self.ahead[:cut], 1)
            self.behind = here.shift(self.behind[cut:], -1)
            self.pieces += [(self.step, 0, self.ahead), (self.step, cut, self.behind)]
        return passing

    def heads(self):
        return self.ahead, self.behind


def placed(rings, here, behind=()):
    plan, arrays, base = [], [], 0
    for ring in rings:
        for offset, row, piece in ring.pieces:
            plan.append((offset % here.chips, base + row))
            arrays.append(piece)
        base += ring.rows
    columns = arrays[0].shape[1]
    return call(
        functools.partial(place_kernel, tuple(plan)),
        array((here.chips, base, columns), arrays[0].dtype),
        (here.table, *arrays),
        [scalars()] + [HBM] * len(arrays),
        VMEM,
        [pltpu.SemaphoreType.DMA((len(arrays),))],
        0,
        4 * here.chips * base * columns,
        behind,
        56 if len(rings) == 1 else 30,
    )


def place_kernel(plan, chips_ref, *refs):
    out, sems = refs[-2:]
    pairs = []
    for piece, (place, row) in zip(refs, plan):
        pairs.append((piece, out.at[chips_ref[place], pl.ds(row, piece.shape[0])]))
    for copy in fetch(pairs, sems):
        copy.wait()


def pack_kernel(project_hbm, merge_hbm, vectors_ref, expand_hbm, out_ref, expand_out, project_ref, merge_ref, expand_ref, sems):
    copies = fetch([(project_hbm, project_ref), (merge_hbm, merge_ref), (expand_hbm, expand_ref)], sems)
    rows, width = merge_ref.shape
    count, wide = vectors_ref.shape
    vectors = jnp.concatenate([vectors_ref[...], jnp.zeros((16 - count, wide), F32)], axis=0)
    out_ref[4 * rows :] = jnp.concatenate(
        [vectors.astype(BF16), jnp.zeros((16, width - wide), BF16)], axis=1
    )
    copies[0].wait()
    for third in range(3):
        out_ref[third * rows : (third + 1) * rows] = project_ref[:, third * width : (third + 1) * width].astype(BF16)
    copies[1].wait()
    out_ref[3 * rows : 4 * rows] = merge_ref[...].astype(BF16)
    copies[2].wait()
    expand_out[...] = expand_ref[...].astype(BF16)


def pack_rows(project, merge, vectors, expand):
    rows, width = merge.shape
    return call(
        pack_kernel,
        (array((4 * rows + 16, width), BF16), array(expand.shape, BF16)),
        (project, merge, vectors, expand),
        [HBM, HBM, VMEM, HBM],
        (VMEM, VMEM),
        [pltpu.VMEM(part.shape, F32) for part in (project, merge, expand)] + [pltpu.SemaphoreType.DMA((3,))],
        0,
        2 << 20,
        limit=56,
    )


def half_kernel(side, whole_ref, out_ref):
    rows = out_ref.shape[0]
    out_ref[...] = whole_ref[side * rows : (side + 1) * rows].astype(BF16)


def half_of(whole, side, behind):
    half = array((whole.shape[0] // 2, whole.shape[1]), BF16)
    return call(functools.partial(half_kernel, side), half, (whole,), [VMEM], VMEM, [], 0, 2 << 20, behind)


def vectors_of(near, far, core, wide):
    cuts = [part[:, -16:, :wide] for part in (near, far)]
    rows = jnp.where(core == 0, jnp.stack(cuts), jnp.stack(cuts[::-1]))
    return rows.transpose(2, 1, 0, 3).reshape(16, -1).astype(F32)


def gather_plainly(project, merge, expand, shrink, vectors):
    width = merge.shape[1]

    def whole_of_rows(rows):
        whole = lax.all_gather(rows.astype(BF16), "dp", axis=0, tiled=True)
        return whole.reshape(PAIRS, 2, -1, whole.shape[1])

    parts = [whole_of_rows(project[:, at * width : (at + 1) * width]) for at in range(3)]
    cuts = [jnp.concatenate([*parts, whole_of_rows(merge)], axis=2)]
    cuts += [whole_of_rows(expand), whole_of_rows(shrink)]
    rows = lax.all_gather(vectors.astype(BF16), "dp", axis=1, tiled=True)
    rows = jnp.pad(rows, ((0, 16 - vectors.shape[0]), (0, 0)))
    return *((cut[:, 0], cut[:, 1]) for cut in cuts), rows.astype(F32)


def far_kernel(half, chips_ref, blocks, upper_ref, lower_ref, sems):
    cut = upper_ref.shape[0]
    chip = chips_ref[half]
    pairs = [
        (blocks.at[chip, pl.ds(0, cut)], upper_ref),
        (blocks.at[chip, pl.ds(cut, lower_ref.shape[0])], lower_ref),
    ]
    for copy in fetch(pairs, sems):
        copy.wait()


def add_kernel(ahead_at, behind_at, chips_ref, blocks, ahead_got, behind_got, ahead_out, behind_out, ahead_ref, behind_ref, sems):
    pairs = [
        (blocks.at[chips_ref[ahead_at]], ahead_out),
        (blocks.at[chips_ref[behind_at]], behind_out),
        (ahead_got, ahead_ref),
        (behind_got, behind_ref),
    ]
    for copy in fetch(pairs, sems):
        copy.wait()
    rows = behind_out.shape[0]
    for got, out, cut in (
        (ahead_ref, ahead_out, pl.ds(0, ahead_ref.shape[0])),
        (behind_ref, behind_out, pl.ds(rows - behind_ref.shape[0], behind_ref.shape[0])),
    ):
        out[cut] = (out[cut].astype(F32) + got[...].astype(F32)).astype(BF16)


class RingSum:
    def __init__(self, blocks, here, far=None):
        self.blocks = blocks
        self.here = here
        self.step = here.chips // 2
        self.sent = None
        if far is not None:
            self.send(far)

    def round(self, *behind, passing=()):
        here, blocks, step = self.here, self.blocks, self.step
        rows, columns = blocks.shape[1:]
        if self.sent is None:
            cut = upper_rows(rows)
            payload = call(
                functools.partial(far_kernel, step),
                (array((cut, columns), BF16), array((rows - cut, columns), BF16)),
                (here.table, blocks),
                [scalars(), HBM],
                (VMEM, VMEM),
                [pltpu.SemaphoreType.DMA((2,))],
                0,
                4 * rows * columns,
                behind,
            )
        else:
            whole = array((rows, columns), BF16)
            payload = call(
                functools.partial(add_kernel, step, here.chips - step),
                (whole, whole),
                (here.table, blocks, *self.sent),
                [scalars(), HBM, HBM, HBM],
                (VMEM, VMEM),
                [pltpu.VMEM(part.shape, BF16) for part in self.sent] + [pltpu.SemaphoreType.DMA((4,))],
                2 * rows * columns,
                12 * rows * columns,
                behind,
                passing=passing,
            )
            if passing:
                payload, passing = payload
        self.send(payload)
        return (payload[0], *passing)

    def send(self, payload):
        self.step -= 1
        self.sent = (self.here.shift(payload[0], 1), self.here.shift(payload[1], -1))

    def parts(self):
        return (self.blocks, *self.sent)


def small_sum(vector, here):
    if not here.small:
        return lax.psum(vector, "dp")
    vector = vector + here.swap(vector)
    near = [here.cross(vector, mask) for mask in (1, 2, 3)]
    vector = (vector + near[0]) + (near[1] + near[2])
    for mask in here.masks()[2:]:
        vector = vector + here.cross(vector, mask)
    return vector


def segments(lengths_row, count):
    ends = jnp.cumsum(lengths_row)
    places = jnp.arange(count, dtype=jnp.int32)
    return jnp.sum((places[:, None] >= ends[None, :]).astype(jnp.int32), axis=1)


def per_device(
    frames,
    lengths,
    cotangent,
    project_weight,
    merge_weight,
    expand_weight,
    shrink_weight,
    vectors,
    project_row,
    project_col,
    merge_row,
    merge_col,
    expand_row,
    expand_col,
    shrink_row,
    shrink_col,
    vector_moment,
):
    here = Place()
    core = here.core.reshape(1)
    is_first = lax.axis_index("section") == 0
    micro = lengths.shape[0]
    count, width = frames.shape
    block = count // micro
    segment = jax.vmap(lambda lengths_row: segments(lengths_row, block))(lengths)
    live = (segment < UTTS).astype(F32).reshape(count, 1)
    visible = (segment[:, :, None] == segment[:, None, :]).astype(F32)

    masters = (project_weight[0], merge_weight[0], expand_weight[0], shrink_weight[0])
    first = is_first.astype(jnp.int32).reshape(1)
    if here.small:
        pm_rows, e_rows = pack_rows(masters[0], masters[1], vectors[0], masters[2])
        pm_ring, e_ring = RingGather(pm_rows, here), RingGather(e_rows, here)
        pm_ring.round()
        pm_ring.round(e_ring.heads())
        e_ring.round()
        upper_ring = RingGather(half_of(masters[3], 0, pm_ring.heads()), here)
        pm_ring.round(e_ring.heads())
        e_ring.round()
        lower_ring = RingGather(half_of(masters[3], 1, e_ring.heads()), here)
        e_ring.round(upper_ring.heads())
        upper_ring.round()
        upper_ring.round(lower_ring.heads())
        lower_ring.round()
        upper_ring.round(lower_ring.heads())
        lower_ring.round()
        lower_ring.round()
        near = placed([pm_ring], here)
        pm = (near, here.swap(near))
        vec = vectors_of(*pm, here.core, vectors.shape[2])
        near = placed([e_ring], here)
        e = (near, here.swap(near))
        near = placed([upper_ring, lower_ring], here)
        s = (near, here.swap(near))
        kept = attend_block(core, frames, visible, vec, pm, (near,))
        hidden, slope = expand_block(core, kept[-1], vec, e)
    else:
        pm, e, s, vec = gather_plainly(*masters, vectors[0])
        kept = attend_block(core, frames, visible, vec, pm)
        hidden, slope = expand_block(core, kept[-1], vec, e)

    unused, low = shrink_block(core, kept[3], hidden, vec, s)
    start = jnp.where(is_first, frames, section_shift(low, 1))
    kept = attend_block(core, start, visible, vec, pm)
    normed, packed, mixed, middle, normed_two = kept
    hidden, slope = expand_block(core, normed_two, vec, e)

    incoming, unused = incoming_grad(jnp.zeros((1,), jnp.int32), frames, cotangent, live, ())
    unused, unused, back_middle, back_branch, sums_two, sums_up = back_hidden_block(
        core, incoming, middle, vec, s, e, slope, ()
    )
    unused, unused, low, unused = back_attend_block(
        core, first, start, back_middle, back_branch, packed, visible, vec, sums_two, sums_up, pm, ()
    )
    output, unused = shrink_block(core, middle, hidden, vec, s, (low,))
    incoming, low_incoming = incoming_grad(first, section_shift(low, -1), cotangent, live, (output,))
    swap = here.swap if here.small else lambda rows: rows

    shared = [swap(rows) for rows in (hidden, normed_two, normed, mixed)]
    behind = ()
    if here.small:
        operands = (hidden, shared[0], low_incoming, swap(low_incoming))
        far = shrink_far(here, core, *operands, shared[1:])
        shrink_ring = RingSum(shrink_grad(core, *operands, far[:1]), here, far)
        behind = shrink_ring.round()
    low_out, back_pre, back_middle, back_branch, sums_two, sums_up = back_hidden_block(
        core, incoming, middle, vec, s, e, slope, behind
    )
    if here.small:
        last, back_pre, back_branch = shrink_ring.round(passing=(back_pre, back_branch))
        behind = (last,)
    back_packed, back_inputs, low, vector_sums = back_attend_block(
        core, first, start, back_middle, back_branch, packed, visible, vec, sums_two, sums_up, pm, behind
    )
    layer_outputs = output[None]
    input_grads = back_inputs[None]

    rows = masters[0].shape[0]
    shrink_cuts = ((0, masters[3].shape[0], 1),)
    expand_cuts = ((0, rows, 1),)
    both_cuts = ((0, rows, 3), (3 * rows, rows, 1))
    shrink_olds, expand_olds = (shrink_row,), (expand_row,)
    both_olds = (project_row, merge_row)
    moment = vector_moment[0]
    if here.small:
        last, back_packed, vector_sums = shrink_ring.round(passing=(back_packed, vector_sums))
        expand_ring = RingSum(
            expand_grad(core, normed_two, shared[1], back_pre, swap(back_pre), (last,)), here
        )
        (last,) = expand_ring.round()
        both_ring = RingSum(
            project_grad(
                core,
                (
                    normed,
                    shared[2],
                    back_packed,
                    swap(back_packed),
                    mixed,
                    shared[3],
                    back_branch,
                    swap(back_branch),
                    vector_sums,
                    swap(vector_sums),
                ),
                (last,),
            ),
            here,
        )
        (last,) = both_ring.round()
        (last,) = expand_ring.round(last)
        shrink_ends = finish(shrink_ring.parts(), shrink_olds, shrink_cuts, None, here, (last,))
        (last,) = both_ring.round(shrink_ends[0])
        (last,) = expand_ring.round(last)
        (last,) = both_ring.round(last)
        (last,) = expand_ring.round(last)
        (last,) = both_ring.round(last)
        expand_ends = finish(expand_ring.parts(), expand_olds, expand_cuts, None, here, (last,))
        both_parts = both_ring.parts()
    else:

        def total(left, right):
            whole = dot_first(left, right).astype(BF16)
            return lax.psum_scatter(whole, "dp", scatter_dimension=0, tiled=True).astype(F32)

        shrink_ends = finish((total(hidden, low_out),), shrink_olds, shrink_cuts, None, here)
        expand_ends = finish((total(normed_two, back_pre),), expand_olds, expand_cuts, None, here)
        thirds = [total(normed, back_packed[:, at * width : (at + 1) * width]) for at in range(3)]
        vector_rows = lax.psum_scatter(vector_sums, "dp", scatter_dimension=1, tiled=True)
        vector_rows = jnp.pad(vector_rows, ((0, 0), (0, width - vector_rows.shape[1])))
        both_parts = (jnp.concatenate([*thirds, total(mixed, back_branch), vector_rows], axis=0),)
        last = vector_sums

    both_ends = finish(both_parts, both_olds, both_cuts, moment, here)
    ends = (shrink_ends, expand_ends, both_ends)
    sums = small_sum(jnp.concatenate([end[-1] for end in ends], axis=0), here)
    chunks = ((shrink_cuts, width, False), (expand_cuts, 4 * width, False), (both_cuts, width, True))
    matrices = (masters[3:], masters[2:3], masters[:2])
    cols_old = ((shrink_col,), (expand_col,), (project_col, merge_col))
    operands = []
    for (cuts, columns, with_vectors), end, masters_own, olds in zip(chunks, ends, matrices, cols_old):
        count = len(cuts)
        values = (*end[3 * count : -1], vectors[0]) if with_vectors else ()
        operands.append((end[2 * count : 3 * count], masters_own, olds, values))
    outs = []
    for end, operand, results in zip(ends, operands, update(chunks, operands, sums, here.size)):
        count, values = len(operand[0]), operand[-1]
        own = []
        for part in range(count):
            own += [end[part][None], end[count + part], results[count + part], results[part][None]]
        outs.append(own)
        vector_outs = (*values[:2], *results[2 * count :])
    shrink_outs, expand_outs, both_outs = outs
    return (
        layer_outputs,
        input_grads,
        *both_outs,
        *expand_outs,
        *shrink_outs,
        *(rows[None] for rows in vector_outs),
    )


def solution(mesh):
    placed = (
        P("dp", None),
        P("dp", None),
        P("dp", None),
        P("section", "dp", None),
        P("section", "dp", None),
        P("section", "dp", None),
        P("section", "dp", None),
        P("section", None, "dp"),
        P("section", "dp"),
        P("section", None),
        P("section", "dp"),
        P("section", None),
        P("section", "dp"),
        P("section", None),
        P("section", "dp"),
        P("section", None),
        P("section", None, "dp"),
    )
    matrix = (
        P("section", "dp", None),
        P("section", "dp"),
        P("section", None),
        P("section", "dp", None),
    )
    return jax.shard_map(
        per_device,
        mesh=mesh,
        in_specs=placed,
        out_specs=(
            P("section", "dp", None),
            P("section", "dp", None),
            *matrix,
            *matrix,
            *matrix,
            *matrix,
            P("section", None, "dp"),
            P("section", None, "dp"),
            P("section", None, "dp"),
        ),
        check_vma=False,
    )
```

```python
import functools
import math

import jax
import jax.numpy as jnp
from jax import lax
from jax.experimental import pallas as pl
from jax.experimental.pallas import tpu as pltpu
from jax.sharding import PartitionSpec as P

HEADS = 16
HEAD_DIM = 64
PAIRS = HEADS // 2
UTTS = 3
STEP = 10

EPSILON = 1e-05
RATE = 0.04
VECTOR_RATE = 0.25
MASKED = -1e30
BF16 = jnp.bfloat16
F32 = jnp.float32
VMEM = pl.BlockSpec(memory_space=pltpu.VMEM)
HBM = pl.BlockSpec(memory_space=pl.ANY)
MIB = 1024 * 1024


def dot(left, right):
    return lax.dot_general(left, right, (((1,), (0,)), ((), ())), preferred_element_type=F32)


def dot_last(left, right):
    return lax.dot_general(left, right, (((1,), (1,)), ((), ())), preferred_element_type=F32)


def dot_first(left, right):
    return lax.dot_general(left, right, (((0,), (0,)), ((), ())), preferred_element_type=F32)


def moments(values):
    centred = values - jnp.mean(values, axis=-1, keepdims=True)
    spread = jnp.mean(centred * centred, axis=-1, keepdims=True)
    scale = lax.rsqrt(spread + EPSILON)
    return centred * scale, scale


def norm_back(grad, unit, scale, gain):
    inner = grad * gain
    first = jnp.mean(inner, axis=-1, keepdims=True)
    second = jnp.mean(inner * unit, axis=-1, keepdims=True)
    return scale * (inner - first - unit * second)


def fetch(pairs, sems):
    copies = [
        pltpu.make_async_copy(source, target, sems.at[index])
        for index, (source, target) in enumerate(pairs)
    ]
    for copy in copies:
        copy.start()
    return copies


def half_masks():
    lane = lax.broadcasted_iota(jnp.int32, (1, 128), 1)
    low = jnp.where(lane < HEAD_DIM, 1.0, 0.0)
    return low.astype(BF16), (1.0 - low).astype(BF16)


def two_heads(tile, masks):
    return jnp.concatenate([tile * masks[0], tile * masks[1]], axis=0)


def side_by_side(both):
    half = both.shape[0] // 2
    return jnp.concatenate([both[:half], both[half:]], axis=1)


def weights_of(scores, visible):
    scores = jnp.where(visible, scores * HEAD_DIM**-0.5, MASKED)
    shifted = jnp.exp(scores - jnp.max(scores, axis=-1, keepdims=True))
    return shifted / jnp.sum(shifted, axis=-1, keepdims=True)


def scalars():
    return pl.BlockSpec(memory_space=pltpu.SMEM)


def array(shape, kind):
    return jax.ShapeDtypeStruct(shape, kind)


def call(kernel, outs, args, in_specs, out_specs, scratch, flops, size, behind=(), limit=12, passing=()):
    given, skipped = len(args), len(behind) + len(passing)
    single = not isinstance(outs, tuple)
    results = (outs,) if single else outs
    result_specs = (out_specs,) if single else out_specs
    count = len(results)

    def body(*refs):
        kernel(*refs[:given], *refs[given + skipped :][:count], *refs[given + skipped + count + len(passing) :])

    returned = pl.pallas_call(
        body,
        out_shape=(*results, *(array(value.shape, value.dtype) for value in passing)),
        in_specs=[
            *in_specs,
            *(HBM for unused in range(skipped)),
        ],
        out_specs=(*result_specs, *(HBM for unused in passing)),
        scratch_shapes=scratch,
        input_output_aliases={given + len(behind) + at: count + at for at in range(len(passing))},
        compiler_params=pltpu.CompilerParams(vmem_limit_bytes=limit * MIB),
        cost_estimate=pl.CostEstimate(flops=flops, bytes_accessed=size, transcendentals=0),
    )(*args, *behind, *passing)
    own = returned[0] if single else tuple(returned[:count])
    return (own, tuple(returned[count:])) if passing else own


def both_cores(core, near, far, whole, cuts):
    pairs = []
    for cut in cuts:
        pairs.append((near.at[cut], whole.at[cut[0], core, *cut[1:]]))
        pairs.append((far.at[cut], whole.at[cut[0], 1 - core, *cut[1:]]))
    return pairs


ALL = slice(None)


def quarters_of(core, near, far, whole, order):
    rows = whole.shape[3]
    pairs = []
    for at in order:
        pairs.append((near.at[:, pl.ds(at * rows, rows)], whole.at[at, :, core]))
        pairs.append((far.at[:, pl.ds(at * rows, rows)], whole.at[at, :, 1 - core]))
    return pairs


def quarters_scratch(width):
    return pltpu.VMEM((4, PAIRS, 2, width // HEADS, width), BF16)


def columns_cut(start, size):
    return (ALL, ALL, pl.ds(start, size))


def attend_kernel(core_ref, x_ref, mask_ref, vec_ref, near, far, a_ref, packed_ref, o_ref, x1_ref, c_ref, w, sems):
    count, width = x_ref.shape
    block = mask_ref.shape[1]
    step = 512
    copies = fetch(quarters_of(core_ref[0], near, far, w, range(4)), sems)
    unit, unused = moments(x_ref[...].astype(F32))
    a_ref[...] = (unit * vec_ref[0:1] + vec_ref[1:2]).astype(BF16)
    for third in range(3):
        copies[2 * third].wait()
        copies[2 * third + 1].wait()
        for cut in range(width // step):
            at = third * width + cut * step
            matrix = w[third, :, :, :, cut * step : (cut + 1) * step].reshape(width, step)
            result = dot(a_ref[...], matrix)
            if third != 1:
                row = 2 if third == 0 else 3
                result = result + vec_ref[row : row + 1, cut * step : (cut + 1) * step]
            packed_ref[:, at : at + step] = result.astype(BF16)
    masks = half_masks()
    for micro in range(count // block):
        rows = slice(micro * block, (micro + 1) * block)
        visible = mask_ref[micro] > 0.0
        visible = jnp.concatenate([visible, visible], axis=0)
        for at in range(0, width, 128):
            queries = packed_ref[rows, at : at + 128]
            keys = packed_ref[rows, at + width : at + width + 128]
            values = packed_ref[rows, at + 2 * width : at + 2 * width + 128]
            attend = weights_of(dot_last(two_heads(queries, masks), keys), visible).astype(BF16)
            mixed = dot(side_by_side(attend), two_heads(values, masks))
            o_ref[rows, at : at + 128] = mixed.astype(BF16)
    copies[6].wait()
    copies[7].wait()
    for at in range(0, width, step):
        cut = slice(at, at + step)
        matrix = w[3, :, :, :, cut].reshape(width, step)
        x1_ref[:, cut] = x_ref[:, cut].astype(F32) + (dot(o_ref[...], matrix) + vec_ref[4:5, cut])
    unit, unused = moments(x1_ref[...])
    c_ref[...] = (unit * vec_ref[5:6] + vec_ref[6:7]).astype(BF16)


def whole_of(near):
    chips, rows, columns = near.shape
    return pltpu.VMEM((chips, 2, rows, columns), near.dtype)


def attend_block(core, x, mask, vec, pm, behind=()):
    count, width = x.shape
    low = array((count, width), BF16)
    return call(
        attend_kernel,
        (low, array((count, 3 * width), BF16), low, array((count, width), F32), low),
        (core, x, mask, vec, *pm),
        [scalars()] + [VMEM] * 3 + [HBM] * 2,
        (VMEM,) * 5,
        [quarters_scratch(width), pltpu.SemaphoreType.DMA((8,))],
        8 * count * width * width,
        20 << 20,
        behind=behind,
        limit=32,
    )


def gelu_parts(values):
    cdf = 0.5 * (1.0 + lax.erf(values * math.sqrt(0.5)))
    slope = cdf + values * jnp.exp(-0.5 * values * values) * (1.0 / math.sqrt(2.0 * math.pi))
    return values * cdf, slope


def expand_kernel(with_slope, core_ref, c_ref, vec_ref, near, far, hidden_ref, *refs):
    if with_slope:
        slope_hbm, w, slope, sems, out_sems = refs
    else:
        w, sems = refs
    count, width = c_ref.shape
    step = 256
    quarters = w.shape[3] // width
    copies = fetch(
        both_cores(core_ref[0], near, far, w, [columns_cut(at * width, width) for at in range(quarters)]), sems
    )
    sent = []
    for quarter in range(quarters):
        copies[2 * quarter].wait()
        copies[2 * quarter + 1].wait()
        for cut in range(width // step):
            at = quarter * width + cut * step
            result = dot(c_ref[...], w[:, :, :, at : at + step].reshape(width, step))
            bias = vec_ref[8 + quarter : 9 + quarter, cut * step : (cut + 1) * step]
            hidden, rise = gelu_parts(result + bias)
            hidden_ref[:, at : at + step] = hidden.astype(BF16)
            if with_slope:
                slope[:, at : at + step] = rise
        if not with_slope:
            continue
        at = slice(quarter * width, (quarter + 1) * width)
        copy = pltpu.make_async_copy(slope.at[:, at], slope_hbm.at[:, at], out_sems.at[quarter])
        copy.start()
        sent.append(copy)
    for copy in sent:
        copy.wait()


def expand_block(core, c, vec, e, with_slope=True):
    count, width = c.shape
    hidden = 4 * width
    outs, specs, scratch = [array((count, hidden), BF16)], [VMEM], [whole_of(e[0])]
    if with_slope:
        outs.append(array((count, hidden), F32))
        specs.append(HBM)
        scratch.append(pltpu.VMEM((count, hidden), F32))
    scratch.append(pltpu.SemaphoreType.DMA((8,)))
    if with_slope:
        scratch.append(pltpu.SemaphoreType.DMA((4,)))
    return call(
        functools.partial(expand_kernel, with_slope),
        tuple(outs),
        (core, c, vec, *e),
        [scalars()] + [VMEM] * 2 + [HBM] * 2,
        tuple(specs),
        scratch,
        2 * count * width * hidden,
        20 << 20,
        limit=32,
    )


def shrink_kernel(core_ref, x1_ref, hidden_ref, vec_ref, near, far, y_ref, low_ref, w, sems):
    chips, unused, rows, width = w.shape
    step = 512
    group = width // (2 * rows)
    copies = fetch(
        both_cores(core_ref[0], near, far, w, [(pl.ds(at, group),) for at in range(0, chips, group)]), sems
    )
    for index in range(chips // group):
        copies[2 * index].wait()
        copies[2 * index + 1].wait()
        left = hidden_ref[:, index * width : (index + 1) * width]
        for at in range(0, width, step):
            cut = slice(at, at + step)
            matrix = w[index * group : (index + 1) * group, :, :, cut].reshape(width, step)
            result = dot(left, matrix)
            if index == 0:
                y_ref[:, cut] = x1_ref[:, cut] + result
            elif index < chips // group - 1:
                y_ref[:, cut] += result
            else:
                total = y_ref[:, cut] + result + vec_ref[7:8, cut]
                y_ref[:, cut] = total
                low_ref[:, cut] = total.astype(BF16)


def shrink_block(core, x1, hidden, vec, s, behind=()):
    count, width = x1.shape
    return call(
        shrink_kernel,
        (array((count, width), F32), array((count, width), BF16)),
        (core, x1, hidden, vec, *s),
        [scalars()] + [VMEM] * 3 + [HBM] * 2,
        (VMEM, VMEM),
        [whole_of(s[0]), pltpu.SemaphoreType.DMA((8,))],
        8 * count * width * width,
        16 << 20,
        behind=behind,
        limit=28,
    )


def back_hidden_kernel(core_ref, dy_ref, x1_ref, vec_ref, s_near, s_far, e_near, e_far, slope_hbm, gf_ref, gu_ref, dx1_ref, gat_ref, sums_ref, bias_ref, ws, we, slope, dc, sems, slope_sems):
    chips, unused, rows, width = ws.shape
    group = width // (2 * rows)
    quarters = chips // group
    core = core_ref[0]
    pairs = []
    for index in range(quarters):
        at = pl.ds(index * width, width)
        pairs += both_cores(core, s_near, s_far, ws, [(pl.ds(index * group, group),)])
        pairs.append((slope_hbm.at[:, at], slope.at[:, at]))
        pairs += both_cores(core, e_near, e_far, we, [columns_cut(index * width, width)])
    copies = fetch(pairs, sems)
    gf_ref[...] = dy_ref[...].astype(BF16)
    step = 512
    for index in range(quarters):
        for copy in copies[5 * index : 5 * index + 3]:
            copy.wait()
        for near in range(group):
            matrix = ws[index * group + near].reshape(2 * rows, width)
            at = slice(index * width + near * 2 * rows, index * width + (near + 1) * 2 * rows)
            back = (dot_last(gf_ref[...], matrix) * slope[:, at]).astype(BF16)
            gu_ref[:, at] = back
            bias_ref[:, at] = jnp.sum(back.astype(F32), axis=0, keepdims=True)
        for copy in copies[5 * index + 3 : 5 * index + 5]:
            copy.wait()
        at = slice(index * width, (index + 1) * width)
        left = gu_ref[:, at]
        for half in range(2):
            matrix = we[half * (chips // 2) : (half + 1) * (chips // 2), :, :, at].reshape(step, width)
            to = slice(half * step, (half + 1) * step)
            result = dot_last(left, matrix)
            if index == 0:
                dc[:, to] = result
            else:
                dc[:, to] += result
    unit, scale = moments(x1_ref[...])
    grad = dc[...]
    back = dy_ref[...] + norm_back(grad, unit, scale, vec_ref[5:6])
    dx1_ref[...] = back
    gat_ref[...] = back.astype(BF16)
    sums_ref[...] = jnp.zeros_like(sums_ref)
    sums_ref[0:1] = jnp.sum(grad * unit, axis=0, keepdims=True)
    sums_ref[1:2] = jnp.sum(grad, axis=0, keepdims=True)
    sums_ref[2:3] = jnp.sum(gf_ref[...].astype(F32), axis=0, keepdims=True)
    sums_ref[3:4] = jnp.sum(gat_ref[...].astype(F32), axis=0, keepdims=True)


def back_hidden_block(core, dy, x1, vec, s, e, slope, behind):
    count, width = x1.shape
    hidden = slope.shape[1]
    return call(
        back_hidden_kernel,
        (
            array((count, width), BF16),
            array((count, hidden), BF16),
            array((count, width), F32),
            array((count, width), BF16),
            array((8, width), F32),
            array((1, hidden), F32),
        ),
        (core, dy, x1, vec, *s, *e, slope),
        [scalars()] + [VMEM] * 3 + [HBM] * 5,
        (VMEM,) * 6,
        [
            whole_of(s[0]),
            whole_of(e[0]),
            pltpu.VMEM((count, hidden), F32),
            pltpu.VMEM((count, width), F32),
            pltpu.SemaphoreType.DMA((20,)),
            pltpu.SemaphoreType.DMA((4,)),
        ],
        16 * count * width * width,
        32 << 20,
        behind,
        limit=44,
    )


def back_attend_kernel(core_ref, first_ref, x_ref, dx1_ref, gat_ref, packed_ref, mask_ref, vec_ref, two_ref, up_ref, near, far, gqkv_ref, dx_ref, low_ref, sums_ref, w, go, sems):
    count, width = x_ref.shape
    block = mask_ref.shape[1]
    step = 512
    copies = fetch(quarters_of(core_ref[0], near, far, w, (3, 0, 1, 2)), sems)
    masks = half_masks()
    factor = HEAD_DIM**-0.5
    copies[0].wait()
    copies[1].wait()
    chips = w.shape[1]
    for half in range(2):
        matrix = w[3, half * (chips // 2) : (half + 1) * (chips // 2)].reshape(step, width)
        go[:, half * step : (half + 1) * step] = dot_last(gat_ref[...], matrix).astype(BF16)
    tiles = range(0, width, 128)
    for micro in range(count // block):
        rows = slice(micro * block, (micro + 1) * block)
        visible = mask_ref[micro] > 0.0
        visible = jnp.concatenate([visible, visible], axis=0)
        queries = [two_heads(packed_ref[rows, at : at + 128], masks) for at in tiles]
        keys = [packed_ref[rows, at + width : at + width + 128] for at in tiles]
        values = [packed_ref[rows, at + 2 * width : at + 2 * width + 128] for at in tiles]
        back = [two_heads(go[rows, at : at + 128], masks) for at in tiles]
        scores = [dot_last(query, key) for query, key in zip(queries, keys)]
        slopes = [dot_last(grad, value) for grad, value in zip(back, values)]
        attend = [weights_of(score, visible) for score in scores]
        low = [weight.astype(BF16) for weight in attend]
        inner = [jnp.sum(weight * slope, axis=-1, keepdims=True) for weight, slope in zip(attend, slopes)]
        scores = [
            (weight * (slope - total)).astype(BF16)
            for weight, slope, total in zip(attend, slopes, inner)
        ]
        grad_q = [dot(side_by_side(score), two_heads(key, masks)) for score, key in zip(scores, keys)]
        grad_k = [dot_first(score, query) for score, query in zip(scores, queries)]
        grad_v = [dot_first(weight, grad) for weight, grad in zip(low, back)]
        for at, one, two, three in zip(tiles, grad_q, grad_k, grad_v):
            gqkv_ref[rows, at : at + 128] = (one * factor).astype(BF16)
            gqkv_ref[rows, at + width : at + width + 128] = (two * factor).astype(BF16)
            gqkv_ref[rows, at + 2 * width : at + 2 * width + 128] = three.astype(BF16)
    for copy in copies[2:]:
        copy.wait()
    for half in range(2):
        total = None
        for third in range(3):
            matrix = w[third, half * (chips // 2) : (half + 1) * (chips // 2)].reshape(step, width)
            result = dot_last(gqkv_ref[:, third * width : (third + 1) * width], matrix)
            total = result if total is None else total + result
        dx_ref[:, half * step : (half + 1) * step] = total
    unit, scale = moments(x_ref[...].astype(F32))
    grad = dx_ref[...]
    sums_ref[...] = jnp.zeros_like(sums_ref)
    sums_ref[0:1] = jnp.sum(grad * unit, axis=0, keepdims=True)
    sums_ref[1:2] = jnp.sum(grad, axis=0, keepdims=True)
    back = dx1_ref[...] + norm_back(grad, unit, scale, vec_ref[0:1])
    low = back.astype(BF16)
    low_ref[...] = low
    dx_ref[...] = jnp.where(first_ref[0] == 1, back, low.astype(F32))
    for row, third in ((2, 0), (3, 2)):
        part = gqkv_ref[:, third * width : (third + 1) * width]
        sums_ref[row : row + 1] = jnp.sum(part.astype(F32), axis=0, keepdims=True)
    sums_ref[4:5] = two_ref[3:4]
    sums_ref[5:8] = two_ref[0:3]
    for quarter in range(4):
        sums_ref[8 + quarter : 9 + quarter] = up_ref[:, quarter * width : (quarter + 1) * width]


def back_attend_block(core, first, x, dx1, gat, packed, mask, vec, two, up, pm, behind):
    count, width = x.shape
    return call(
        back_attend_kernel,
        (
            array((count, 3 * width), BF16),
            array((count, width), F32),
            array((count, width), BF16),
            array((16, width), F32),
        ),
        (core, first, x, dx1, gat, packed, mask, vec, two, up, *pm),
        [scalars()] * 2 + [VMEM] * 8 + [HBM] * 2,
        (VMEM,) * 4,
        [quarters_scratch(width), pltpu.VMEM((count, width), BF16), pltpu.SemaphoreType.DMA((8,))],
        12 * count * width * width,
        20 << 20,
        behind,
        limit=32,
    )


def incoming_kernel(first_ref, mail_ref, cotangent_ref, live_ref, out_ref, low_ref):
    targets = cotangent_ref[...].astype(F32) * live_ref[...]
    mail = mail_ref[...].astype(F32)
    out = jnp.where(first_ref[0] == 1, mail, targets)
    out_ref[...] = out
    low_ref[...] = out.astype(BF16)


def incoming_grad(first, mail, cotangent, live, behind):
    shape = cotangent.shape
    return call(
        incoming_kernel,
        (array(shape, F32), array(shape, BF16)),
        (first, mail, cotangent, live),
        [scalars()] + [VMEM] * 3,
        (VMEM, VMEM),
        [],
        0,
        10 * cotangent.size,
        behind,
    )


def shrink_grad_kernel(core_ref, near_ref, far_ref, right_ref, other_ref, out_ref):
    chips, rows, width = out_ref.shape
    for chip in range(chips):
        at = pl.ds(pl.multiple_of((2 * chip + core_ref[0]) * rows, rows), rows)
        total = dot_first(near_ref[:, at], right_ref[...]) + dot_first(far_ref[:, at], other_ref[...])
        out_ref[chip] = total.astype(BF16)


def shrink_far_kernel(half, chips_ref, core_ref, near_ref, far_ref, right_ref, other_ref, upper_ref, lower_ref):
    cut, lower = upper_ref.shape[0], lower_ref.shape[0]
    at = (2 * chips_ref[half] + core_ref[0]) * (cut + lower)
    for start, out in ((0, upper_ref), (cut, lower_ref)):
        rows = pl.ds(pl.multiple_of(at + start, cut), out.shape[0])
        total = dot_first(near_ref[:, rows], right_ref[...]) + dot_first(far_ref[:, rows], other_ref[...])
        out[...] = total.astype(BF16)


def shrink_far(here, core, near, far, right, other, behind):
    tokens, hidden = near.shape
    width = right.shape[1]
    half = array((hidden // HEADS // 2, width), BF16)
    return call(
        functools.partial(shrink_far_kernel, here.chips // 2),
        (half, half),
        (here.table, core, near, far, right, other),
        [scalars()] * 2 + [VMEM] * 4,
        (VMEM, VMEM),
        [],
        2 * tokens * width * hidden // PAIRS,
        5 << 20,
        behind,
        24,
    )


def shrink_grad(core, near, far, right, other, behind):
    tokens, hidden = near.shape
    width = right.shape[1]
    return call(
        shrink_grad_kernel,
        array((PAIRS, hidden // HEADS, width), BF16),
        (core, near, far, right, other),
        [scalars()] + [VMEM] * 4,
        VMEM,
        [],
        2 * tokens * width * hidden,
        12 << 20,
        behind,
        limit=24,
    )


def own_rows(core, near_ref, far_ref, turned):
    chips, unused, rows, both = turned.shape
    tokens = near_ref.shape[0]
    turned[:, :, :, :tokens] = near_ref[...].T.reshape(chips, 2, rows, tokens)
    turned[:, :, :, tokens:] = far_ref[...].T.reshape(chips, 2, rows, tokens)
    return turned[:, pl.ds(core, 1)].reshape(chips * rows, both)


def own_columns_grad(left, right_ref, other_ref, cut):
    right = jnp.concatenate([right_ref[:, cut], other_ref[:, cut]], axis=0)
    return dot(left, right).astype(BF16)


def expand_grad_kernel(core_ref, near_ref, far_ref, right_ref, other_ref, out_ref, turned):
    chips, rows, columns = out_ref.shape
    left = own_rows(core_ref[0], near_ref, far_ref, turned)
    step = 512
    for at in range(0, columns, step):
        cut = slice(at, at + step)
        out_ref[:, :, cut] = own_columns_grad(left, right_ref, other_ref, cut).reshape(chips, rows, step)


def turned_scratch(tokens, width):
    return pltpu.VMEM((PAIRS, 2, width // HEADS, 2 * tokens), BF16)


def expand_grad(core, near, far, right, other, behind):
    tokens, width = near.shape
    hidden = right.shape[1]
    return call(
        expand_grad_kernel,
        array((PAIRS, width // HEADS, hidden), BF16),
        (core, near, far, right, other),
        [scalars()] + [VMEM] * 4,
        VMEM,
        [turned_scratch(tokens, width)],
        2 * tokens * width * hidden,
        12 << 20,
        behind=behind,
        limit=24,
    )


def project_grad_kernel(core_ref, a_ref, a_far, packed_ref, packed_far, o_ref, o_far, gat_ref, gat_far, vec_ref, vec_far, out_ref, turned):
    chips, unused, width = out_ref.shape
    rows = width // HEADS
    core = core_ref[0]
    step = 512
    left = own_rows(core, a_ref, a_far, turned)
    for third in range(3):
        for at in range(0, width, step):
            result = own_columns_grad(left, packed_ref, packed_far, slice(third * width + at, third * width + at + step))
            out_ref[:, third * rows : (third + 1) * rows, at : at + step] = result.reshape(chips, rows, step)
    left = own_rows(core, o_ref, o_far, turned)
    for at in range(0, width, step):
        result = own_columns_grad(left, gat_ref, gat_far, slice(at, at + step))
        out_ref[:, 3 * rows : 4 * rows, at : at + step] = result.reshape(chips, rows, step)
    total = vec_ref[...] + vec_far[...]
    for chip in range(chips):
        pair = total[:, chip * 2 * rows : (chip + 1) * 2 * rows]
        turn = jnp.concatenate([pair[:, rows:], pair[:, :rows]], axis=1)
        own = jnp.where(core == 0, pair, turn)
        out_ref[chip, 4 * rows :, : 2 * rows] = own.astype(BF16)
        out_ref[chip, 4 * rows :, 2 * rows :] = jnp.zeros((own.shape[0], width - 2 * rows), BF16)


def project_grad(core, operands, behind):
    tokens, width = operands[0].shape
    rows = width // HEADS
    return call(
        project_grad_kernel,
        array((PAIRS, 4 * rows + 16, width), BF16),
        (core, *operands),
        [scalars()] + [VMEM] * len(operands),
        VMEM,
        [turned_scratch(tokens, width)],
        8 * tokens * width * width,
        12 << 20,
        behind=behind,
        limit=24,
    )


DECAY = 1.0 - STEP ** (-0.8)
LANES = 128


def sums_at(cuts, columns):
    lines = sum(blocks for first, rows, blocks in cuts) * columns // LANES
    return lines, 2 * lines, 2 * lines + 8


def turned_row(row):
    return jnp.sum(jnp.where(diagonal(row.shape[1]), row, 0.0), axis=1, keepdims=True)


def turned_column(column):
    return jnp.sum(jnp.where(diagonal(column.shape[0]), column, 0.0), axis=0, keepdims=True)


def diagonal(count):
    rows = lax.broadcasted_iota(jnp.int32, (count, count), 0)
    return rows == lax.broadcasted_iota(jnp.int32, (count, count), 1)


def finish_kernel(addends, cuts, with_vectors, *refs):
    parts = len(cuts)
    refs = list(refs)

    def take(count):
        taken = refs[:count]
        del refs[:count]
        return taken

    if addends > 1:
        (chips_ref, blocks), addend_refs = take(2), take(addends - 1)
    else:
        addend_refs = take(1)
    old_refs = take(parts)
    moment_refs = take(int(with_vectors))
    grad_refs, row_refs, over_refs = take(parts), take(parts), take(parts)
    vector_refs = take(2 * int(with_vectors))
    (sums_ref,) = take(1)
    if addends > 1:
        own, sems = refs
        for copy in fetch([(blocks.at[chips_ref[0]], own)], sems):
            copy.wait()
        addend_refs.append(own)
    columns = addend_refs[0].shape[1]
    norms, totals, vector_line = sums_at(cuts, columns)

    def sum_of(rows, cut):
        total = None
        for ref in addend_refs:
            value = ref[rows, cut].astype(F32)
            total = value if total is None else total + value
        return total

    sums_ref[totals : totals + 8] = jnp.zeros((8, LANES), F32)
    line = 0
    for part, (first, rows, blocks) in enumerate(cuts):
        row_sum = None
        for block in range(blocks):
            grad = sum_of(slice(first + block * rows, first + (block + 1) * rows), ALL)
            cut = slice(block * columns, (block + 1) * columns)
            grad_refs[part][:, cut] = grad
            square = grad * grad + 1e-30
            block_sum = jnp.sum(square, axis=1, keepdims=True)
            row_sum = block_sum if row_sum is None else row_sum + block_sum
            column_sum = jnp.sum(square, axis=0, keepdims=True)
            for at in range(columns // LANES):
                to = line + block * columns // LANES + at
                sums_ref[to : to + 1] = column_sum[:, at * LANES : (at + 1) * LANES]
        row_stat = DECAY * turned_row(old_refs[part][...]) + (1.0 - DECAY) * (row_sum / (blocks * columns))
        row_refs[part][...] = turned_column(row_stat)
        root = lax.rsqrt(row_stat)
        for block in range(blocks):
            grad = grad_refs[part][:, block * columns : (block + 1) * columns]
            over = grad * root
            over_refs[part][:, block * columns : (block + 1) * columns] = over
            column_sum = jnp.sum(over * over, axis=0, keepdims=True)
            for at in range(columns // LANES):
                to = norms + line + block * columns // LANES + at
                sums_ref[to : to + 1] = column_sum[:, at * LANES : (at + 1) * LANES]
        line += blocks * columns // LANES
        total = jnp.sum(row_stat, axis=0, keepdims=True)
        sums_ref[totals + part : totals + part + 1] = jnp.broadcast_to(total, (1, LANES))
    if with_vectors:
        last = cuts[-1][0] + cuts[-1][1] * cuts[-1][2]
        moment = moment_refs[0][...]
        count, wide = moment.shape
        grad = sum_of(slice(last, last + 16), slice(0, LANES))[:count, :wide]
        second = DECAY * moment + (1.0 - DECAY) * (grad * grad + 1e-30)
        vector_refs[0][...] = grad
        vector_refs[1][...] = second
        move = grad * lax.rsqrt(second)
        norm = jnp.sum(move * move, axis=1, keepdims=True)
        sums_ref[vector_line:] = jnp.zeros((16, LANES), F32)
        sums_ref[vector_line : vector_line + count] = jnp.broadcast_to(norm, (count, LANES))


def finish(parts, olds, cuts, moment, here, behind=()):
    columns = parts[-1].shape[1]
    rows = parts[-1].shape[0]
    outs = [array((count, blocks * columns), F32) for first, count, blocks in cuts]
    outs += [array((1, count), F32) for first, count, blocks in cuts]
    outs += outs[: len(cuts)]
    vectors = () if moment is None else (moment,)
    outs += [array(value.shape, F32) for value in vectors for unused in range(2)]
    outs += [array((sums_at(cuts, columns)[2] + 16 * len(vectors), LANES), F32)]
    args, specs, scratch = list(parts), [VMEM] * len(parts), []
    if len(parts) > 1:
        args, specs = [here.table, *parts], [scalars(), HBM] + [VMEM] * (len(parts) - 1)
        scratch = [pltpu.VMEM((rows, columns), parts[0].dtype), pltpu.SemaphoreType.DMA((1,))]
    args += list(olds) + list(vectors)
    specs += [VMEM] * (len(olds) + len(vectors))
    return call(
        functools.partial(finish_kernel, len(parts), cuts, bool(vectors)),
        tuple(outs),
        tuple(args),
        specs,
        (VMEM,) * len(outs),
        scratch,
        8 * rows * columns,
        8 * rows * columns,
        behind,
        16,
    )


def update_kernel(chunks, full_rows, *refs):
    refs = list(refs)

    def take(count):
        taken = refs[:count]
        del refs[:count]
        return taken

    operands = []
    for cuts, columns, with_vectors in chunks:
        operands.append([take(len(cuts)) for unused in range(3)] + [take(3 * int(with_vectors))])
    (sums_ref,) = take(1)
    base = 0
    for (cuts, columns, with_vectors), operand in zip(chunks, operands):
        over_refs, master_refs, old_refs, vector_refs = operand
        updated_refs, column_refs = take(len(cuts)), take(len(cuts))
        norms, totals, vector_line = sums_at(cuts, columns)

        def lanes(start, count):
            return jnp.concatenate([sums_ref[start + at : start + at + 1] for at in range(count)], axis=1)

        line = base
        for part, (first, rows, blocks) in enumerate(cuts):
            wide = blocks * columns
            lines = wide // LANES
            square, weighted = lanes(line, lines), lanes(norms + line, lines)
            line += lines
            count = full_rows[rows]
            row_mean = sums_ref[base + totals + part : base + totals + part + 1, 0:1] / count
            col_stat = DECAY * old_refs[part][...] + (1.0 - DECAY) * (square / count)
            column_refs[part][...] = col_stat
            norm = row_mean * jnp.sum(weighted / col_stat, axis=1, keepdims=True)
            scale = jnp.sqrt(norm / (count * wide))
            rate = jnp.sqrt(row_mean) * (RATE / jnp.maximum(1.0, scale))
            updated_refs[part][...] = master_refs[part][...] - over_refs[part][...] * (rate * lax.rsqrt(col_stat))
        if with_vectors:
            grad_ref, second_ref, vectors_ref = vector_refs
            count = grad_ref.shape[0]
            norm = sums_ref[base + vector_line : base + vector_line + count, 0:1]
            scale = jnp.sqrt(norm / columns)
            move = grad_ref[...] * lax.rsqrt(second_ref[...])
            (updated_ref,) = take(1)
            updated_ref[...] = vectors_ref[...] - VECTOR_RATE * move / jnp.maximum(1.0, scale)
        base += vector_line + 16 * int(with_vectors)


def update(chunks, operands, sums, size):
    outs, args = [], []
    for grads, masters, olds, vectors in operands:
        outs += [array(grad.shape, F32) for grad in grads]
        outs += [array((1, grad.shape[1]), F32) for grad in grads]
        outs += [array(value.shape, F32) for value in vectors[2:]]
        args += [*grads, *masters, *olds, *vectors]
    full_rows = {grad.shape[0]: grad.shape[0] * size for operand in operands for grad in operand[0]}
    results = call(
        functools.partial(update_kernel, chunks, full_rows),
        tuple(outs),
        (*args, sums),
        [VMEM] * (len(args) + 1),
        (VMEM,) * len(outs),
        [],
        8 << 20,
        10 << 20,
        limit=24,
    )
    split = []
    for grads, masters, olds, vectors in operands:
        count = 2 * len(grads) + len(vectors[2:])
        split.append(results[:count])
        results = results[count:]
    return split


class Place:
    def __init__(self):
        self.size = lax.axis_size("dp")
        self.chips = self.size // 2
        self.ring = list(range(0, self.chips, 2)) + list(range(self.chips - 1, 0, -2))
        self.small = self.size == HEADS
        index = lax.axis_index("dp")
        self.chip = index // 2
        self.core = index % 2 if self.small else jnp.zeros_like(index)
        where = [0] * self.chips
        for place, chip in enumerate(self.ring):
            where[chip] = place
        tables = [
            [self.ring[(where[chip] + offset) % self.chips] for offset in range(self.chips)]
            for chip in range(self.chips)
        ]
        self.table = lax.dynamic_index_in_dim(
            jnp.array(tables, jnp.int32), self.chip, 0, keepdims=False
        )

    def permute(self, array, target):
        pairs = []
        for chip in range(self.chips):
            for core in range(2):
                to_chip, to_core = target(chip, core)
                pairs.append((chip * 2 + core, to_chip * 2 + to_core))
        return lax.ppermute(array, "dp", pairs)

    def shift(self, array, by):
        where = {chip: place for place, chip in enumerate(self.ring)}
        return self.permute(
            array, lambda chip, core: (self.ring[(where[chip] + by) % self.chips], core)
        )

    def swap(self, array):
        return self.permute(array, lambda chip, core: (chip, 1 - core))

    def cross(self, array, mask):
        return self.permute(array, lambda chip, core: (chip ^ mask, core))

    def masks(self):
        return [1 << bit for bit in range(self.chips.bit_length() - 1)]


def section_shift(array, by):
    size = lax.axis_size("section")
    pairs = [(i, i + by) for i in range(size) if 0 <= i + by < size]
    return lax.ppermute(array, "section", pairs)


def upper_rows(rows):
    return (rows // 2 + 15) // 16 * 16


def gate_kernel():
    pass


def gated(arrays, behind):
    return call(gate_kernel, (), (), [], (), [], 0, 1 << 10, behind, passing=arrays)[1]


class RingGather:
    def __init__(self, own, here):
        self.here = here
        self.rows, self.columns = own.shape
        self.pieces = [(0, 0, own)]
        self.ahead = self.behind = own
        self.step = 0
        self.round()

    def round(self, behind=(), passing=()):
        here = self.here
        self.step += 1
        if behind or passing:
            self.ahead, self.behind, *passing = gated((self.ahead, self.behind, *passing), behind)
            if self.step > 1:
                self.pieces[-2:] = [
                    (1 - self.step, 0, self.ahead),
                    (self.step - 1, 0, self.behind),
                ]
        if self.step < here.chips // 2:
            self.ahead = here.shift(self.ahead, 1)
            self.behind = here.shift(self.behind, -1)
            self.pieces += [(-self.step, 0, self.ahead), (self.step, 0, self.behind)]
        else:
            cut = upper_rows(self.rows)
            self.ahead = here.shift(self.ahead[:cut], 1)
            self.behind = here.shift(self.behind[cut:], -1)
            self.pieces += [(self.step, 0, self.ahead), (self.step, cut, self.behind)]
        return passing

    def heads(self):
        return self.ahead, self.behind


def placed(rings, here, behind=()):
    plan, arrays, base = [], [], 0
    for ring in rings:
        for offset, row, piece in ring.pieces:
            plan.append((offset % here.chips, base + row))
            arrays.append(piece)
        base += ring.rows
    columns = arrays[0].shape[1]
    return call(
        functools.partial(place_kernel, tuple(plan)),
        array((here.chips, base, columns), arrays[0].dtype),
        (here.table, *arrays),
        [scalars()] + [HBM] * len(arrays),
        VMEM,
        [pltpu.SemaphoreType.DMA((len(arrays),))],
        0,
        4 * here.chips * base * columns,
        behind,
        56 if len(rings) == 1 else 30,
    )


def place_kernel(plan, chips_ref, *refs):
    out, sems = refs[-2:]
    pairs = []
    for piece, (place, row) in zip(refs, plan):
        pairs.append((piece, out.at[chips_ref[place], pl.ds(row, piece.shape[0])]))
    for copy in fetch(pairs, sems):
        copy.wait()


def pack_kernel(project_hbm, merge_hbm, vectors_ref, expand_hbm, out_ref, expand_out, project_ref, merge_ref, expand_ref, sems):
    copies = fetch([(project_hbm, project_ref), (merge_hbm, merge_ref), (expand_hbm, expand_ref)], sems)
    rows, width = merge_ref.shape
    count, wide = vectors_ref.shape
    vectors = jnp.concatenate([vectors_ref[...], jnp.zeros((16 - count, wide), F32)], axis=0)
    out_ref[4 * rows :] = jnp.concatenate(
        [vectors.astype(BF16), jnp.zeros((16, width - wide), BF16)], axis=1
    )
    copies[0].wait()
    for third in range(3):
        out_ref[third * rows : (third + 1) * rows] = project_ref[:, third * width : (third + 1) * width].astype(BF16)
    copies[1].wait()
    out_ref[3 * rows : 4 * rows] = merge_ref[...].astype(BF16)
    copies[2].wait()
    expand_out[...] = expand_ref[...].astype(BF16)


def pack_rows(project, merge, vectors, expand):
    rows, width = merge.shape
    return call(
        pack_kernel,
        (array((4 * rows + 16, width), BF16), array(expand.shape, BF16)),
        (project, merge, vectors, expand),
        [HBM, HBM, VMEM, HBM],
        (VMEM, VMEM),
        [pltpu.VMEM(part.shape, F32) for part in (project, merge, expand)] + [pltpu.SemaphoreType.DMA((3,))],
        0,
        2 << 20,
        limit=56,
    )


def half_kernel(side, whole_ref, out_ref):
    rows = out_ref.shape[0]
    out_ref[...] = whole_ref[side * rows : (side + 1) * rows].astype(BF16)


def half_of(whole, side, behind):
    half = array((whole.shape[0] // 2, whole.shape[1]), BF16)
    return call(functools.partial(half_kernel, side), half, (whole,), [VMEM], VMEM, [], 0, 2 << 20, behind)


def vectors_of(near, far, core, wide):
    cuts = [part[:, -16:, :wide] for part in (near, far)]
    rows = jnp.where(core == 0, jnp.stack(cuts), jnp.stack(cuts[::-1]))
    return rows.transpose(2, 1, 0, 3).reshape(16, -1).astype(F32)


def gather_plainly(project, merge, expand, shrink, vectors):
    width = merge.shape[1]

    def whole_of_rows(rows):
        whole = lax.all_gather(rows.astype(BF16), "dp", axis=0, tiled=True)
        return whole.reshape(PAIRS, 2, -1, whole.shape[1])

    parts = [whole_of_rows(project[:, at * width : (at + 1) * width]) for at in range(3)]
    cuts = [jnp.concatenate([*parts, whole_of_rows(merge)], axis=2)]
    cuts += [whole_of_rows(expand), whole_of_rows(shrink)]
    rows = lax.all_gather(vectors.astype(BF16), "dp", axis=1, tiled=True)
    rows = jnp.pad(rows, ((0, 16 - vectors.shape[0]), (0, 0)))
    return *((cut[:, 0], cut[:, 1]) for cut in cuts), rows.astype(F32)


def far_kernel(half, chips_ref, blocks, upper_ref, lower_ref, sems):
    cut = upper_ref.shape[0]
    chip = chips_ref[half]
    pairs = [
        (blocks.at[chip, pl.ds(0, cut)], upper_ref),
        (blocks.at[chip, pl.ds(cut, lower_ref.shape[0])], lower_ref),
    ]
    for copy in fetch(pairs, sems):
        copy.wait()


def add_kernel(ahead_at, behind_at, chips_ref, blocks, ahead_got, behind_got, ahead_out, behind_out, ahead_ref, behind_ref, sems):
    pairs = [
        (blocks.at[chips_ref[ahead_at]], ahead_out),
        (blocks.at[chips_ref[behind_at]], behind_out),
        (ahead_got, ahead_ref),
        (behind_got, behind_ref),
    ]
    for copy in fetch(pairs, sems):
        copy.wait()
    rows = behind_out.shape[0]
    for got, out, cut in (
        (ahead_ref, ahead_out, pl.ds(0, ahead_ref.shape[0])),
        (behind_ref, behind_out, pl.ds(rows - behind_ref.shape[0], behind_ref.shape[0])),
    ):
        out[cut] = (out[cut].astype(F32) + got[...].astype(F32)).astype(BF16)


class RingSum:
    def __init__(self, blocks, here, far=None):
        self.blocks = blocks
        self.here = here
        self.step = here.chips // 2
        self.sent = None
        if far is not None:
            self.send(far)

    def round(self, *behind, passing=()):
        here, blocks, step = self.here, self.blocks, self.step
        rows, columns = blocks.shape[1:]
        if self.sent is None:
            cut = upper_rows(rows)
            payload = call(
                functools.partial(far_kernel, step),
                (array((cut, columns), BF16), array((rows - cut, columns), BF16)),
                (here.table, blocks),
                [scalars(), HBM],
                (VMEM, VMEM),
                [pltpu.SemaphoreType.DMA((2,))],
                0,
                4 * rows * columns,
                behind,
            )
        else:
            whole = array((rows, columns), BF16)
            payload = call(
                functools.partial(add_kernel, step, here.chips - step),
                (whole, whole),
                (here.table, blocks, *self.sent),
                [scalars(), HBM, HBM, HBM],
                (VMEM, VMEM),
                [pltpu.VMEM(part.shape, BF16) for part in self.sent] + [pltpu.SemaphoreType.DMA((4,))],
                2 * rows * columns,
                12 * rows * columns,
                behind,
                passing=passing,
            )
            if passing:
                payload, passing = payload
        self.send(payload)
        return (payload[0], *passing)

    def send(self, payload):
        self.step -= 1
        self.sent = (self.here.shift(payload[0], 1), self.here.shift(payload[1], -1))

    def parts(self):
        return (self.blocks, *self.sent)


def small_sum(vector, here):
    if not here.small:
        return lax.psum(vector, "dp")
    vector = vector + here.swap(vector)
    near = [here.cross(vector, mask) for mask in (1, 2, 3)]
    vector = (vector + near[0]) + (near[1] + near[2])
    for mask in here.masks()[2:]:
        vector = vector + here.cross(vector, mask)
    return vector


def segments(lengths_row, count):
    ends = jnp.cumsum(lengths_row)
    places = jnp.arange(count, dtype=jnp.int32)
    return jnp.sum((places[:, None] >= ends[None, :]).astype(jnp.int32), axis=1)


def per_device(
    frames,
    lengths,
    cotangent,
    project_weight,
    merge_weight,
    expand_weight,
    shrink_weight,
    vectors,
    project_row,
    project_col,
    merge_row,
    merge_col,
    expand_row,
    expand_col,
    shrink_row,
    shrink_col,
    vector_moment,
):
    here = Place()
    core = here.core.reshape(1)
    is_first = lax.axis_index("section") == 0
    micro = lengths.shape[0]
    count, width = frames.shape
    block = count // micro
    segment = jax.vmap(lambda lengths_row: segments(lengths_row, block))(lengths)
    live = (segment < UTTS).astype(F32).reshape(count, 1)
    visible = (segment[:, :, None] == segment[:, None, :]).astype(F32)

    masters = (project_weight[0], merge_weight[0], expand_weight[0], shrink_weight[0])
    first = is_first.astype(jnp.int32).reshape(1)
    if here.small:
        pm_rows, e_rows = pack_rows(masters[0], masters[1], vectors[0], masters[2])
        pm_ring, e_ring = RingGather(pm_rows, here), RingGather(e_rows, here)
        pm_ring.round()
        pm_ring.round(e_ring.heads())
        e_ring.round()
        upper_ring = RingGather(half_of(masters[3], 0, pm_ring.heads()), here)
        pm_ring.round(e_ring.heads())
        e_ring.round()
        lower_ring = RingGather(half_of(masters[3], 1, e_ring.heads()), here)
        e_ring.round(upper_ring.heads())
        upper_ring.round()
        upper_ring.round(lower_ring.heads())
        lower_ring.round()
        upper_ring.round(lower_ring.heads())
        lower_ring.round()
        lower_ring.round()
        near = placed([pm_ring], here)
        pm = (near, here.swap(near))
        vec = vectors_of(*pm, here.core, vectors.shape[2])
        near = placed([e_ring], here)
        e = (near, here.swap(near))
        near = placed([upper_ring, lower_ring], here)
        s = (near, here.swap(near))
        kept = attend_block(core, frames, visible, vec, pm, (near,))
        (hidden,) = expand_block(core, kept[-1], vec, e, False)
    else:
        pm, e, s, vec = gather_plainly(*masters, vectors[0])
        kept = attend_block(core, frames, visible, vec, pm)
        (hidden,) = expand_block(core, kept[-1], vec, e, False)

    unused, low = shrink_block(core, kept[3], hidden, vec, s)
    start = jnp.where(is_first, frames, section_shift(low, 1))
    kept = attend_block(core, start, visible, vec, pm)
    normed, packed, mixed, middle, normed_two = kept
    hidden, slope = expand_block(core, normed_two, vec, e)

    incoming, unused = incoming_grad(jnp.zeros((1,), jnp.int32), frames, cotangent, live, ())
    unused, unused, back_middle, back_branch, sums_two, sums_up = back_hidden_block(
        core, incoming, middle, vec, s, e, slope, ()
    )
    unused, unused, low, unused = back_attend_block(
        core, first, start, back_middle, back_branch, packed, visible, vec, sums_two, sums_up, pm, ()
    )
    output, unused = shrink_block(core, middle, hidden, vec, s, (low,))
    incoming, low_incoming = incoming_grad(first, section_shift(low, -1), cotangent, live, (output,))
    swap = here.swap if here.small else lambda rows: rows

    shared = [swap(rows) for rows in (hidden, normed_two, normed, mixed)]
    behind = ()
    if here.small:
        operands = (hidden, shared[0], low_incoming, swap(low_incoming))
        far = shrink_far(here, core, *operands, shared[1:])
        shrink_ring = RingSum(shrink_grad(core, *operands, far[:1]), here, far)
        behind = shrink_ring.round()
    low_out, back_pre, back_middle, back_branch, sums_two, sums_up = back_hidden_block(
        core, incoming, middle, vec, s, e, slope, behind
    )
    if here.small:
        last, back_pre, back_branch = shrink_ring.round(passing=(back_pre, back_branch))
        behind = (last,)
    back_packed, back_inputs, low, vector_sums = back_attend_block(
        core, first, start, back_middle, back_branch, packed, visible, vec, sums_two, sums_up, pm, behind
    )
    layer_outputs = output[None]
    input_grads = back_inputs[None]

    rows = masters[0].shape[0]
    shrink_cuts = ((0, masters[3].shape[0], 1),)
    expand_cuts = ((0, rows, 1),)
    both_cuts = ((0, rows, 3), (3 * rows, rows, 1))
    shrink_olds, expand_olds = (shrink_row,), (expand_row,)
    both_olds = (project_row, merge_row)
    moment = vector_moment[0]
    if here.small:
        last, back_packed, vector_sums = shrink_ring.round(passing=(back_packed, vector_sums))
        expand_ring = RingSum(
            expand_grad(core, normed_two, shared[1], back_pre, swap(back_pre), (last,)), here
        )
        (last,) = expand_ring.round()
        both_ring = RingSum(
            project_grad(
                core,
                (
                    normed,
                    shared[2],
                    back_packed,
                    swap(back_packed),
                    mixed,
                    shared[3],
                    back_branch,
                    swap(back_branch),
                    vector_sums,
                    swap(vector_sums),
                ),
                (last,),
            ),
            here,
        )
        (last,) = both_ring.round()
        (last,) = expand_ring.round(last)
        shrink_ends = finish(shrink_ring.parts(), shrink_olds, shrink_cuts, None, here, (last,))
        (last,) = both_ring.round(shrink_ends[0])
        (last,) = expand_ring.round(last)
        (last,) = both_ring.round(last)
        (last,) = expand_ring.round(last)
        (last,) = both_ring.round(last)
        expand_ends = finish(expand_ring.parts(), expand_olds, expand_cuts, None, here, (last,))
        both_parts = both_ring.parts()
    else:

        def total(left, right):
            whole = dot_first(left, right).astype(BF16)
            return lax.psum_scatter(whole, "dp", scatter_dimension=0, tiled=True).astype(F32)

        shrink_ends = finish((total(hidden, low_out),), shrink_olds, shrink_cuts, None, here)
        expand_ends = finish((total(normed_two, back_pre),), expand_olds, expand_cuts, None, here)
        thirds = [total(normed, back_packed[:, at * width : (at + 1) * width]) for at in range(3)]
        vector_rows = lax.psum_scatter(vector_sums, "dp", scatter_dimension=1, tiled=True)
        vector_rows = jnp.pad(vector_rows, ((0, 0), (0, width - vector_rows.shape[1])))
        both_parts = (jnp.concatenate([*thirds, total(mixed, back_branch), vector_rows], axis=0),)
        last = vector_sums

    both_ends = finish(both_parts, both_olds, both_cuts, moment, here)
    ends = (shrink_ends, expand_ends, both_ends)
    sums = small_sum(jnp.concatenate([end[-1] for end in ends], axis=0), here)
    chunks = ((shrink_cuts, width, False), (expand_cuts, 4 * width, False), (both_cuts, width, True))
    matrices = (masters[3:], masters[2:3], masters[:2])
    cols_old = ((shrink_col,), (expand_col,), (project_col, merge_col))
    operands = []
    for (cuts, columns, with_vectors), end, masters_own, olds in zip(chunks, ends, matrices, cols_old):
        count = len(cuts)
        values = (*end[3 * count : -1], vectors[0]) if with_vectors else ()
        operands.append((end[2 * count : 3 * count], masters_own, olds, values))
    outs = []
    for end, operand, results in zip(ends, operands, update(chunks, operands, sums, here.size)):
        count, values = len(operand[0]), operand[-1]
        own = []
        for part in range(count):
            own += [end[part][None], end[count + part], results[count + part], results[part][None]]
        outs.append(own)
        vector_outs = (*values[:2], *results[2 * count :])
    shrink_outs, expand_outs, both_outs = outs
    return (
        layer_outputs,
        input_grads,
        *both_outs,
        *expand_outs,
        *shrink_outs,
        *(rows[None] for rows in vector_outs),
    )


def solution(mesh):
    placed = (
        P("dp", None),
        P("dp", None),
        P("dp", None),
        P("section", "dp", None),
        P("section", "dp", None),
        P("section", "dp", None),
        P("section", "dp", None),
        P("section", None, "dp"),
        P("section", "dp"),
        P("section", None),
        P("section", "dp"),
        P("section", None),
        P("section", "dp"),
        P("section", None),
        P("section", "dp"),
        P("section", None),
        P("section", None, "dp"),
    )
    matrix = (
        P("section", "dp", None),
        P("section", "dp"),
        P("section", None),
        P("section", "dp", None),
    )
    return jax.shard_map(
        per_device,
        mesh=mesh,
        in_specs=placed,
        out_specs=(
            P("section", "dp", None),
            P("section", "dp", None),
            *matrix,
            *matrix,
            *matrix,
            *matrix,
            P("section", None, "dp"),
            P("section", None, "dp"),
            P("section", None, "dp"),
        ),
        check_vma=False,
    )
```

```python
import functools
import math

import jax
import jax.numpy as jnp
from jax import lax
from jax.experimental import pallas as pl
from jax.experimental.pallas import tpu as pltpu
from jax.sharding import PartitionSpec as P

HEADS = 16
HEAD_DIM = 64
PAIRS = HEADS // 2
UTTS = 3
STEP = 10

EPSILON = 1e-05
RATE = 0.04
VECTOR_RATE = 0.25
MASKED = -1e30
BF16 = jnp.bfloat16
F32 = jnp.float32
VMEM = pl.BlockSpec(memory_space=pltpu.VMEM)
HBM = pl.BlockSpec(memory_space=pl.ANY)
MIB = 1024 * 1024


def dot(left, right):
    return lax.dot_general(left, right, (((1,), (0,)), ((), ())), preferred_element_type=F32)


def dot_last(left, right):
    return lax.dot_general(left, right, (((1,), (1,)), ((), ())), preferred_element_type=F32)


def dot_first(left, right):
    return lax.dot_general(left, right, (((0,), (0,)), ((), ())), preferred_element_type=F32)


def moments(values):
    centred = values - jnp.mean(values, axis=-1, keepdims=True)
    spread = jnp.mean(centred * centred, axis=-1, keepdims=True)
    scale = lax.rsqrt(spread + EPSILON)
    return centred * scale, scale


def norm_back(grad, unit, scale, gain):
    inner = grad * gain
    first = jnp.mean(inner, axis=-1, keepdims=True)
    second = jnp.mean(inner * unit, axis=-1, keepdims=True)
    return scale * (inner - first - unit * second)


def fetch(pairs, sems):
    copies = [
        pltpu.make_async_copy(source, target, sems.at[index])
        for index, (source, target) in enumerate(pairs)
    ]
    for copy in copies:
        copy.start()
    return copies


def half_masks():
    lane = lax.broadcasted_iota(jnp.int32, (1, 128), 1)
    low = jnp.where(lane < HEAD_DIM, 1.0, 0.0)
    return low.astype(BF16), (1.0 - low).astype(BF16)


def two_heads(tile, masks):
    return jnp.concatenate([tile * masks[0], tile * masks[1]], axis=0)


def side_by_side(both):
    half = both.shape[0] // 2
    return jnp.concatenate([both[:half], both[half:]], axis=1)


def weights_of(scores, visible):
    scores = jnp.where(visible, scores * HEAD_DIM**-0.5, MASKED)
    shifted = jnp.exp(scores - jnp.max(scores, axis=-1, keepdims=True))
    return shifted / jnp.sum(shifted, axis=-1, keepdims=True)


def scalars():
    return pl.BlockSpec(memory_space=pltpu.SMEM)


def array(shape, kind):
    return jax.ShapeDtypeStruct(shape, kind)


def call(kernel, outs, args, in_specs, out_specs, scratch, flops, size, behind=(), limit=12, passing=()):
    given, skipped = len(args), len(behind) + len(passing)
    single = not isinstance(outs, tuple)
    results = (outs,) if single else outs
    result_specs = (out_specs,) if single else out_specs
    count = len(results)

    def body(*refs):
        kernel(*refs[:given], *refs[given + skipped :][:count], *refs[given + skipped + count + len(passing) :])

    returned = pl.pallas_call(
        body,
        out_shape=(*results, *(array(value.shape, value.dtype) for value in passing)),
        in_specs=[
            *in_specs,
            *(HBM for unused in range(skipped)),
        ],
        out_specs=(*result_specs, *(HBM for unused in passing)),
        scratch_shapes=scratch,
        input_output_aliases={given + len(behind) + at: count + at for at in range(len(passing))},
        compiler_params=pltpu.CompilerParams(vmem_limit_bytes=limit * MIB),
        cost_estimate=pl.CostEstimate(flops=flops, bytes_accessed=size, transcendentals=0),
    )(*args, *behind, *passing)
    own = returned[0] if single else tuple(returned[:count])
    return (own, tuple(returned[count:])) if passing else own


def both_cores(core, near, far, whole, cuts):
    pairs = []
    for cut in cuts:
        pairs.append((near.at[cut], whole.at[cut[0], core, *cut[1:]]))
        pairs.append((far.at[cut], whole.at[cut[0], 1 - core, *cut[1:]]))
    return pairs


ALL = slice(None)


def quarters_of(core, near, far, whole, order):
    rows = whole.shape[3]
    pairs = []
    for at in order:
        pairs.append((near.at[:, pl.ds(at * rows, rows)], whole.at[at, :, core]))
        pairs.append((far.at[:, pl.ds(at * rows, rows)], whole.at[at, :, 1 - core]))
    return pairs


def quarters_scratch(width):
    return pltpu.VMEM((4, PAIRS, 2, width // HEADS, width), BF16)


def columns_cut(start, size):
    return (ALL, ALL, pl.ds(start, size))


def attend_kernel(core_ref, x_ref, mask_ref, vec_ref, near, far, a_ref, packed_ref, o_ref, x1_ref, c_ref, w, sems):
    count, width = x_ref.shape
    block = mask_ref.shape[1]
    step = 512
    copies = fetch(quarters_of(core_ref[0], near, far, w, range(4)), sems)
    unit, unused = moments(x_ref[...].astype(F32))
    a_ref[...] = (unit * vec_ref[0:1] + vec_ref[1:2]).astype(BF16)
    for third in range(3):
        copies[2 * third].wait()
        copies[2 * third + 1].wait()
        for cut in range(width // step):
            at = third * width + cut * step
            matrix = w[third, :, :, :, cut * step : (cut + 1) * step].reshape(width, step)
            result = dot(a_ref[...], matrix)
            if third != 1:
                row = 2 if third == 0 else 3
                result = result + vec_ref[row : row + 1, cut * step : (cut + 1) * step]
            packed_ref[:, at : at + step] = result.astype(BF16)
    masks = half_masks()
    for micro in range(count // block):
        rows = slice(micro * block, (micro + 1) * block)
        visible = mask_ref[micro] > 0.0
        visible = jnp.concatenate([visible, visible], axis=0)
        for at in range(0, width, 128):
            queries = packed_ref[rows, at : at + 128]
            keys = packed_ref[rows, at + width : at + width + 128]
            values = packed_ref[rows, at + 2 * width : at + 2 * width + 128]
            attend = weights_of(dot_last(two_heads(queries, masks), keys), visible).astype(BF16)
            mixed = dot(side_by_side(attend), two_heads(values, masks))
            o_ref[rows, at : at + 128] = mixed.astype(BF16)
    copies[6].wait()
    copies[7].wait()
    for at in range(0, width, step):
        cut = slice(at, at + step)
        matrix = w[3, :, :, :, cut].reshape(width, step)
        x1_ref[:, cut] = x_ref[:, cut].astype(F32) + (dot(o_ref[...], matrix) + vec_ref[4:5, cut])
    unit, unused = moments(x1_ref[...])
    c_ref[...] = (unit * vec_ref[5:6] + vec_ref[6:7]).astype(BF16)


def whole_of(near):
    chips, rows, columns = near.shape
    return pltpu.VMEM((chips, 2, rows, columns), near.dtype)


def attend_block(core, x, mask, vec, pm, behind=()):
    count, width = x.shape
    low = array((count, width), BF16)
    return call(
        attend_kernel,
        (low, array((count, 3 * width), BF16), low, array((count, width), F32), low),
        (core, x, mask, vec, *pm),
        [scalars()] + [VMEM] * 3 + [HBM] * 2,
        (VMEM,) * 5,
        [quarters_scratch(width), pltpu.SemaphoreType.DMA((8,))],
        8 * count * width * width,
        20 << 20,
        behind=behind,
        limit=32,
    )


def gelu_parts(values):
    cdf = 0.5 * (1.0 + lax.erf(values * math.sqrt(0.5)))
    slope = cdf + values * jnp.exp(-0.5 * values * values) * (1.0 / math.sqrt(2.0 * math.pi))
    return values * cdf, slope


def expand_kernel(with_slope, core_ref, c_ref, vec_ref, near, far, hidden_ref, *refs):
    if with_slope:
        slope_hbm, w, slope, sems, out_sems = refs
    else:
        w, sems = refs
    count, width = c_ref.shape
    step = 256
    quarters = w.shape[3] // width
    copies = fetch(
        both_cores(core_ref[0], near, far, w, [columns_cut(at * width, width) for at in range(quarters)]), sems
    )
    sent = []
    for quarter in range(quarters):
        copies[2 * quarter].wait()
        copies[2 * quarter + 1].wait()
        for cut in range(width // step):
            at = quarter * width + cut * step
            result = dot(c_ref[...], w[:, :, :, at : at + step].reshape(width, step))
            bias = vec_ref[8 + quarter : 9 + quarter, cut * step : (cut + 1) * step]
            hidden, rise = gelu_parts(result + bias)
            hidden_ref[:, at : at + step] = hidden.astype(BF16)
            if with_slope:
                slope[:, at : at + step] = rise
        if not with_slope:
            continue
        at = slice(quarter * width, (quarter + 1) * width)
        copy = pltpu.make_async_copy(slope.at[:, at], slope_hbm.at[:, at], out_sems.at[quarter])
        copy.start()
        sent.append(copy)
    for copy in sent:
        copy.wait()


def expand_block(core, c, vec, e, with_slope=True):
    count, width = c.shape
    hidden = 4 * width
    outs, specs, scratch = [array((count, hidden), BF16)], [VMEM], [whole_of(e[0])]
    if with_slope:
        outs.append(array((count, hidden), F32))
        specs.append(HBM)
        scratch.append(pltpu.VMEM((count, hidden), F32))
    scratch.append(pltpu.SemaphoreType.DMA((8,)))
    if with_slope:
        scratch.append(pltpu.SemaphoreType.DMA((4,)))
    return call(
        functools.partial(expand_kernel, with_slope),
        tuple(outs),
        (core, c, vec, *e),
        [scalars()] + [VMEM] * 2 + [HBM] * 2,
        tuple(specs),
        scratch,
        2 * count * width * hidden,
        20 << 20,
        limit=32,
    )


def shrink_kernel(core_ref, x1_ref, hidden_ref, vec_ref, near, far, y_ref, low_ref, w, sems):
    chips, unused, rows, width = w.shape
    step = 512
    group = width // (2 * rows)
    copies = fetch(
        both_cores(core_ref[0], near, far, w, [(pl.ds(at, group),) for at in range(0, chips, group)]), sems
    )
    for index in range(chips // group):
        copies[2 * index].wait()
        copies[2 * index + 1].wait()
        left = hidden_ref[:, index * width : (index + 1) * width]
        for at in range(0, width, step):
            cut = slice(at, at + step)
            matrix = w[index * group : (index + 1) * group, :, :, cut].reshape(width, step)
            result = dot(left, matrix)
            if index == 0:
                y_ref[:, cut] = x1_ref[:, cut] + result
            elif index < chips // group - 1:
                y_ref[:, cut] += result
            else:
                total = y_ref[:, cut] + result + vec_ref[7:8, cut]
                y_ref[:, cut] = total
                low_ref[:, cut] = total.astype(BF16)


def shrink_block(core, x1, hidden, vec, s, behind=()):
    count, width = x1.shape
    return call(
        shrink_kernel,
        (array((count, width), F32), array((count, width), BF16)),
        (core, x1, hidden, vec, *s),
        [scalars()] + [VMEM] * 3 + [HBM] * 2,
        (VMEM, VMEM),
        [whole_of(s[0]), pltpu.SemaphoreType.DMA((8,))],
        8 * count * width * width,
        16 << 20,
        behind=behind,
        limit=28,
    )


def back_hidden_kernel(with_sums, core_ref, dy_ref, x1_ref, vec_ref, s_near, s_far, e_near, e_far, slope_hbm, gf_ref, gu_ref, dx1_ref, gat_ref, sums_ref, bias_ref, ws, we, slope, dc, sems, slope_sems):
    chips, unused, rows, width = ws.shape
    group = width // (2 * rows)
    quarters = chips // group
    core = core_ref[0]
    pairs = []
    for index in range(quarters):
        at = pl.ds(index * width, width)
        pairs += both_cores(core, s_near, s_far, ws, [(pl.ds(index * group, group),)])
        pairs.append((slope_hbm.at[:, at], slope.at[:, at]))
        pairs += both_cores(core, e_near, e_far, we, [columns_cut(index * width, width)])
    copies = fetch(pairs, sems)
    gf_ref[...] = dy_ref[...].astype(BF16)
    step = 512
    for index in range(quarters):
        for copy in copies[5 * index : 5 * index + 3]:
            copy.wait()
        for near in range(group):
            matrix = ws[index * group + near].reshape(2 * rows, width)
            at = slice(index * width + near * 2 * rows, index * width + (near + 1) * 2 * rows)
            back = (dot_last(gf_ref[...], matrix) * slope[:, at]).astype(BF16)
            gu_ref[:, at] = back
            if with_sums:
                bias_ref[:, at] = jnp.sum(back.astype(F32), axis=0, keepdims=True)
        for copy in copies[5 * index + 3 : 5 * index + 5]:
            copy.wait()
        at = slice(index * width, (index + 1) * width)
        left = gu_ref[:, at]
        for half in range(2):
            matrix = we[half * (chips // 2) : (half + 1) * (chips // 2), :, :, at].reshape(step, width)
            to = slice(half * step, (half + 1) * step)
            result = dot_last(left, matrix)
            if index == 0:
                dc[:, to] = result
            else:
                dc[:, to] += result
    unit, scale = moments(x1_ref[...])
    grad = dc[...]
    back = dy_ref[...] + norm_back(grad, unit, scale, vec_ref[5:6])
    dx1_ref[...] = back
    gat_ref[...] = back.astype(BF16)
    sums_ref[...] = jnp.zeros_like(sums_ref)
    if not with_sums:
        bias_ref[...] = jnp.zeros_like(bias_ref)
        return
    sums_ref[0:1] = jnp.sum(grad * unit, axis=0, keepdims=True)
    sums_ref[1:2] = jnp.sum(grad, axis=0, keepdims=True)
    sums_ref[2:3] = jnp.sum(gf_ref[...].astype(F32), axis=0, keepdims=True)
    sums_ref[3:4] = jnp.sum(gat_ref[...].astype(F32), axis=0, keepdims=True)


def back_hidden_block(core, dy, x1, vec, s, e, slope, behind, with_sums=True):
    count, width = x1.shape
    hidden = slope.shape[1]
    return call(
        functools.partial(back_hidden_kernel, with_sums),
        (
            array((count, width), BF16),
            array((count, hidden), BF16),
            array((count, width), F32),
            array((count, width), BF16),
            array((8, width), F32),
            array((1, hidden), F32),
        ),
        (core, dy, x1, vec, *s, *e, slope),
        [scalars()] + [VMEM] * 3 + [HBM] * 5,
        (VMEM,) * 6,
        [
            whole_of(s[0]),
            whole_of(e[0]),
            pltpu.VMEM((count, hidden), F32),
            pltpu.VMEM((count, width), F32),
            pltpu.SemaphoreType.DMA((20,)),
            pltpu.SemaphoreType.DMA((4,)),
        ],
        16 * count * width * width,
        32 << 20,
        behind,
        limit=44,
    )


def back_attend_kernel(with_sums, core_ref, first_ref, x_ref, dx1_ref, gat_ref, packed_ref, mask_ref, vec_ref, two_ref, up_ref, near, far, gqkv_ref, dx_ref, low_ref, sums_ref, w, go, sems):
    count, width = x_ref.shape
    block = mask_ref.shape[1]
    step = 512
    copies = fetch(quarters_of(core_ref[0], near, far, w, (3, 0, 1, 2)), sems)
    masks = half_masks()
    factor = HEAD_DIM**-0.5
    copies[0].wait()
    copies[1].wait()
    chips = w.shape[1]
    for half in range(2):
        matrix = w[3, half * (chips // 2) : (half + 1) * (chips // 2)].reshape(step, width)
        go[:, half * step : (half + 1) * step] = dot_last(gat_ref[...], matrix).astype(BF16)
    tiles = range(0, width, 128)
    for micro in range(count // block):
        rows = slice(micro * block, (micro + 1) * block)
        visible = mask_ref[micro] > 0.0
        visible = jnp.concatenate([visible, visible], axis=0)
        queries = [two_heads(packed_ref[rows, at : at + 128], masks) for at in tiles]
        keys = [packed_ref[rows, at + width : at + width + 128] for at in tiles]
        values = [packed_ref[rows, at + 2 * width : at + 2 * width + 128] for at in tiles]
        back = [two_heads(go[rows, at : at + 128], masks) for at in tiles]
        scores = [dot_last(query, key) for query, key in zip(queries, keys)]
        slopes = [dot_last(grad, value) for grad, value in zip(back, values)]
        attend = [weights_of(score, visible) for score in scores]
        low = [weight.astype(BF16) for weight in attend]
        inner = [jnp.sum(weight * slope, axis=-1, keepdims=True) for weight, slope in zip(attend, slopes)]
        scores = [
            (weight * (slope - total)).astype(BF16)
            for weight, slope, total in zip(attend, slopes, inner)
        ]
        grad_q = [dot(side_by_side(score), two_heads(key, masks)) for score, key in zip(scores, keys)]
        grad_k = [dot_first(score, query) for score, query in zip(scores, queries)]
        grad_v = [dot_first(weight, grad) for weight, grad in zip(low, back)]
        for at, one, two, three in zip(tiles, grad_q, grad_k, grad_v):
            gqkv_ref[rows, at : at + 128] = (one * factor).astype(BF16)
            gqkv_ref[rows, at + width : at + width + 128] = (two * factor).astype(BF16)
            gqkv_ref[rows, at + 2 * width : at + 2 * width + 128] = three.astype(BF16)
    for copy in copies[2:]:
        copy.wait()
    for half in range(2):
        total = None
        for third in range(3):
            matrix = w[third, half * (chips // 2) : (half + 1) * (chips // 2)].reshape(step, width)
            result = dot_last(gqkv_ref[:, third * width : (third + 1) * width], matrix)
            total = result if total is None else total + result
        dx_ref[:, half * step : (half + 1) * step] = total
    unit, scale = moments(x_ref[...].astype(F32))
    grad = dx_ref[...]
    sums_ref[...] = jnp.zeros_like(sums_ref)
    if with_sums:
        sums_ref[0:1] = jnp.sum(grad * unit, axis=0, keepdims=True)
        sums_ref[1:2] = jnp.sum(grad, axis=0, keepdims=True)
    back = dx1_ref[...] + norm_back(grad, unit, scale, vec_ref[0:1])
    low = back.astype(BF16)
    low_ref[...] = low
    dx_ref[...] = jnp.where(first_ref[0] == 1, back, low.astype(F32))
    if not with_sums:
        return
    for row, third in ((2, 0), (3, 2)):
        part = gqkv_ref[:, third * width : (third + 1) * width]
        sums_ref[row : row + 1] = jnp.sum(part.astype(F32), axis=0, keepdims=True)
    sums_ref[4:5] = two_ref[3:4]
    sums_ref[5:8] = two_ref[0:3]
    for quarter in range(4):
        sums_ref[8 + quarter : 9 + quarter] = up_ref[:, quarter * width : (quarter + 1) * width]


def back_attend_block(core, first, x, dx1, gat, packed, mask, vec, two, up, pm, behind, with_sums=True):
    count, width = x.shape
    return call(
        functools.partial(back_attend_kernel, with_sums),
        (
            array((count, 3 * width), BF16),
            array((count, width), F32),
            array((count, width), BF16),
            array((16, width), F32),
        ),
        (core, first, x, dx1, gat, packed, mask, vec, two, up, *pm),
        [scalars()] * 2 + [VMEM] * 8 + [HBM] * 2,
        (VMEM,) * 4,
        [quarters_scratch(width), pltpu.VMEM((count, width), BF16), pltpu.SemaphoreType.DMA((8,))],
        12 * count * width * width,
        20 << 20,
        behind,
        limit=32,
    )


def incoming_kernel(first_ref, mail_ref, cotangent_ref, live_ref, out_ref, low_ref):
    targets = cotangent_ref[...].astype(F32) * live_ref[...]
    mail = mail_ref[...].astype(F32)
    out = jnp.where(first_ref[0] == 1, mail, targets)
    out_ref[...] = out
    low_ref[...] = out.astype(BF16)


def incoming_grad(first, mail, cotangent, live, behind):
    shape = cotangent.shape
    return call(
        incoming_kernel,
        (array(shape, F32), array(shape, BF16)),
        (first, mail, cotangent, live),
        [scalars()] + [VMEM] * 3,
        (VMEM, VMEM),
        [],
        0,
        10 * cotangent.size,
        behind,
    )


def shrink_grad_kernel(core_ref, near_ref, far_ref, right_ref, other_ref, out_ref):
    chips, rows, width = out_ref.shape
    for chip in range(chips):
        at = pl.ds(pl.multiple_of((2 * chip + core_ref[0]) * rows, rows), rows)
        total = dot_first(near_ref[:, at], right_ref[...]) + dot_first(far_ref[:, at], other_ref[...])
        out_ref[chip] = total.astype(BF16)


def shrink_far_kernel(half, chips_ref, core_ref, near_ref, far_ref, right_ref, other_ref, upper_ref, lower_ref):
    cut, lower = upper_ref.shape[0], lower_ref.shape[0]
    at = (2 * chips_ref[half] + core_ref[0]) * (cut + lower)
    for start, out in ((0, upper_ref), (cut, lower_ref)):
        rows = pl.ds(pl.multiple_of(at + start, cut), out.shape[0])
        total = dot_first(near_ref[:, rows], right_ref[...]) + dot_first(far_ref[:, rows], other_ref[...])
        out[...] = total.astype(BF16)


def shrink_far(here, core, near, far, right, other, behind):
    tokens, hidden = near.shape
    width = right.shape[1]
    half = array((hidden // HEADS // 2, width), BF16)
    return call(
        functools.partial(shrink_far_kernel, here.chips // 2),
        (half, half),
        (here.table, core, near, far, right, other),
        [scalars()] * 2 + [VMEM] * 4,
        (VMEM, VMEM),
        [],
        2 * tokens * width * hidden // PAIRS,
        5 << 20,
        behind,
        24,
    )


def shrink_grad(core, near, far, right, other, behind):
    tokens, hidden = near.shape
    width = right.shape[1]
    return call(
        shrink_grad_kernel,
        array((PAIRS, hidden // HEADS, width), BF16),
        (core, near, far, right, other),
        [scalars()] + [VMEM] * 4,
        VMEM,
        [],
        2 * tokens * width * hidden,
        12 << 20,
        behind,
        limit=24,
    )


def own_rows(core, near_ref, far_ref, turned):
    chips, unused, rows, both = turned.shape
    tokens = near_ref.shape[0]
    turned[:, :, :, :tokens] = near_ref[...].T.reshape(chips, 2, rows, tokens)
    turned[:, :, :, tokens:] = far_ref[...].T.reshape(chips, 2, rows, tokens)
    return turned[:, pl.ds(core, 1)].reshape(chips * rows, both)


def own_columns_grad(left, right_ref, other_ref, cut):
    right = jnp.concatenate([right_ref[:, cut], other_ref[:, cut]], axis=0)
    return dot(left, right).astype(BF16)


def expand_grad_kernel(core_ref, near_ref, far_ref, right_ref, other_ref, out_ref, turned):
    chips, rows, columns = out_ref.shape
    left = own_rows(core_ref[0], near_ref, far_ref, turned)
    step = 512
    for at in range(0, columns, step):
        cut = slice(at, at + step)
        out_ref[:, :, cut] = own_columns_grad(left, right_ref, other_ref, cut).reshape(chips, rows, step)


def turned_scratch(tokens, width):
    return pltpu.VMEM((PAIRS, 2, width // HEADS, 2 * tokens), BF16)


def expand_grad(core, near, far, right, other, behind):
    tokens, width = near.shape
    hidden = right.shape[1]
    return call(
        expand_grad_kernel,
        array((PAIRS, width // HEADS, hidden), BF16),
        (core, near, far, right, other),
        [scalars()] + [VMEM] * 4,
        VMEM,
        [turned_scratch(tokens, width)],
        2 * tokens * width * hidden,
        12 << 20,
        behind=behind,
        limit=24,
    )


def project_grad_kernel(core_ref, a_ref, a_far, packed_ref, packed_far, o_ref, o_far, gat_ref, gat_far, vec_ref, vec_far, out_ref, turned):
    chips, unused, width = out_ref.shape
    rows = width // HEADS
    core = core_ref[0]
    step = 512
    left = own_rows(core, a_ref, a_far, turned)
    for third in range(3):
        for at in range(0, width, step):
            result = own_columns_grad(left, packed_ref, packed_far, slice(third * width + at, third * width + at + step))
            out_ref[:, third * rows : (third + 1) * rows, at : at + step] = result.reshape(chips, rows, step)
    left = own_rows(core, o_ref, o_far, turned)
    for at in range(0, width, step):
        result = own_columns_grad(left, gat_ref, gat_far, slice(at, at + step))
        out_ref[:, 3 * rows : 4 * rows, at : at + step] = result.reshape(chips, rows, step)
    total = vec_ref[...] + vec_far[...]
    for chip in range(chips):
        pair = total[:, chip * 2 * rows : (chip + 1) * 2 * rows]
        turn = jnp.concatenate([pair[:, rows:], pair[:, :rows]], axis=1)
        own = jnp.where(core == 0, pair, turn)
        out_ref[chip, 4 * rows :, : 2 * rows] = own.astype(BF16)
        out_ref[chip, 4 * rows :, 2 * rows :] = jnp.zeros((own.shape[0], width - 2 * rows), BF16)


def project_grad(core, operands, behind):
    tokens, width = operands[0].shape
    rows = width // HEADS
    return call(
        project_grad_kernel,
        array((PAIRS, 4 * rows + 16, width), BF16),
        (core, *operands),
        [scalars()] + [VMEM] * len(operands),
        VMEM,
        [turned_scratch(tokens, width)],
        8 * tokens * width * width,
        12 << 20,
        behind=behind,
        limit=24,
    )


DECAY = 1.0 - STEP ** (-0.8)
LANES = 128


def sums_at(cuts, columns):
    lines = sum(blocks for first, rows, blocks in cuts) * columns // LANES
    return lines, 2 * lines, 2 * lines + 8


def turned_row(row):
    return jnp.sum(jnp.where(diagonal(row.shape[1]), row, 0.0), axis=1, keepdims=True)


def turned_column(column):
    return jnp.sum(jnp.where(diagonal(column.shape[0]), column, 0.0), axis=0, keepdims=True)


def diagonal(count):
    rows = lax.broadcasted_iota(jnp.int32, (count, count), 0)
    return rows == lax.broadcasted_iota(jnp.int32, (count, count), 1)


def finish_kernel(addends, cuts, with_vectors, *refs):
    parts = len(cuts)
    refs = list(refs)

    def take(count):
        taken = refs[:count]
        del refs[:count]
        return taken

    if addends > 1:
        (chips_ref, blocks), addend_refs = take(2), take(addends - 1)
    else:
        addend_refs = take(1)
    old_refs = take(parts)
    moment_refs = take(int(with_vectors))
    grad_refs, row_refs, over_refs = take(parts), take(parts), take(parts)
    vector_refs = take(2 * int(with_vectors))
    (sums_ref,) = take(1)
    if addends > 1:
        own, sems = refs
        for copy in fetch([(blocks.at[chips_ref[0]], own)], sems):
            copy.wait()
        addend_refs.append(own)
    columns = addend_refs[0].shape[1]
    norms, totals, vector_line = sums_at(cuts, columns)

    def sum_of(rows, cut):
        total = None
        for ref in addend_refs:
            value = ref[rows, cut].astype(F32)
            total = value if total is None else total + value
        return total

    sums_ref[totals : totals + 8] = jnp.zeros((8, LANES), F32)
    line = 0
    for part, (first, rows, blocks) in enumerate(cuts):
        row_sum = None
        for block in range(blocks):
            grad = sum_of(slice(first + block * rows, first + (block + 1) * rows), ALL)
            cut = slice(block * columns, (block + 1) * columns)
            grad_refs[part][:, cut] = grad
            square = grad * grad + 1e-30
            block_sum = jnp.sum(square, axis=1, keepdims=True)
            row_sum = block_sum if row_sum is None else row_sum + block_sum
            column_sum = jnp.sum(square, axis=0, keepdims=True)
            for at in range(columns // LANES):
                to = line + block * columns // LANES + at
                sums_ref[to : to + 1] = column_sum[:, at * LANES : (at + 1) * LANES]
        row_stat = DECAY * turned_row(old_refs[part][...]) + (1.0 - DECAY) * (row_sum / (blocks * columns))
        row_refs[part][...] = turned_column(row_stat)
        root = lax.rsqrt(row_stat)
        for block in range(blocks):
            grad = grad_refs[part][:, block * columns : (block + 1) * columns]
            over = grad * root
            over_refs[part][:, block * columns : (block + 1) * columns] = over
            column_sum = jnp.sum(over * over, axis=0, keepdims=True)
            for at in range(columns // LANES):
                to = norms + line + block * columns // LANES + at
                sums_ref[to : to + 1] = column_sum[:, at * LANES : (at + 1) * LANES]
        line += blocks * columns // LANES
        total = jnp.sum(row_stat, axis=0, keepdims=True)
        sums_ref[totals + part : totals + part + 1] = jnp.broadcast_to(total, (1, LANES))
    if with_vectors:
        last = cuts[-1][0] + cuts[-1][1] * cuts[-1][2]
        moment = moment_refs[0][...]
        count, wide = moment.shape
        grad = sum_of(slice(last, last + 16), slice(0, LANES))[:count, :wide]
        second = DECAY * moment + (1.0 - DECAY) * (grad * grad + 1e-30)
        vector_refs[0][...] = grad
        vector_refs[1][...] = second
        move = grad * lax.rsqrt(second)
        norm = jnp.sum(move * move, axis=1, keepdims=True)
        sums_ref[vector_line:] = jnp.zeros((16, LANES), F32)
        sums_ref[vector_line : vector_line + count] = jnp.broadcast_to(norm, (count, LANES))


def finish(parts, olds, cuts, moment, here, behind=()):
    columns = parts[-1].shape[1]
    rows = parts[-1].shape[0]
    outs = [array((count, blocks * columns), F32) for first, count, blocks in cuts]
    outs += [array((1, count), F32) for first, count, blocks in cuts]
    outs += outs[: len(cuts)]
    vectors = () if moment is None else (moment,)
    outs += [array(value.shape, F32) for value in vectors for unused in range(2)]
    outs += [array((sums_at(cuts, columns)[2] + 16 * len(vectors), LANES), F32)]
    args, specs, scratch = list(parts), [VMEM] * len(parts), []
    if len(parts) > 1:
        args, specs = [here.table, *parts], [scalars(), HBM] + [VMEM] * (len(parts) - 1)
        scratch = [pltpu.VMEM((rows, columns), parts[0].dtype), pltpu.SemaphoreType.DMA((1,))]
    args += list(olds) + list(vectors)
    specs += [VMEM] * (len(olds) + len(vectors))
    return call(
        functools.partial(finish_kernel, len(parts), cuts, bool(vectors)),
        tuple(outs),
        tuple(args),
        specs,
        (VMEM,) * len(outs),
        scratch,
        8 * rows * columns,
        8 * rows * columns,
        behind,
        16,
    )


def update_kernel(chunks, full_rows, *refs):
    refs = list(refs)

    def take(count):
        taken = refs[:count]
        del refs[:count]
        return taken

    operands = []
    for cuts, columns, with_vectors in chunks:
        operands.append([take(len(cuts)) for unused in range(3)] + [take(3 * int(with_vectors))])
    (sums_ref,) = take(1)
    base = 0
    for (cuts, columns, with_vectors), operand in zip(chunks, operands):
        over_refs, master_refs, old_refs, vector_refs = operand
        updated_refs, column_refs = take(len(cuts)), take(len(cuts))
        norms, totals, vector_line = sums_at(cuts, columns)

        def lanes(start, count):
            return jnp.concatenate([sums_ref[start + at : start + at + 1] for at in range(count)], axis=1)

        line = base
        for part, (first, rows, blocks) in enumerate(cuts):
            wide = blocks * columns
            lines = wide // LANES
            square, weighted = lanes(line, lines), lanes(norms + line, lines)
            line += lines
            count = full_rows[rows]
            row_mean = sums_ref[base + totals + part : base + totals + part + 1, 0:1] / count
            col_stat = DECAY * old_refs[part][...] + (1.0 - DECAY) * (square / count)
            column_refs[part][...] = col_stat
            norm = row_mean * jnp.sum(weighted / col_stat, axis=1, keepdims=True)
            scale = jnp.sqrt(norm / (count * wide))
            rate = jnp.sqrt(row_mean) * (RATE / jnp.maximum(1.0, scale))
            updated_refs[part][...] = master_refs[part][...] - over_refs[part][...] * (rate * lax.rsqrt(col_stat))
        if with_vectors:
            grad_ref, second_ref, vectors_ref = vector_refs
            count = grad_ref.shape[0]
            norm = sums_ref[base + vector_line : base + vector_line + count, 0:1]
            scale = jnp.sqrt(norm / columns)
            move = grad_ref[...] * lax.rsqrt(second_ref[...])
            (updated_ref,) = take(1)
            updated_ref[...] = vectors_ref[...] - VECTOR_RATE * move / jnp.maximum(1.0, scale)
        base += vector_line + 16 * int(with_vectors)


def update(chunks, operands, sums, size):
    outs, args = [], []
    for grads, masters, olds, vectors in operands:
        outs += [array(grad.shape, F32) for grad in grads]
        outs += [array((1, grad.shape[1]), F32) for grad in grads]
        outs += [array(value.shape, F32) for value in vectors[2:]]
        args += [*grads, *masters, *olds, *vectors]
    full_rows = {grad.shape[0]: grad.shape[0] * size for operand in operands for grad in operand[0]}
    results = call(
        functools.partial(update_kernel, chunks, full_rows),
        tuple(outs),
        (*args, sums),
        [VMEM] * (len(args) + 1),
        (VMEM,) * len(outs),
        [],
        8 << 20,
        10 << 20,
        limit=24,
    )
    split = []
    for grads, masters, olds, vectors in operands:
        count = 2 * len(grads) + len(vectors[2:])
        split.append(results[:count])
        results = results[count:]
    return split


class Place:
    def __init__(self):
        self.size = lax.axis_size("dp")
        self.chips = self.size // 2
        self.ring = list(range(0, self.chips, 2)) + list(range(self.chips - 1, 0, -2))
        self.small = self.size == HEADS
        index = lax.axis_index("dp")
        self.chip = index // 2
        self.core = index % 2 if self.small else jnp.zeros_like(index)
        where = [0] * self.chips
        for place, chip in enumerate(self.ring):
            where[chip] = place
        tables = [
            [self.ring[(where[chip] + offset) % self.chips] for offset in range(self.chips)]
            for chip in range(self.chips)
        ]
        self.table = lax.dynamic_index_in_dim(
            jnp.array(tables, jnp.int32), self.chip, 0, keepdims=False
        )

    def permute(self, array, target):
        pairs = []
        for chip in range(self.chips):
            for core in range(2):
                to_chip, to_core = target(chip, core)
                pairs.append((chip * 2 + core, to_chip * 2 + to_core))
        return lax.ppermute(array, "dp", pairs)

    def shift(self, array, by):
        where = {chip: place for place, chip in enumerate(self.ring)}
        return self.permute(
            array, lambda chip, core: (self.ring[(where[chip] + by) % self.chips], core)
        )

    def swap(self, array):
        return self.permute(array, lambda chip, core: (chip, 1 - core))

    def cross(self, array, mask):
        return self.permute(array, lambda chip, core: (chip ^ mask, core))

    def masks(self):
        return [1 << bit for bit in range(self.chips.bit_length() - 1)]


def section_shift(array, by):
    size = lax.axis_size("section")
    pairs = [(i, i + by) for i in range(size) if 0 <= i + by < size]
    return lax.ppermute(array, "section", pairs)


def upper_rows(rows):
    return (rows // 2 + 15) // 16 * 16


def gate_kernel():
    pass


def gated(arrays, behind):
    return call(gate_kernel, (), (), [], (), [], 0, 1 << 10, behind, passing=arrays)[1]


class RingGather:
    def __init__(self, own, here):
        self.here = here
        self.rows, self.columns = own.shape
        self.pieces = [(0, 0, own)]
        self.ahead = self.behind = own
        self.step = 0
        self.round()

    def round(self, behind=(), passing=()):
        here = self.here
        self.step += 1
        if behind or passing:
            self.ahead, self.behind, *passing = gated((self.ahead, self.behind, *passing), behind)
            if self.step > 1:
                self.pieces[-2:] = [
                    (1 - self.step, 0, self.ahead),
                    (self.step - 1, 0, self.behind),
                ]
        if self.step < here.chips // 2:
            self.ahead = here.shift(self.ahead, 1)
            self.behind = here.shift(self.behind, -1)
            self.pieces += [(-self.step, 0, self.ahead), (self.step, 0, self.behind)]
        else:
            cut = upper_rows(self.rows)
            self.ahead = here.shift(self.ahead[:cut], 1)
            self.behind = here.shift(self.behind[cut:], -1)
            self.pieces += [(self.step, 0, self.ahead), (self.step, cut, self.behind)]
        return passing

    def heads(self):
        return self.ahead, self.behind


def placed(rings, here, behind=()):
    plan, arrays, base = [], [], 0
    for ring in rings:
        for offset, row, piece in ring.pieces:
            plan.append((offset % here.chips, base + row))
            arrays.append(piece)
        base += ring.rows
    columns = arrays[0].shape[1]
    return call(
        functools.partial(place_kernel, tuple(plan)),
        array((here.chips, base, columns), arrays[0].dtype),
        (here.table, *arrays),
        [scalars()] + [HBM] * len(arrays),
        VMEM,
        [pltpu.SemaphoreType.DMA((len(arrays),))],
        0,
        4 * here.chips * base * columns,
        behind,
        56 if len(rings) == 1 else 30,
    )


def place_kernel(plan, chips_ref, *refs):
    out, sems = refs[-2:]
    pairs = []
    for piece, (place, row) in zip(refs, plan):
        pairs.append((piece, out.at[chips_ref[place], pl.ds(row, piece.shape[0])]))
    for copy in fetch(pairs, sems):
        copy.wait()


def pack_kernel(project_hbm, merge_hbm, vectors_ref, expand_hbm, out_ref, expand_out, project_ref, merge_ref, expand_ref, sems):
    copies = fetch([(project_hbm, project_ref), (merge_hbm, merge_ref), (expand_hbm, expand_ref)], sems)
    rows, width = merge_ref.shape
    count, wide = vectors_ref.shape
    vectors = jnp.concatenate([vectors_ref[...], jnp.zeros((16 - count, wide), F32)], axis=0)
    out_ref[4 * rows :] = jnp.concatenate(
        [vectors.astype(BF16), jnp.zeros((16, width - wide), BF16)], axis=1
    )
    copies[0].wait()
    for third in range(3):
        out_ref[third * rows : (third + 1) * rows] = project_ref[:, third * width : (third + 1) * width].astype(BF16)
    copies[1].wait()
    out_ref[3 * rows : 4 * rows] = merge_ref[...].astype(BF16)
    copies[2].wait()
    expand_out[...] = expand_ref[...].astype(BF16)


def pack_rows(project, merge, vectors, expand):
    rows, width = merge.shape
    return call(
        pack_kernel,
        (array((4 * rows + 16, width), BF16), array(expand.shape, BF16)),
        (project, merge, vectors, expand),
        [HBM, HBM, VMEM, HBM],
        (VMEM, VMEM),
        [pltpu.VMEM(part.shape, F32) for part in (project, merge, expand)] + [pltpu.SemaphoreType.DMA((3,))],
        0,
        2 << 20,
        limit=56,
    )


def half_kernel(side, whole_ref, out_ref):
    rows = out_ref.shape[0]
    out_ref[...] = whole_ref[side * rows : (side + 1) * rows].astype(BF16)


def half_of(whole, side, behind):
    half = array((whole.shape[0] // 2, whole.shape[1]), BF16)
    return call(functools.partial(half_kernel, side), half, (whole,), [VMEM], VMEM, [], 0, 2 << 20, behind)


def vectors_of(near, far, core, wide):
    cuts = [part[:, -16:, :wide] for part in (near, far)]
    rows = jnp.where(core == 0, jnp.stack(cuts), jnp.stack(cuts[::-1]))
    return rows.transpose(2, 1, 0, 3).reshape(16, -1).astype(F32)


def gather_plainly(project, merge, expand, shrink, vectors):
    width = merge.shape[1]

    def whole_of_rows(rows):
        whole = lax.all_gather(rows.astype(BF16), "dp", axis=0, tiled=True)
        return whole.reshape(PAIRS, 2, -1, whole.shape[1])

    parts = [whole_of_rows(project[:, at * width : (at + 1) * width]) for at in range(3)]
    cuts = [jnp.concatenate([*parts, whole_of_rows(merge)], axis=2)]
    cuts += [whole_of_rows(expand), whole_of_rows(shrink)]
    rows = lax.all_gather(vectors.astype(BF16), "dp", axis=1, tiled=True)
    rows = jnp.pad(rows, ((0, 16 - vectors.shape[0]), (0, 0)))
    return *((cut[:, 0], cut[:, 1]) for cut in cuts), rows.astype(F32)


def far_kernel(half, chips_ref, blocks, upper_ref, lower_ref, sems):
    cut = upper_ref.shape[0]
    chip = chips_ref[half]
    pairs = [
        (blocks.at[chip, pl.ds(0, cut)], upper_ref),
        (blocks.at[chip, pl.ds(cut, lower_ref.shape[0])], lower_ref),
    ]
    for copy in fetch(pairs, sems):
        copy.wait()


def add_kernel(ahead_at, behind_at, chips_ref, blocks, ahead_got, behind_got, ahead_out, behind_out, ahead_ref, behind_ref, sems):
    pairs = [
        (blocks.at[chips_ref[ahead_at]], ahead_out),
        (blocks.at[chips_ref[behind_at]], behind_out),
        (ahead_got, ahead_ref),
        (behind_got, behind_ref),
    ]
    for copy in fetch(pairs, sems):
        copy.wait()
    rows = behind_out.shape[0]
    for got, out, cut in (
        (ahead_ref, ahead_out, pl.ds(0, ahead_ref.shape[0])),
        (behind_ref, behind_out, pl.ds(rows - behind_ref.shape[0], behind_ref.shape[0])),
    ):
        out[cut] = (out[cut].astype(F32) + got[...].astype(F32)).astype(BF16)


class RingSum:
    def __init__(self, blocks, here, far=None):
        self.blocks = blocks
        self.here = here
        self.step = here.chips // 2
        self.sent = None
        if far is not None:
            self.send(far)

    def round(self, *behind, passing=()):
        here, blocks, step = self.here, self.blocks, self.step
        rows, columns = blocks.shape[1:]
        if self.sent is None:
            cut = upper_rows(rows)
            payload = call(
                functools.partial(far_kernel, step),
                (array((cut, columns), BF16), array((rows - cut, columns), BF16)),
                (here.table, blocks),
                [scalars(), HBM],
                (VMEM, VMEM),
                [pltpu.SemaphoreType.DMA((2,))],
                0,
                4 * rows * columns,
                behind,
            )
        else:
            whole = array((rows, columns), BF16)
            payload = call(
                functools.partial(add_kernel, step, here.chips - step),
                (whole, whole),
                (here.table, blocks, *self.sent),
                [scalars(), HBM, HBM, HBM],
                (VMEM, VMEM),
                [pltpu.VMEM(part.shape, BF16) for part in self.sent] + [pltpu.SemaphoreType.DMA((4,))],
                2 * rows * columns,
                12 * rows * columns,
                behind,
                passing=passing,
            )
            if passing:
                payload, passing = payload
        self.send(payload)
        return (payload[0], *passing)

    def send(self, payload):
        self.step -= 1
        self.sent = (self.here.shift(payload[0], 1), self.here.shift(payload[1], -1))

    def parts(self):
        return (self.blocks, *self.sent)


def small_sum(vector, here):
    if not here.small:
        return lax.psum(vector, "dp")
    vector = vector + here.swap(vector)
    near = [here.cross(vector, mask) for mask in (1, 2, 3)]
    vector = (vector + near[0]) + (near[1] + near[2])
    for mask in here.masks()[2:]:
        vector = vector + here.cross(vector, mask)
    return vector


def segments(lengths_row, count):
    ends = jnp.cumsum(lengths_row)
    places = jnp.arange(count, dtype=jnp.int32)
    return jnp.sum((places[:, None] >= ends[None, :]).astype(jnp.int32), axis=1)


def per_device(
    frames,
    lengths,
    cotangent,
    project_weight,
    merge_weight,
    expand_weight,
    shrink_weight,
    vectors,
    project_row,
    project_col,
    merge_row,
    merge_col,
    expand_row,
    expand_col,
    shrink_row,
    shrink_col,
    vector_moment,
):
    here = Place()
    core = here.core.reshape(1)
    is_first = lax.axis_index("section") == 0
    micro = lengths.shape[0]
    count, width = frames.shape
    block = count // micro
    segment = jax.vmap(lambda lengths_row: segments(lengths_row, block))(lengths)
    live = (segment < UTTS).astype(F32).reshape(count, 1)
    visible = (segment[:, :, None] == segment[:, None, :]).astype(F32)

    masters = (project_weight[0], merge_weight[0], expand_weight[0], shrink_weight[0])
    first = is_first.astype(jnp.int32).reshape(1)
    if here.small:
        pm_rows, e_rows = pack_rows(masters[0], masters[1], vectors[0], masters[2])
        pm_ring, e_ring = RingGather(pm_rows, here), RingGather(e_rows, here)
        pm_ring.round()
        pm_ring.round(e_ring.heads())
        e_ring.round()
        upper_ring = RingGather(half_of(masters[3], 0, pm_ring.heads()), here)
        pm_ring.round(e_ring.heads())
        e_ring.round()
        lower_ring = RingGather(half_of(masters[3], 1, e_ring.heads()), here)
        e_ring.round(upper_ring.heads())
        upper_ring.round()
        upper_ring.round(lower_ring.heads())
        lower_ring.round()
        upper_ring.round(lower_ring.heads())
        lower_ring.round()
        lower_ring.round()
        near = placed([pm_ring], here)
        pm = (near, here.swap(near))
        vec = vectors_of(*pm, here.core, vectors.shape[2])
        near = placed([e_ring], here)
        e = (near, here.swap(near))
        near = placed([upper_ring, lower_ring], here)
        s = (near, here.swap(near))
        kept = attend_block(core, frames, visible, vec, pm, (near,))
        (hidden,) = expand_block(core, kept[-1], vec, e, False)
    else:
        pm, e, s, vec = gather_plainly(*masters, vectors[0])
        kept = attend_block(core, frames, visible, vec, pm)
        (hidden,) = expand_block(core, kept[-1], vec, e, False)

    unused, low = shrink_block(core, kept[3], hidden, vec, s)
    start = jnp.where(is_first, frames, section_shift(low, 1))
    kept = attend_block(core, start, visible, vec, pm)
    normed, packed, mixed, middle, normed_two = kept
    hidden, slope = expand_block(core, normed_two, vec, e)

    incoming, unused = incoming_grad(jnp.zeros((1,), jnp.int32), frames, cotangent, live, ())
    unused, unused, back_middle, back_branch, sums_two, sums_up = back_hidden_block(
        core, incoming, middle, vec, s, e, slope, (), False
    )
    unused, unused, low, unused = back_attend_block(
        core, first, start, back_middle, back_branch, packed, visible, vec, sums_two, sums_up, pm, (), False
    )
    output, unused = shrink_block(core, middle, hidden, vec, s, (low,))
    incoming, low_incoming = incoming_grad(first, section_shift(low, -1), cotangent, live, (output,))
    swap = here.swap if here.small else lambda rows: rows

    shared = [swap(rows) for rows in (hidden, normed_two, normed, mixed)]
    behind = ()
    if here.small:
        operands = (hidden, shared[0], low_incoming, swap(low_incoming))
        far = shrink_far(here, core, *operands, shared[1:])
        shrink_ring = RingSum(shrink_grad(core, *operands, far[:1]), here, far)
        behind = shrink_ring.round()
    low_out, back_pre, back_middle, back_branch, sums_two, sums_up = back_hidden_block(
        core, incoming, middle, vec, s, e, slope, behind
    )
    if here.small:
        last, back_pre, back_branch = shrink_ring.round(passing=(back_pre, back_branch))
        behind = (last,)
    back_packed, back_inputs, low, vector_sums = back_attend_block(
        core, first, start, back_middle, back_branch, packed, visible, vec, sums_two, sums_up, pm, behind
    )
    layer_outputs = output[None]
    input_grads = back_inputs[None]

    rows = masters[0].shape[0]
    shrink_cuts = ((0, masters[3].shape[0], 1),)
    expand_cuts = ((0, rows, 1),)
    both_cuts = ((0, rows, 3), (3 * rows, rows, 1))
    shrink_olds, expand_olds = (shrink_row,), (expand_row,)
    both_olds = (project_row, merge_row)
    moment = vector_moment[0]
    if here.small:
        last, back_packed, vector_sums = shrink_ring.round(passing=(back_packed, vector_sums))
        expand_ring = RingSum(
            expand_grad(core, normed_two, shared[1], back_pre, swap(back_pre), (last,)), here
        )
        (last,) = expand_ring.round()
        both_ring = RingSum(
            project_grad(
                core,
                (
                    normed,
                    shared[2],
                    back_packed,
                    swap(back_packed),
                    mixed,
                    shared[3],
                    back_branch,
                    swap(back_branch),
                    vector_sums,
                    swap(vector_sums),
                ),
                (last,),
            ),
            here,
        )
        (last,) = both_ring.round()
        (last,) = expand_ring.round(last)
        shrink_ends = finish(shrink_ring.parts(), shrink_olds, shrink_cuts, None, here, (last,))
        (last,) = both_ring.round(shrink_ends[0])
        (last,) = expand_ring.round(last)
        (last,) = both_ring.round(last)
        (last,) = expand_ring.round(last)
        (last,) = both_ring.round(last)
        expand_ends = finish(expand_ring.parts(), expand_olds, expand_cuts, None, here, (last,))
        both_parts = both_ring.parts()
    else:

        def total(left, right):
            whole = dot_first(left, right).astype(BF16)
            return lax.psum_scatter(whole, "dp", scatter_dimension=0, tiled=True).astype(F32)

        shrink_ends = finish((total(hidden, low_out),), shrink_olds, shrink_cuts, None, here)
        expand_ends = finish((total(normed_two, back_pre),), expand_olds, expand_cuts, None, here)
        thirds = [total(normed, back_packed[:, at * width : (at + 1) * width]) for at in range(3)]
        vector_rows = lax.psum_scatter(vector_sums, "dp", scatter_dimension=1, tiled=True)
        vector_rows = jnp.pad(vector_rows, ((0, 0), (0, width - vector_rows.shape[1])))
        both_parts = (jnp.concatenate([*thirds, total(mixed, back_branch), vector_rows], axis=0),)
        last = vector_sums

    both_ends = finish(both_parts, both_olds, both_cuts, moment, here)
    ends = (shrink_ends, expand_ends, both_ends)
    sums = small_sum(jnp.concatenate([end[-1] for end in ends], axis=0), here)
    chunks = ((shrink_cuts, width, False), (expand_cuts, 4 * width, False), (both_cuts, width, True))
    matrices = (masters[3:], masters[2:3], masters[:2])
    cols_old = ((shrink_col,), (expand_col,), (project_col, merge_col))
    operands = []
    for (cuts, columns, with_vectors), end, masters_own, olds in zip(chunks, ends, matrices, cols_old):
        count = len(cuts)
        values = (*end[3 * count : -1], vectors[0]) if with_vectors else ()
        operands.append((end[2 * count : 3 * count], masters_own, olds, values))
    outs = []
    for end, operand, results in zip(ends, operands, update(chunks, operands, sums, here.size)):
        count, values = len(operand[0]), operand[-1]
        own = []
        for part in range(count):
            own += [end[part][None], end[count + part], results[count + part], results[part][None]]
        outs.append(own)
        vector_outs = (*values[:2], *results[2 * count :])
    shrink_outs, expand_outs, both_outs = outs
    return (
        layer_outputs,
        input_grads,
        *both_outs,
        *expand_outs,
        *shrink_outs,
        *(rows[None] for rows in vector_outs),
    )


def solution(mesh):
    placed = (
        P("dp", None),
        P("dp", None),
        P("dp", None),
        P("section", "dp", None),
        P("section", "dp", None),
        P("section", "dp", None),
        P("section", "dp", None),
        P("section", None, "dp"),
        P("section", "dp"),
        P("section", None),
        P("section", "dp"),
        P("section", None),
        P("section", "dp"),
        P("section", None),
        P("section", "dp"),
        P("section", None),
        P("section", None, "dp"),
    )
    matrix = (
        P("section", "dp", None),
        P("section", "dp"),
        P("section", None),
        P("section", "dp", None),
    )
    return jax.shard_map(
        per_device,
        mesh=mesh,
        in_specs=placed,
        out_specs=(
            P("section", "dp", None),
            P("section", "dp", None),
            *matrix,
            *matrix,
            *matrix,
            *matrix,
            P("section", None, "dp"),
            P("section", None, "dp"),
            P("section", None, "dp"),
        ),
        check_vma=False,
    )
```
